32 devices in a mesh: parts: 2 (over y), dp: 4 (over z), fsdp: 4 (over x, core).
Axes of the slice: x: 2, y: 2, z: 4, core: 2. Of those that a mesh axis runs over, the one named last changes fastest.
Arguments:
- tokens: bfloat16 [12288, 5120], P(('parts', 'dp', 'fsdp')), parts along dimension 0, may hold values from -6 to 6
- cotangent: bfloat16 [12288, 1024], P(('parts', 'dp', 'fsdp')), parts along dimension 0, may hold values from -0.1875 to 0.1875
- lengths: int32 [32, 12], P(('parts', 'dp', 'fsdp')), parts along dimension 0, may hold values from 1 to 32, 288 in all within a row
- slot_adapter_index: int32 [32, 12], P(('parts', 'dp', 'fsdp')), parts along dimension 0, may hold values from 0 to 3, as said below
- adapter_rank_sizes: int32 [4], replicated, may hold values from 8 to 128
- frozen: bfloat16 [5120, 1024], P('fsdp'), may hold values from -0.078125 to 0.078125
- key_norm_weight: float32 [128], replicated, may hold values from 0.25 to 1.75
- adapter_down_factor: float32 [8, 5120, 128], P(('parts', 'dp'), 'fsdp'), parts along dimension 0, may hold values from -0.078125 to 0.078125
- adapter_up_factor: float32 [8, 128, 1024], P(('parts', 'dp'), 'fsdp'), parts along dimension 0, may hold values from -0.5 to 0.5
- down_first_moment: float32 [8, 5120, 128], P(('parts', 'dp'), 'fsdp'), parts along dimension 0, may hold values from -1.75 to 1.75
- up_first_moment: float32 [8, 128, 1024], P(('parts', 'dp'), 'fsdp'), parts along dimension 0, may hold values from -1.75 to 1.75
- down_second_moment: float32 [8, 5120, 128], P(('parts', 'dp'), 'fsdp'), parts along dimension 0, may hold values from 0.01 to 1
- up_second_moment: float32 [8, 128, 1024], P(('parts', 'dp'), 'fsdp'), parts along dimension 0, may hold values from 0.01 to 1
Outputs:
- updated_down_factor: float32 [8, 5120, 128], P(('parts', 'dp'), 'fsdp'), parts along dimension 0
- updated_up_factor: float32 [8, 128, 1024], P(('parts', 'dp'), 'fsdp'), parts along dimension 0
- updated_down_first_moment: float32 [8, 5120, 128], P(('parts', 'dp'), 'fsdp'), parts along dimension 0
- updated_up_first_moment: float32 [8, 128, 1024], P(('parts', 'dp'), 'fsdp'), parts along dimension 0
- updated_down_second_moment: float32 [8, 5120, 128], P(('parts', 'dp'), 'fsdp'), parts along dimension 0
- updated_up_second_moment: float32 [8, 128, 1024], P(('parts', 'dp'), 'fsdp'), parts along dimension 0
The draws below stay inside these ranges and needn't reach their ends.
There are 2 independent parts, one for each index of `parts`. The reference program is written for one: setup_inputs(seed, part) draws one part's arguments, and reference() takes and returns one part's arrays. A program takes and returns all parts, laid end to end along the dimension named above; an argument that names none is the same for every part. Nothing has to cross between parts.
Inputs may be any that keep to these rules, and one draw needn't show every extreme that they name: `slot_adapter_index`: no adapter is used by more than 3 sequence slots of one device; some adapter is used by exactly 3 slots on every device.
All inputs are finite; a program needn't handle non-finite values.
Results may differ from the reference program's by a relative error of at most 0.0018.
Values may be sent and summed in bfloat16 or wider, within the bound.
No kernel may reach another device: no remote copies, remote signals or barrier semaphores. Data moves between devices by JAX's collectives and lax.ppermute only.
A program may use at most 128 MiB of HBM per device.

```python
import math
import jax
import jax.numpy as jnp
import numpy as np
from jax import lax

MODEL_WIDTH = 5120
HEAD = 128
KEY_WIDTH = 1024
PADDED_RANK = 128
SEQ = 32
SEQ_DEV = 12
TOK_DEV = 384
ADAPTER_COUNT = 4
PAIR = 3
UNITS = 16
TOKENS = 6144


def draw_slot_adapter_index(key, part):
    key = jax.random.fold_in(key, 7)
    first_key, second_key, third_key, fourth_key = jax.random.split(key, 4)
    popularity = jax.random.randint(first_key, (ADAPTER_COUNT,), 0, 4)
    favored = jax.random.randint(second_key, (), 0, ADAPTER_COUNT)
    popularity = jnp.where(jnp.arange(ADAPTER_COUNT) == favored, 64, popularity)
    candidates = jnp.arange(ADAPTER_COUNT * PAIR)
    jitter = jax.random.randint(third_key, (UNITS, ADAPTER_COUNT * PAIR), 0, 4096)
    scores = popularity[candidates // PAIR][None, :] * 1048576 + jitter * 1024 + candidates[None, :]
    picked = lax.top_k(scores, SEQ_DEV)[1] // PAIR
    shuffle = jax.random.randint(fourth_key, (UNITS, SEQ_DEV), 0, 65536) * 64 + jnp.arange(SEQ_DEV)[None, :]
    placing = lax.top_k(shuffle, SEQ_DEV)[1]
    return jnp.take_along_axis(picked, placing, axis=1).astype(jnp.int32)


def set_ends(array, rng, low, largest):
    place = [jax.random.randint(jax.random.fold_in(rng, axis), (), 0, length) for axis, length in enumerate(array.shape)]
    widest = array.shape.index(max(array.shape))
    next_to = place[:widest] + [(place[widest] + 1) % array.shape[widest]] + place[widest + 1:]
    return array.at[tuple(place)].set(low).at[tuple(next_to)].set(largest)


def level_of(own_key, dims, cuts, least, high):
    loudness, own = 1.0, jax.random.fold_in(own_key, 6)
    for dim, blocks in cuts:
        steps = jnp.exp(jax.random.uniform(jax.random.fold_in(own, dim), (blocks,), jnp.float32, least / len(cuts), high / len(cuts)))
        loudness = loudness * jnp.repeat(steps, dims[dim] // blocks).reshape([-1 if axis == dim else 1 for axis in range(len(dims))])
    return loudness


def split_up(amount, total, reach, slope):
    loads = [(1 << 20) // math.isqrt(grade ** slope) + 1 for grade in range(2, amount + 1)]
    spare, holding = total - reach - (amount - 1), [1] * (amount - 1)
    while spare > 0:
        free = [i for i in range(amount - 1) if holding[i] < reach]
        pool, left = sum([loads[i] for i in free]), spare
        for i in free:
            more = min(reach - holding[i], max(1, left * loads[i] // pool), spare)
            holding[i] = holding[i] + more
            spare = spare - more
    return np.array([reach] + holding)


def ragged_sizes(rng, number_of, total, reach, skew):
    if number_of == 2:
        one = jax.random.randint(rng, (), max(1, total - reach), min(reach, total - 1) + 1)
        return jnp.stack([one, total - one])
    sizes = jnp.asarray(split_up(number_of, total, reach, skew), jnp.int32)
    couples = (number_of - 1) // 2
    donor, sink = sizes[1:1 + 2 * couples:2], sizes[2:2 + 2 * couples:2]
    room = jnp.minimum(donor - 1, reach - sink)
    shifted = jax.random.randint(jax.random.fold_in(rng, 1), (couples,), 0, 1 << 20) % (room + 1)
    sizes = sizes.at[1:1 + 2 * couples:2].set(donor - shifted).at[2:2 + 2 * couples:2].set(sink + shifted)
    return sizes[jax.random.permutation(jax.random.fold_in(rng, 2), number_of)]


def normal_values(key, extent, scale, bound, cuts=(), held_as=jnp.bfloat16):
    gain = level_of(key, extent, cuts, -0.22, 0.18) if cuts else 1.0
    entries = jax.random.normal(key, extent, jnp.float32) * scale * gain
    return jnp.minimum(jnp.maximum(entries, -bound), bound).astype(held_as)


def setup_inputs(seed: int = 0, part: int = 0) -> dict:
    keys = jax.random.split(jax.random.key(seed), 14)
    own_keys = jax.random.split(jax.random.fold_in(keys[13], part), 14)
    tokens = normal_values(own_keys[0], (TOKENS, MODEL_WIDTH), 1.0, 6.0, ((0, 16),))
    cotangent = normal_values(own_keys[1], (TOKENS, KEY_WIDTH), 0.03, 0.1875, ((0, 16),))
    lengths = jax.vmap(lambda own: ragged_sizes(own, SEQ_DEV, 3 * TOK_DEV // 4, SEQ, 1))(jax.random.split(own_keys[2], UNITS)).reshape((UNITS, SEQ_DEV)).astype(jnp.int32)
    slot_adapter_index = draw_slot_adapter_index(jax.random.fold_in(jax.random.fold_in(keys[13], part), 71), part)
    adapter_rank_sizes = set_ends(jax.random.randint(keys[4], (ADAPTER_COUNT,), PADDED_RANK // 16, PADDED_RANK + 1), jax.random.fold_in(keys[4], 1), PADDED_RANK // 16, PADDED_RANK).astype(jnp.int32)
    frozen = normal_values(keys[5], (MODEL_WIDTH, KEY_WIDTH), MODEL_WIDTH ** -0.5, 0.078125, ((0, 4),))
    key_norm_weight = jnp.clip(1.0 + 0.15 * jax.random.normal(keys[6], (HEAD,), jnp.float32), 0.25, 1.75)
    adapter_down_factor = normal_values(own_keys[7], (ADAPTER_COUNT, MODEL_WIDTH, PADDED_RANK), MODEL_WIDTH ** -0.5, 0.078125, ((0, 4), (1, 4)), jnp.float32)
    adapter_up_factor = normal_values(own_keys[8], (ADAPTER_COUNT, PADDED_RANK, KEY_WIDTH), PADDED_RANK ** -0.5, 0.5, ((0, 4), (1, 4)), jnp.float32)
    down_first_moment = normal_values(own_keys[9], (ADAPTER_COUNT, MODEL_WIDTH, PADDED_RANK), 0.3, 1.75, ((0, 4), (1, 4)), jnp.float32)
    up_first_moment = normal_values(own_keys[10], (ADAPTER_COUNT, PADDED_RANK, KEY_WIDTH), 0.3, 1.75, ((0, 4), (1, 4)), jnp.float32)
    down_second_moment = jnp.clip(jnp.exp(math.log(1.0) - 4.6051702 * jax.random.uniform(own_keys[11], (ADAPTER_COUNT, MODEL_WIDTH, PADDED_RANK), jnp.float32) ** level_of(own_keys[11], (ADAPTER_COUNT, MODEL_WIDTH, PADDED_RANK), ((0, 4), (1, 4)), -0.2, 0.2)), 0.01, 1.0)
    up_second_moment = jnp.clip(jnp.exp(math.log(1.0) - 4.6051702 * jax.random.uniform(own_keys[12], (ADAPTER_COUNT, PADDED_RANK, KEY_WIDTH), jnp.float32) ** level_of(own_keys[12], (ADAPTER_COUNT, PADDED_RANK, KEY_WIDTH), ((0, 4), (1, 4)), -0.2, 0.2)), 0.01, 1.0)
    return dict(tokens=tokens, cotangent=cotangent, lengths=lengths, slot_adapter_index=slot_adapter_index, adapter_rank_sizes=adapter_rank_sizes, frozen=frozen, key_norm_weight=key_norm_weight, adapter_down_factor=adapter_down_factor, adapter_up_factor=adapter_up_factor, down_first_moment=down_first_moment, up_first_moment=up_first_moment, down_second_moment=down_second_moment, up_second_moment=up_second_moment)


adapter_alpha_scale = 16.0
norm_epsilon = 1e-06
learn_rate = 0.001
weight_decay = 0.01
beta_one = 0.9
beta_two = 0.999
correct_one = 1.0 - 0.9 ** 10
correct_two = 1.0 - 0.999 ** 10
adam_epsilon = 1e-08

def adapter_grads(row_tokens, row_base, row_grads, down_factor_weight, up_factor_weight, owned_adapter_rank, key_norm_weight):
    columns = jnp.arange(PADDED_RANK) < owned_adapter_rank
    masked_down = jnp.where(columns[None, :], down_factor_weight, jnp.zeros((), jnp.bfloat16))
    masked_up = jnp.where(columns[:, None], up_factor_weight, jnp.zeros((), jnp.bfloat16))
    adapter_scale_factor = adapter_alpha_scale / owned_adapter_rank.astype(jnp.float32)
    lowrank = jnp.dot(row_tokens, masked_down, preferred_element_type=jnp.float32).astype(jnp.bfloat16)
    key_rows = row_base.astype(jnp.float32) + adapter_scale_factor * jnp.dot(lowrank, masked_up, preferred_element_type=jnp.float32)
    per_head = key_rows.reshape(key_rows.shape[0], KEY_WIDTH // HEAD, HEAD)
    inverse = lax.rsqrt(lax.optimization_barrier(jnp.mean(per_head * per_head, axis=-1, keepdims=True)) + norm_epsilon)
    normed = per_head * inverse
    incoming = row_grads.astype(jnp.float32).reshape(per_head.shape) * key_norm_weight
    key_grads = inverse * (incoming - normed * lax.optimization_barrier(jnp.mean(incoming * normed, axis=-1, keepdims=True)))
    key_grads = key_grads.reshape(key_rows.shape).astype(jnp.bfloat16)
    up_factor_gradient = adapter_scale_factor * lax.dot_general(lowrank, key_grads, (((0,), (0,)), ((), ())), preferred_element_type=jnp.float32)
    up_factor_gradient = jnp.where(columns[:, None], up_factor_gradient, 0.0)
    low_grads = (adapter_scale_factor * lax.dot_general(key_grads, masked_up, (((1,), (1,)), ((), ())), preferred_element_type=jnp.float32)).astype(jnp.bfloat16)
    down_factor_gradient = lax.dot_general(row_tokens, low_grads, (((0,), (0,)), ((), ())), preferred_element_type=jnp.float32)
    return (down_factor_gradient, up_factor_gradient)

def optimizer_update(weights, gradient, moment, variance):
    moment_new = beta_one * moment + (1.0 - beta_one) * gradient
    variance_new = beta_two * variance + (1.0 - beta_two) * gradient * gradient
    update = moment_new / correct_one / (jnp.sqrt(variance_new / correct_two) + adam_epsilon)
    return (weights - learn_rate * (update + weight_decay * weights), moment_new, variance_new)

def reference(tokens, cotangent, lengths, slot_adapter_index, adapter_rank_sizes, frozen, key_norm_weight, adapter_down_factor, adapter_up_factor, down_first_moment, up_first_moment, down_second_moment, up_second_moment):
    token_seqs = tokens.reshape(UNITS, SEQ_DEV, SEQ, MODEL_WIDTH)
    base_keys = jnp.dot(tokens, frozen, preferred_element_type=jnp.float32).astype(jnp.bfloat16).reshape(UNITS, SEQ_DEV, SEQ, KEY_WIDTH)
    positions = jnp.arange(SEQ)
    live_mask = positions[None, None, :] < lengths[:, :, None]
    upstream = jnp.where(live_mask[..., None], cotangent.reshape(UNITS, SEQ_DEV, SEQ, KEY_WIDTH), jnp.zeros((), cotangent.dtype))
    target = slot_adapter_index
    seq_index = jnp.arange(SEQ_DEV)

    def per_owner(owning_replica):
        wanted = target == owning_replica
        slot_order = jnp.cumsum(wanted.astype(jnp.int32), axis=1) - 1
        chosen_seq = []
        valid_slot = []
        for slot_index in range(PAIR):
            chosen = wanted & (slot_order == slot_index)
            chosen_seq.append(lax.optimization_barrier(jnp.sum(jnp.where(chosen, seq_index[None, :], 0), axis=1)))
            valid_slot.append(jnp.any(chosen, axis=1))
        chosen_seq = jnp.stack(chosen_seq, axis=1).astype(jnp.int32)
        valid_slot = jnp.stack(valid_slot, axis=1)

        def select(values):
            picked = jnp.take_along_axis(values, chosen_seq[:, :, None, None], axis=1)
            picked = jnp.where(valid_slot[:, :, None, None], picked, jnp.zeros((), values.dtype))
            return picked.reshape(-1, values.shape[-1])
        owned_adapter_rank = jnp.sum(jnp.where(jnp.arange(ADAPTER_COUNT) == owning_replica, adapter_rank_sizes, 0))
        down_factor_weight = lax.dynamic_index_in_dim(adapter_down_factor, owning_replica, 0, keepdims=False).astype(jnp.bfloat16)
        up_factor_weight = lax.dynamic_index_in_dim(adapter_up_factor, owning_replica, 0, keepdims=False).astype(jnp.bfloat16)
        return adapter_grads(select(token_seqs), select(base_keys), select(upstream), down_factor_weight, up_factor_weight, owned_adapter_rank, key_norm_weight)
    down_factor_gradient, up_factor_gradient = lax.map(per_owner, jnp.arange(ADAPTER_COUNT).astype(jnp.int32))
    updated_down_factor, updated_down_first_moment, updated_down_second_moment = optimizer_update(adapter_down_factor, down_factor_gradient, down_first_moment, down_second_moment)
    updated_up_factor, updated_up_first_moment, updated_up_second_moment = optimizer_update(adapter_up_factor, up_factor_gradient, up_first_moment, up_second_moment)
    return (updated_down_factor, updated_up_factor, updated_down_first_moment, updated_up_first_moment, updated_down_second_moment, updated_up_second_moment)
```

```python
import jax
import jax.numpy as jnp
from jax import lax
from jax.experimental import pallas as pl
from jax.experimental.pallas import tpu as pltpu
from jax.sharding import PartitionSpec as P

MODEL_WIDTH = 5120
HEAD = 128
KEY_WIDTH = 1024
PADDED_RANK = 128
SEQ = 32
LIVE = 288
FIRST = 192
QUARTER = MODEL_WIDTH // 4


adapter_alpha_scale = 16.0
norm_epsilon = 1e-06
learn_rate = 0.001
weight_decay = 0.01
beta_one = 0.9
beta_two = 0.999
correct_one = 1.0 - 0.9**10
correct_two = 1.0 - 0.999**10
adam_epsilon = 1e-08

bf16 = jnp.bfloat16
f32 = jnp.float32
i32 = jnp.int32


def optimizer_update(weights, gradient, moment, variance):
    moment_new = beta_one * moment + (1.0 - beta_one) * gradient
    variance_new = beta_two * variance + (1.0 - beta_two) * gradient * gradient
    update = moment_new / correct_one / (jnp.sqrt(variance_new / correct_two) + adam_epsilon)
    return (weights - learn_rate * (update + weight_decay * weights), moment_new, variance_new)


def adapter_grads(
    row_tokens,
    row_base,
    row_grads,
    down_factor_weight,
    up_factor_weight,
    owned_adapter_rank,
    key_norm_weight,
):
    columns = jnp.arange(PADDED_RANK) < owned_adapter_rank
    masked_down = jnp.where(columns[None, :], down_factor_weight, jnp.zeros((), bf16))
    masked_up = jnp.where(columns[:, None], up_factor_weight, jnp.zeros((), bf16))
    adapter_scale_factor = adapter_alpha_scale / owned_adapter_rank.astype(f32)
    lowrank = jnp.dot(row_tokens, masked_down, preferred_element_type=f32).astype(bf16)
    key_rows = row_base.astype(f32) + adapter_scale_factor * jnp.dot(
        lowrank, masked_up, preferred_element_type=f32
    )
    per_head = key_rows.reshape(key_rows.shape[0], KEY_WIDTH // HEAD, HEAD)
    inverse = lax.rsqrt(jnp.mean(per_head * per_head, axis=-1, keepdims=True) + norm_epsilon)
    normed = per_head * inverse
    incoming = row_grads.astype(f32).reshape(per_head.shape) * key_norm_weight
    key_grads = inverse * (incoming - normed * jnp.mean(incoming * normed, axis=-1, keepdims=True))
    key_grads = key_grads.reshape(key_rows.shape).astype(bf16)
    up_factor_gradient = adapter_scale_factor * lax.dot_general(
        lowrank, key_grads, (((0,), (0,)), ((), ())), preferred_element_type=f32
    )
    up_factor_gradient = jnp.where(columns[:, None], up_factor_gradient, 0.0)
    low_grads = (
        adapter_scale_factor
        * lax.dot_general(key_grads, masked_up, (((1,), (1,)), ((), ())), preferred_element_type=f32)
    ).astype(bf16)
    down_factor_gradient = lax.dot_general(
        row_tokens, low_grads, (((0,), (0,)), ((), ())), preferred_element_type=f32
    )
    return (down_factor_gradient, up_factor_gradient)


def general_gradients(
    tokens,
    cotangent,
    lengths,
    slot_adapter_index,
    adapter_rank_sizes,
    frozen,
    key_norm_weight,
    adapter_down_factor,
    adapter_up_factor,
):
    data_ranks = lax.axis_size("dp")
    owning_replica = lax.axis_index("dp")
    seq_count = lengths.shape[1]
    per_pair = -(-seq_count // data_ranks)
    slot_total = data_ranks * per_pair
    token_seqs = tokens.reshape(seq_count, SEQ, MODEL_WIDTH)
    live_mask = jnp.arange(SEQ)[None, :] < lengths[0][:, None]
    upstream = jnp.where(
        live_mask[:, :, None],
        cotangent.reshape(seq_count, SEQ, KEY_WIDTH),
        jnp.zeros((), cotangent.dtype),
    )
    target = slot_adapter_index[0]
    seq_index = jnp.arange(seq_count)
    earlier = (target[None, :] == target[:, None]) & (seq_index[None, :] < seq_index[:, None])
    slot_order = jnp.sum(earlier.astype(i32), axis=1)
    slot_of = target * per_pair + slot_order
    matches = slot_of[None, :] == jnp.arange(slot_total)[:, None]
    source = jnp.sum(jnp.where(matches, seq_index[None, :], 0), axis=1)
    filled = jnp.any(matches, axis=1)

    def pack_slots(values):
        picked = jnp.take(values, source, axis=0)
        picked = jnp.where(filled[:, None, None], picked, jnp.zeros((), values.dtype))
        return picked.reshape(data_ranks, per_pair * SEQ, values.shape[-1])

    arrived_tokens, arrived_grads = (
        lax.all_to_all(pack_slots(token_seqs), "dp", split_axis=0, concat_axis=0, tiled=True),
        lax.all_to_all(pack_slots(upstream), "dp", split_axis=0, concat_axis=0, tiled=True),
    )
    row_tokens = arrived_tokens.reshape(-1, MODEL_WIDTH)
    row_base = jnp.dot(
        row_tokens,
        lax.all_gather(frozen, "fsdp", axis=0, tiled=True),
        preferred_element_type=f32,
    ).astype(bf16)
    row_grads = arrived_grads.reshape(-1, KEY_WIDTH)
    owned_adapter_rank = jnp.sum(
        jnp.where(jnp.arange(adapter_rank_sizes.shape[0]) == owning_replica, adapter_rank_sizes, 0)
    )
    full_down, full_up = (
        lax.all_gather(adapter_down_factor.astype(bf16), "fsdp", axis=1, tiled=True),
        lax.all_gather(adapter_up_factor.astype(bf16), "fsdp", axis=1, tiled=True),
    )
    down_factor_gradient, up_factor_gradient = adapter_grads(
        row_tokens,
        row_base,
        row_grads,
        full_down[0],
        full_up[0],
        owned_adapter_rank,
        key_norm_weight,
    )
    return (
        lax.psum_scatter(down_factor_gradient, "fsdp", scatter_dimension=0, tiled=True),
        lax.psum_scatter(up_factor_gradient, "fsdp", scatter_dimension=0, tiled=True),
    )


def local_general(
    tokens,
    cotangent,
    lengths,
    slot_adapter_index,
    adapter_rank_sizes,
    frozen,
    key_norm_weight,
    adapter_down_factor,
    adapter_up_factor,
    down_first_moment,
    up_first_moment,
    down_second_moment,
    up_second_moment,
):
    down_gradient, up_gradient = general_gradients(
        tokens,
        cotangent,
        lengths,
        slot_adapter_index,
        adapter_rank_sizes,
        frozen,
        key_norm_weight,
        adapter_down_factor,
        adapter_up_factor,
    )
    new_down, down_first, down_second = optimizer_update(
        adapter_down_factor[0], down_gradient, down_first_moment[0], down_second_moment[0]
    )
    new_up, up_first, up_second = optimizer_update(
        adapter_up_factor[0], up_gradient, up_first_moment[0], up_second_moment[0]
    )
    return (
        new_down[None],
        new_up[None],
        down_first[None],
        up_first[None],
        down_second[None],
        up_second[None],
    )


SMEM = pl.BlockSpec(memory_space=pltpu.SMEM)
VMEM = pl.BlockSpec(memory_space=pltpu.VMEM)
HBM = pl.BlockSpec(memory_space=pl.ANY)


def call(kernel, name, specs, outs, args, scratch=(), flops=0):
    moved = sum(a.size * a.dtype.itemsize for a in list(args) + list(outs))
    return pl.pallas_call(
        kernel,
        name=name,
        in_specs=list(specs),
        out_specs=tuple(VMEM for _ in outs),
        out_shape=tuple(outs),
        scratch_shapes=list(scratch),
        compiler_params=pltpu.CompilerParams(vmem_limit_bytes=56 * 2**20),
        cost_estimate=pl.CostEstimate(flops=flops, bytes_accessed=moved, transcendentals=0),
    )(*args)


def shape(dims, dtype):
    return jax.ShapeDtypeStruct(dims, dtype)


def packing(meta, first, rows, slots):
    token = lax.broadcasted_iota(i32, (1, slots * SEQ), 1)
    place = jnp.full((1, slots * SEQ), -1, i32)
    for s in range(slots):
        position = token - s * SEQ
        inside = (position >= 0) & (position < meta[1, s])
        place = jnp.where(inside, position + meta[0, s], place)
    row = lax.broadcasted_iota(i32, (rows, slots * SEQ), 0) + first
    return jnp.where(row == place, 1.0, 0.0).astype(bf16)


def row_adapters(meta, first, rows, slots):
    row = lax.broadcasted_iota(i32, (rows, HEAD), 0) + first
    adapter = jnp.zeros((rows, HEAD), i32)
    for s in range(slots):
        inside = (row >= meta[0, s]) & (row < meta[0, s] + meta[1, s])
        adapter = jnp.where(inside, meta[2, s], adapter)
    return adapter


def mm(a, b):
    return jnp.dot(a, b, preferred_element_type=f32)


def mm_t(a, b):
    return lax.dot_general(a, b, (((0,), (0,)), ((), ())), preferred_element_type=f32)


def mm_nt(a, b):
    return lax.dot_general(a, b, (((1,), (1,)), ((), ())), preferred_element_type=f32)


def pack_sent_kernel(slots, meta, tokens, first_out, second_out, held, sems):
    f = lax.axis_index("fsdp")
    copies = []
    for q, other in enumerate((2, 3)):
        start = pl.multiple_of((f ^ other) * QUARTER, QUARTER)
        copies.append(
            pltpu.make_async_copy(tokens.at[:, pl.ds(start, QUARTER)], held.at[q], sems.at[q])
        )
        copies[-1].start()
    chosen = packing(meta, 0, LIVE, slots)
    for q in range(2):
        copies[q].wait()
        rows = mm(chosen, held[q]).astype(bf16)
        first_out[q] = rows[:FIRST]
        second_out[q] = rows[FIRST:]


def pack_kept_kernel(slots, meta, tokens, cotangent, near_out, far_out, grads_out, held, sems):
    f = lax.axis_index("fsdp")
    copies = []
    for q in range(2):
        start = pl.multiple_of((f ^ q) * QUARTER, QUARTER)
        copies.append(
            pltpu.make_async_copy(tokens.at[:, pl.ds(start, QUARTER)], held.at[q], sems.at[q])
        )
        copies[-1].start()
    chosen = packing(meta, 0, LIVE, slots)
    grads_out[...] = mm(chosen, cotangent[...]).astype(bf16)
    copies[0].wait()
    near_out[...] = mm(chosen, held[0]).astype(bf16)
    copies[1].wait()
    far_out[...] = mm(chosen, held[1]).astype(bf16)


def weights_kernel(ranks, down, up_own, up_mate, out):
    rank = ranks[lax.axis_index("dp")]
    side = lax.axis_index("fsdp") // 2
    column = lax.broadcasted_iota(i32, (QUARTER, PADDED_RANK), 1)
    out[:QUARTER] = jnp.where(column < rank, down[...], 0.0).astype(bf16)
    own, mate = up_own[...], up_mate[...]
    zero = jnp.full((32, 1), side, i32) == 0
    low_part, high_part = jnp.where(zero, own, mate), jnp.where(zero, mate, own)
    for k in range(8):
        lanes = slice(128 * k, 128 * k + 128)
        out[QUARTER + 64 * k : QUARTER + 64 * k + 32] = low_part[:, lanes]
        out[QUARTER + 64 * k + 32 : QUARTER + 64 * k + 64] = high_part[:, lanes]


def base_mate_kernel(rows, own, mate, out):
    out[...] = (mm(rows[0], own[...]) + mm(rows[1], mate[...])).astype(bf16)


def base_own_kernel(near, far, own, mate, out):
    out[...] = mm(near[...], own[...]) + mm(far[...], mate[...])


def low_kernel(slots, meta, mate_meta, near, far, first, second, *refs):
    own, core, (kept_out, sent_out) = refs[:4], refs[4:8], refs[8:]
    down_own = jnp.concatenate([w[:QUARTER] for w in own], axis=1)
    down_core = jnp.concatenate([w[:QUARTER] for w in core], axis=1)

    def chosen(a, b, which, start, count):
        every = mm(a, down_own) + mm(b, down_core)
        adapter = row_adapters(which, start, count, slots)
        total = jnp.zeros((count, PADDED_RANK), f32)
        for j in range(4):
            total = jnp.where(adapter == j, every[:, 128 * j : 128 * j + 128], total)
        return total

    sent_out[:FIRST] = chosen(first[0], first[1], mate_meta, 0, FIRST)
    sent_out[FIRST:] = chosen(second[0], second[1], mate_meta, FIRST, LIVE - FIRST)
    kept_out[...] = chosen(near[...], far[...], meta, 0, LIVE)


def keys_kernel(slots, start, count, places, meta, ranks, base, arrived, low, low_mate, grads, gain, *refs):
    own, core = refs[:4], refs[4:8]
    has_sum = start > 0
    sums = refs[8] if has_sum else None
    refs = refs[9:] if has_sum else refs[8:]
    dlow_out, kept_out, sent_out = refs[:3]
    rest_out = None if has_sum else refs[3]
    up, total = refs[-2:]
    dp = lax.axis_index("dp")
    c = lax.axis_index("fsdp") % 2
    rows = slice(start, start + count)
    for j in range(4):
        for k in range(8):
            for part in range(2):
                source = QUARTER + 64 * k + 32 * part
                target = pl.multiple_of(128 * j + 64 * part + 32 * c, 32)
                up[pl.ds(target, 32), 128 * k : 128 * k + 128] = own[j][source : source + 32]
                target = pl.multiple_of(128 * j + 64 * part + 32 * (1 - c), 32)
                up[pl.ds(target, 32), 128 * k : 128 * k + 128] = core[j][source : source + 32]
    adapter = row_adapters(meta, start, count, slots)
    scales = [adapter_alpha_scale / jnp.full((1, HEAD), ranks[dp ^ j], i32).astype(f32) for j in range(4)]
    scale = jnp.zeros((count, HEAD), f32)
    for j in range(4):
        scale = jnp.where(adapter == j, scales[j], scale)
    lowrank = (low[rows] + low_mate[rows]).astype(bf16).astype(f32)
    spread = jnp.concatenate([jnp.where(adapter == j, lowrank, 0.0).astype(bf16) for j in range(4)], axis=1)
    added = mm(spread, up[...])
    parts = []
    for k in range(8):
        lanes = slice(128 * k, 128 * k + 128)
        held = (base[rows, lanes] + arrived[:, lanes].astype(f32)).astype(bf16).astype(f32)
        head = held + scale * added[:, lanes]
        inverse = lax.rsqrt(jnp.mean(head * head, axis=-1, keepdims=True) + norm_epsilon)
        normed = head * inverse
        incoming = grads[rows, lanes].astype(f32) * gain[...]
        mean = jnp.mean(incoming * normed, axis=-1, keepdims=True)
        parts.append((inverse * (incoming - normed * mean)).astype(bf16))
    key_grads = jnp.concatenate(parts, axis=1)
    every = mm_nt(key_grads, up[...])
    picked = jnp.zeros((count, PADDED_RANK), f32)
    for j in range(4):
        picked = jnp.where(adapter == j, every[:, 128 * j : 128 * j + 128], picked)
    dlow_out[...] = (scale * picked).astype(bf16)
    total[...] = mm_t(spread, key_grads)
    for i, j in enumerate(places):
        scale_j = scales[j][0:1, 0:1]
        for part in range(2):
            kept = pl.multiple_of(128 * j + 64 * part + 32 * c, 32)
            sent = pl.multiple_of(128 * j + 64 * part + 32 * (1 - c), 32)
            here = slice(32 * part, 32 * part + 32)
            one, two = total[pl.ds(kept, 32), :], total[pl.ds(sent, 32), :]
            if has_sum:
                one = one + sums[pl.ds(pl.multiple_of(kept, 32), 32), :]
                two = two + sums[pl.ds(pl.multiple_of(sent, 32), 32), :]
            kept_out[i, here, :] = one * scale_j
            sent_out[i, here, :] = two * scale_j
    if rest_out is not None:
        rest_out[...] = total[:256]


def up_kernel(kept, arrived, own_out, mate_out):
    x = lax.axis_index("fsdp") // 2
    for i in range(kept.shape[0]):
        here = pl.ds(pl.multiple_of(32 * x, 32), 32)
        there = pl.ds(pl.multiple_of(32 * (1 - x), 32), 32)
        own_out[i] = kept[i, here, :] + arrived[i, here, :]
        mate_out[i] = (kept[i, there, :] + arrived[i, there, :]).astype(bf16)


def down_kernel(slots, spans, places, metas, up_own, up_arrived, *refs):
    number = 4 * len(spans)
    tokens, dlows, outs = refs[:number], refs[number : 2 * number], refs[2 * number :]
    total = jnp.zeros((QUARTER, 128 * len(places)), f32)
    lhs, rhs = [], []
    for device in range(4):
        for n, (start, count) in enumerate(spans):
            dlow = dlows[device * len(spans) + n][...].astype(f32)
            adapter = row_adapters(metas.at[device], start, count, slots)
            rhs.append(
                jnp.concatenate([jnp.where(adapter == j, dlow, 0.0).astype(bf16) for j in places], axis=1)
            )
            held = tokens[device * len(spans) + n]
            lhs.append(held[0] if len(held.shape) == 3 else held[start : start + count])
    total = mm_t(jnp.concatenate(lhs, axis=0), jnp.concatenate(rhs, axis=0))
    for i, _ in enumerate(places):
        outs[i][:QUARTER] = total[:, 128 * i : 128 * i + 128].astype(outs[i].dtype)
        rows = up_own[i] + up_arrived[i].astype(f32)
        for k in range(8):
            outs[i][QUARTER + 32 * k : QUARTER + 32 * k + 32] = rows[:, 128 * k : 128 * k + 128].astype(
                outs[i].dtype
            )


def update_kernel(own, one, two, three, *refs):
    (down, up, down_m, up_m, down_v, up_v), outs = refs[:6], refs[6:]

    def gradient(rows):
        return own[rows] + one[rows].astype(f32) + (two[rows].astype(f32) + three[rows].astype(f32))

    step = 256
    for start in range(0, QUARTER, step):
        rows = slice(start, start + step)
        outs[0][rows], outs[2][rows], outs[4][rows] = optimizer_update(
            down[rows], gradient(rows), down_m[rows], down_v[rows]
        )
    for k in range(8):
        lanes = slice(128 * k, 128 * k + 128)
        rows = slice(QUARTER + 32 * k, QUARTER + 32 * k + 32)
        outs[1][:, lanes], outs[3][:, lanes], outs[5][:, lanes] = optimizer_update(
            up[:, lanes], gradient(rows), up_m[:, lanes], up_v[:, lanes]
        )


def after(value, *others):
    return lax.optimization_barrier((value,) + others)[0]


def local(
    tokens,
    cotangent,
    lengths,
    slot_adapter_index,
    adapter_rank_sizes,
    frozen,
    key_norm_weight,
    adapter_down_factor,
    adapter_up_factor,
    down_first_moment,
    up_first_moment,
    down_second_moment,
    up_second_moment,
):
    dp = lax.axis_index("dp")
    f = lax.axis_index("fsdp")
    slots = lengths.shape[1]

    def core(value):
        return lax.ppermute(value, "fsdp", [(i, i ^ 1) for i in range(4)])

    def across(value):
        return lax.ppermute(value, "fsdp", [(i, i ^ 2) for i in range(4)])

    def along(value, distance):
        return lax.ppermute(value, "dp", [(i, i ^ distance) for i in range(4)])

    place = slot_adapter_index[0] ^ dp
    key = (3 - place) * slots + jnp.arange(slots, dtype=i32)
    offset = jnp.sum(jnp.where(key[None, :] < key[:, None], lengths[0][None, :], 0), axis=1)
    meta = jnp.stack([offset, lengths[0], place])

    first, second = call(
        lambda *refs: pack_sent_kernel(slots, *refs),
        "pack_sent",
        [SMEM, HBM],
        [shape((2, FIRST, QUARTER), bf16), shape((2, LIVE - FIRST, QUARTER), bf16)],
        [meta, tokens],
        [pltpu.VMEM((2, tokens.shape[0], QUARTER), bf16), pltpu.SemaphoreType.DMA((2,))],
        flops=2 * LIVE * tokens.shape[0] * 2 * QUARTER,
    )
    first_in = across(first)
    second_in = across(second)

    rank = adapter_rank_sizes[dp]
    up_rows = f * 32 + jnp.arange(32)
    up_own = jnp.where((up_rows < rank)[:, None], adapter_up_factor[0], 0.0).astype(bf16)
    up_mate = across(up_own)
    (message,) = call(
        weights_kernel,
        "weights",
        [SMEM, VMEM, VMEM, VMEM],
        [shape((QUARTER + 512, PADDED_RANK), bf16)],
        [adapter_rank_sizes, adapter_down_factor[0], up_own, up_mate],
    )
    weights = [message, along(message, 1), along(message, 2), along(message, 3)]

    frozen_core = core(frozen)
    near, far, grads = call(
        lambda *refs: pack_kept_kernel(slots, *refs),
        "pack_kept",
        [SMEM, HBM, VMEM],
        [shape((LIVE, QUARTER), bf16), shape((LIVE, QUARTER), bf16), shape((LIVE, KEY_WIDTH), bf16)],
        [meta, tokens, cotangent],
        [pltpu.VMEM((2, tokens.shape[0], QUARTER), bf16), pltpu.SemaphoreType.DMA((2,))],
        flops=2 * LIVE * tokens.shape[0] * 2 * QUARTER,
    )
    far_core = core(far)
    mate_meta = across(meta)
    core_metas = core(jnp.stack([meta, mate_meta]))
    metas = jnp.concatenate([jnp.stack([meta, mate_meta]), core_metas])

    (base,) = call(
        base_own_kernel,
        "base_own",
        [VMEM] * 4,
        [shape((LIVE, KEY_WIDTH), f32)],
        [near, far, frozen, frozen_core],
        flops=2 * LIVE * 2 * QUARTER * KEY_WIDTH,
    )
    returned = []
    for rows in (first_in, second_in):
        (partial,) = call(
            base_mate_kernel,
            "base_mate",
            [VMEM] * 3,
            [shape((rows.shape[1], KEY_WIDTH), bf16)],
            [rows, frozen, frozen_core],
            flops=2 * rows.shape[1] * 2 * QUARTER * KEY_WIDTH,
        )
        returned.append(across(partial))
    first_core, second_core = core(first_in[1]), core(second_in[1])

    weights_core = [core(w) for w in weights]
    low, low_sent = call(
        lambda *refs: low_kernel(slots, *refs),
        "low",
        [SMEM, SMEM] + [VMEM] * 12,
        [shape((LIVE, PADDED_RANK), f32), shape((LIVE, PADDED_RANK), f32)],
        [meta, mate_meta, near, far, first_in, second_in] + weights + weights_core,
        flops=2 * 2 * LIVE * 2 * QUARTER * 512,
    )
    low_mate = across(low_sent)

    gain = key_norm_weight[None, :]

    def keys(start, count, places, arrived, sums):
        outs = [
            shape((count, PADDED_RANK), bf16),
            shape((len(places), 64, KEY_WIDTH), f32),
            shape((len(places), 64, KEY_WIDTH), f32),
        ]
        if not sums:
            outs.append(shape((256, KEY_WIDTH), f32))
        return call(
            lambda *refs: keys_kernel(slots, start, count, places, *refs),
            "keys",
            [SMEM, SMEM] + [VMEM] * (14 + len(sums)),
            outs,
            [meta, adapter_rank_sizes, base, arrived, low, low_mate, grads, gain]
            + weights
            + weights_core
            + sums,
            [pltpu.VMEM((512, KEY_WIDTH), bf16), pltpu.VMEM((512, KEY_WIDTH), f32)],
            flops=3 * 2 * count * 512 * KEY_WIDTH,
        )

    def exchange_low(dlow):
        mate = across(dlow)
        pair = core(jnp.stack([dlow, mate]))
        return [dlow, mate, pair[0], pair[1]]

    def exchange_up(kept, sent):
        own, mate = call(
            up_kernel,
            "up",
            [VMEM] * 2,
            [shape((kept.shape[0], 32, KEY_WIDTH), f32), shape((kept.shape[0], 32, KEY_WIDTH), bf16)],
            [kept, core(sent)],
        )
        return own, across(mate)

    def down(spans, places, up_parts, held, dlows, types):
        return call(
            lambda *refs: down_kernel(slots, spans, places, *refs),
            "down",
            [SMEM] + [VMEM] * (2 + len(held) + len(dlows)),
            [shape((QUARTER + 256, PADDED_RANK), t) for t in types],
            [metas, *up_parts, *held, *dlows],
            flops=2 * 4 * sum(n for _, n in spans) * QUARTER * 128 * len(places),
        )

    dlow_one, kept, sent, rest = keys(0, FIRST, (3, 2), returned[0], [])
    up_parts = exchange_up(kept, sent)
    dlow_first = exchange_low(dlow_one)
    head = ((0, FIRST),)
    first_core, far_core3 = first_core[None], far_core
    three, two = down(head, (3, 2), up_parts, [near, first_in, far_core3, first_core], dlow_first, [bf16, bf16])
    three_in = along(three, 3)
    two_in = along(two, 2)

    dlow_two, kept, sent = keys(FIRST, LIVE - FIRST, (1, 0), returned[1], [rest])
    up_parts = exchange_up(kept, sent)
    dlow_second = exchange_low(dlow_two)
    both = ((0, FIRST), (FIRST, LIVE - FIRST))
    held = [near, near, first_in, second_in, far_core3, far_core3, first_core, second_core[None]]
    dlows = [d for pair in zip(dlow_first, dlow_second) for d in pair]
    one, own = down(both, (1, 0), up_parts, held, dlows, [bf16, f32])
    one_in = along(one, 1)

    outs = call(
        update_kernel,
        "update",
        [VMEM] * 10,
        [shape(adapter_down_factor.shape[1:], f32), shape(adapter_up_factor.shape[1:], f32)] * 3,
        [own, one_in, two_in, three_in]
        + [
            a[0]
            for a in (
                adapter_down_factor,
                adapter_up_factor,
                down_first_moment,
                up_first_moment,
                down_second_moment,
                up_second_moment,
            )
        ],
    )
    return tuple(o[None] for o in outs)


def solution(mesh):
    paired = mesh.shape["dp"] == 4 and mesh.shape["fsdp"] == 4
    return jax.shard_map(
        local if paired else local_general,
        mesh=mesh,
        in_specs=(
            P(("parts", "dp", "fsdp"), None),
            P(("parts", "dp", "fsdp"), None),
            P(("parts", "dp", "fsdp"), None),
            P(("parts", "dp", "fsdp"), None),
            P(),
            P("fsdp", None),
            P(),
            P(("parts", "dp"), "fsdp", None),
            P(("parts", "dp"), "fsdp", None),
            P(("parts", "dp"), "fsdp", None),
            P(("parts", "dp"), "fsdp", None),
            P(("parts", "dp"), "fsdp", None),
            P(("parts", "dp"), "fsdp", None),
        ),
        out_specs=(
            P(("parts", "dp"), "fsdp", None),
            P(("parts", "dp"), "fsdp", None),
            P(("parts", "dp"), "fsdp", None),
            P(("parts", "dp"), "fsdp", None),
            P(("parts", "dp"), "fsdp", None),
            P(("parts", "dp"), "fsdp", None),
        ),
        check_vma=False,
    )
```

```python
import jax
import jax.numpy as jnp
from jax import lax
from jax.experimental import pallas as pl
from jax.experimental.pallas import tpu as pltpu
from jax.sharding import PartitionSpec as P

MODEL_WIDTH = 5120
HEAD = 128
KEY_WIDTH = 1024
PADDED_RANK = 128
SEQ = 32
LIVE = 288
QUARTER = MODEL_WIDTH // 4


adapter_alpha_scale = 16.0
norm_epsilon = 1e-06
learn_rate = 0.001
weight_decay = 0.01
beta_one = 0.9
beta_two = 0.999
correct_one = 1.0 - 0.9**10
correct_two = 1.0 - 0.999**10
adam_epsilon = 1e-08

bf16 = jnp.bfloat16
f32 = jnp.float32
i32 = jnp.int32


def optimizer_update(weights, gradient, moment, variance):
    moment_new = beta_one * moment + (1.0 - beta_one) * gradient
    variance_new = beta_two * variance + (1.0 - beta_two) * gradient * gradient
    update = moment_new / correct_one / (jnp.sqrt(variance_new / correct_two) + adam_epsilon)
    return (weights - learn_rate * (update + weight_decay * weights), moment_new, variance_new)


def adapter_grads(
    row_tokens,
    row_base,
    row_grads,
    down_factor_weight,
    up_factor_weight,
    owned_adapter_rank,
    key_norm_weight,
):
    columns = jnp.arange(PADDED_RANK) < owned_adapter_rank
    masked_down = jnp.where(columns[None, :], down_factor_weight, jnp.zeros((), bf16))
    masked_up = jnp.where(columns[:, None], up_factor_weight, jnp.zeros((), bf16))
    adapter_scale_factor = adapter_alpha_scale / owned_adapter_rank.astype(f32)
    lowrank = jnp.dot(row_tokens, masked_down, preferred_element_type=f32).astype(bf16)
    key_rows = row_base.astype(f32) + adapter_scale_factor * jnp.dot(
        lowrank, masked_up, preferred_element_type=f32
    )
    per_head = key_rows.reshape(key_rows.shape[0], KEY_WIDTH // HEAD, HEAD)
    inverse = lax.rsqrt(jnp.mean(per_head * per_head, axis=-1, keepdims=True) + norm_epsilon)
    normed = per_head * inverse
    incoming = row_grads.astype(f32).reshape(per_head.shape) * key_norm_weight
    key_grads = inverse * (incoming - normed * jnp.mean(incoming * normed, axis=-1, keepdims=True))
    key_grads = key_grads.reshape(key_rows.shape).astype(bf16)
    up_factor_gradient = adapter_scale_factor * lax.dot_general(
        lowrank, key_grads, (((0,), (0,)), ((), ())), preferred_element_type=f32
    )
    up_factor_gradient = jnp.where(columns[:, None], up_factor_gradient, 0.0)
    low_grads = (
        adapter_scale_factor
        * lax.dot_general(key_grads, masked_up, (((1,), (1,)), ((), ())), preferred_element_type=f32)
    ).astype(bf16)
    down_factor_gradient = lax.dot_general(
        row_tokens, low_grads, (((0,), (0,)), ((), ())), preferred_element_type=f32
    )
    return (down_factor_gradient, up_factor_gradient)


def general_gradients(
    tokens,
    cotangent,
    lengths,
    slot_adapter_index,
    adapter_rank_sizes,
    frozen,
    key_norm_weight,
    adapter_down_factor,
    adapter_up_factor,
):
    data_ranks = lax.axis_size("dp")
    owning_replica = lax.axis_index("dp")
    seq_count = lengths.shape[1]
    per_pair = -(-seq_count // data_ranks)
    slot_total = data_ranks * per_pair
    token_seqs = tokens.reshape(seq_count, SEQ, MODEL_WIDTH)
    live_mask = jnp.arange(SEQ)[None, :] < lengths[0][:, None]
    upstream = jnp.where(
        live_mask[:, :, None],
        cotangent.reshape(seq_count, SEQ, KEY_WIDTH),
        jnp.zeros((), cotangent.dtype),
    )
    target = slot_adapter_index[0]
    seq_index = jnp.arange(seq_count)
    earlier = (target[None, :] == target[:, None]) & (seq_index[None, :] < seq_index[:, None])
    slot_order = jnp.sum(earlier.astype(i32), axis=1)
    slot_of = target * per_pair + slot_order
    matches = slot_of[None, :] == jnp.arange(slot_total)[:, None]
    source = jnp.sum(jnp.where(matches, seq_index[None, :], 0), axis=1)
    filled = jnp.any(matches, axis=1)

    def pack_slots(values):
        picked = jnp.take(values, source, axis=0)
        picked = jnp.where(filled[:, None, None], picked, jnp.zeros((), values.dtype))
        return picked.reshape(data_ranks, per_pair * SEQ, values.shape[-1])

    arrived_tokens, arrived_grads = (
        lax.all_to_all(pack_slots(token_seqs), "dp", split_axis=0, concat_axis=0, tiled=True),
        lax.all_to_all(pack_slots(upstream), "dp", split_axis=0, concat_axis=0, tiled=True),
    )
    row_tokens = arrived_tokens.reshape(-1, MODEL_WIDTH)
    row_base = jnp.dot(
        row_tokens,
        lax.all_gather(frozen, "fsdp", axis=0, tiled=True),
        preferred_element_type=f32,
    ).astype(bf16)
    row_grads = arrived_grads.reshape(-1, KEY_WIDTH)
    owned_adapter_rank = jnp.sum(
        jnp.where(jnp.arange(adapter_rank_sizes.shape[0]) == owning_replica, adapter_rank_sizes, 0)
    )
    full_down, full_up = (
        lax.all_gather(adapter_down_factor.astype(bf16), "fsdp", axis=1, tiled=True),
        lax.all_gather(adapter_up_factor.astype(bf16), "fsdp", axis=1, tiled=True),
    )
    down_factor_gradient, up_factor_gradient = adapter_grads(
        row_tokens,
        row_base,
        row_grads,
        full_down[0],
        full_up[0],
        owned_adapter_rank,
        key_norm_weight,
    )
    return (
        lax.psum_scatter(down_factor_gradient, "fsdp", scatter_dimension=0, tiled=True),
        lax.psum_scatter(up_factor_gradient, "fsdp", scatter_dimension=0, tiled=True),
    )


def local_general(
    tokens,
    cotangent,
    lengths,
    slot_adapter_index,
    adapter_rank_sizes,
    frozen,
    key_norm_weight,
    adapter_down_factor,
    adapter_up_factor,
    down_first_moment,
    up_first_moment,
    down_second_moment,
    up_second_moment,
):
    down_gradient, up_gradient = general_gradients(
        tokens,
        cotangent,
        lengths,
        slot_adapter_index,
        adapter_rank_sizes,
        frozen,
        key_norm_weight,
        adapter_down_factor,
        adapter_up_factor,
    )
    new_down, down_first, down_second = optimizer_update(
        adapter_down_factor[0], down_gradient, down_first_moment[0], down_second_moment[0]
    )
    new_up, up_first, up_second = optimizer_update(
        adapter_up_factor[0], up_gradient, up_first_moment[0], up_second_moment[0]
    )
    return (
        new_down[None],
        new_up[None],
        down_first[None],
        up_first[None],
        down_second[None],
        up_second[None],
    )


SMEM = pl.BlockSpec(memory_space=pltpu.SMEM)
VMEM = pl.BlockSpec(memory_space=pltpu.VMEM)
HBM = pl.BlockSpec(memory_space=pl.ANY)


class Late:
    def __init__(self, source, target, sem):
        self.copy, self.target, self.waited = pltpu.make_async_copy(source, target, sem), target, False
        self.copy.start()

    def get(self):
        if not self.waited:
            self.copy.wait()
            self.waited = True
        return self.target


def call(kernel, name, scalars, late, outs, plain=(), order=(), scratch=()):
    n, m, p, d, o = len(scalars), len(late), len(plain), len(order), len(outs)

    def body(*refs):
        ins, rest = refs[: n + m + p], refs[n + m + p + d :]
        outputs, held, sems, scratches = rest[:o], rest[o : o + m], rest[o + m], rest[o + m + 1 :]
        lates = [Late(ins[n + i], held[i], sems.at[i]) for i in range(m)]
        kernel(*ins[:n], *lates, *ins[n + m :], *outputs, *scratches)
        for one in lates:
            one.get()

    args = list(scalars) + list(late) + list(plain) + list(order)
    moved = sum(a.size * a.dtype.itemsize for a in list(scalars) + list(late) + list(plain) + list(outs))
    return pl.pallas_call(
        body,
        name=name,
        in_specs=[SMEM] * n + [HBM] * (m + p + d),
        out_specs=tuple(VMEM for _ in outs),
        out_shape=tuple(outs),
        scratch_shapes=[pltpu.VMEM(a.shape, a.dtype) for a in late]
        + [pltpu.SemaphoreType.DMA((max(m, 1),))]
        + list(scratch),
        compiler_params=pltpu.CompilerParams(vmem_limit_bytes=36 * 2**20),
        cost_estimate=pl.CostEstimate(flops=3 * 10**10, bytes_accessed=moved, transcendentals=0),
    )(*args)


def shape(dims, dtype):
    return jax.ShapeDtypeStruct(dims, dtype)


def offsets(place, length, slots):
    found = []
    for s in range(slots):
        total = jnp.int32(0)
        for t in range(slots):
            if t != s:
                first = place[t] > place[s] if t > s else place[t] >= place[s]
                total = total + jnp.where(first, length[t], 0)
        found.append(total)
    return found


def slot_places(lengths, adapters, slots):
    dp = lax.axis_index("dp")
    place = [adapters[0, s] ^ dp for s in range(slots)]
    length = [lengths[0, s] for s in range(slots)]
    return place, length, offsets(place, length, slots)


def packing(place, length, start, slots):
    token = lax.broadcasted_iota(i32, (1, slots * SEQ), 1)
    row_of = jnp.full((1, slots * SEQ), -1, i32)
    for s in range(slots):
        position = token - s * SEQ
        inside = (position >= 0) & (position < length[s])
        row_of = jnp.where(inside, position + start[s], row_of)
    row = lax.broadcasted_iota(i32, (LIVE, slots * SEQ), 0)
    return jnp.where(row == row_of, 1.0, 0.0).astype(bf16)


def row_places(place, length, start, slots):
    row = lax.broadcasted_iota(i32, (LIVE, HEAD), 0)
    found = jnp.zeros((LIVE, HEAD), f32)
    for s in range(slots):
        inside = (row >= start[s]) & (row < start[s] + length[s])
        found = jnp.where(inside, place[s].astype(f32), found)
    return found.astype(bf16)


def mm(a, b):
    return jnp.dot(a, b, preferred_element_type=f32)


def mm_nt(a, b):
    return lax.dot_general(a, b, (((1,), (1,)), ((), ())), preferred_element_type=f32)


def quarter_copies(tokens, held, sems, others):
    f = lax.axis_index("fsdp")
    copies = []
    for n, other in enumerate(others):
        start = pl.multiple_of((f ^ other) * QUARTER, QUARTER)
        copies.append(pltpu.make_async_copy(tokens.at[:, pl.ds(start, QUARTER)], held.at[n], sems.at[n]))
        copies[-1].start()
    return copies


def pack_sent_kernel(slots, lengths, adapters, tokens, out, held, sems):
    copies = quarter_copies(tokens, held, sems, (2, 3))
    found = slot_places(lengths, adapters, slots)
    chosen = packing(*found, slots)
    ids = row_places(*found, slots)
    for q in range(2):
        for b in range(10):
            at = min(16 * (10 * q + b), LIVE - 16)
            out[q, LIVE:, 128 * b : 128 * b + 128] = ids[at : at + 16]
        copies[q].wait()
        out[q, :LIVE] = mm(chosen, held[q]).astype(bf16)


def pack_kept_kernel(slots, lengths, adapters, cotangent, tokens, near_out, far_out, grads_out, held, sems):
    copies = quarter_copies(tokens, held, sems, (0, 1))
    found = slot_places(lengths, adapters, slots)
    chosen = packing(*found, slots)
    far_out[:, QUARTER:] = row_places(*found, slots)
    copies[0].wait()
    near_out[...] = mm(chosen, held[0]).astype(bf16)
    copies[1].wait()
    far_out[:, :QUARTER] = mm(chosen, held[1]).astype(bf16)
    grads_out[...] = mm(chosen, cotangent.get()[...]).astype(bf16)


def down_mask_kernel(ranks, down, out):
    rank = ranks[lax.axis_index("dp")]
    column = lax.broadcasted_iota(i32, (QUARTER, PADDED_RANK), 1)
    masked = jnp.where(column < rank, down.get()[...], 0.0).astype(bf16)
    for i in range(4):
        out[i] = masked


def up_mask_kernel(ranks, own, mate, out):
    rank = ranks[lax.axis_index("dp")]
    f = lax.axis_index("fsdp")
    row = lax.broadcasted_iota(i32, (32, KEY_WIDTH), 0)
    own_rows = jnp.where(row + 32 * f < rank, own.get()[...], 0.0).astype(bf16)
    mate_rows = jnp.where(row + 32 * (f ^ 2) < rank, mate.get()[...], 0.0).astype(bf16)
    for i in range(4):
        out[i, 0] = own_rows
        out[i, 1] = mate_rows


def base_left_kernel(rows, own, mate, out):
    half = KEY_WIDTH // 2
    total = mm(rows.get()[0, :LIVE], own.get()[:, :half])
    out[...] = (total + mm(rows.get()[1, :LIVE], mate.get()[:, :half])).astype(bf16)


def down_factors(held):
    dp = lax.axis_index("dp")
    return jnp.concatenate([held.get()[dp ^ j] for j in range(4)], axis=1)


def mate_places(rows):
    blocks = [rows[n // 10, LIVE:, 128 * (n % 10) : 128 * (n % 10) + 128] for n in range(LIVE // 16)]
    return jnp.concatenate(blocks, axis=0)


def own_adapter(every, places):
    adapter = places.astype(f32)
    total = jnp.zeros((LIVE, PADDED_RANK), f32)
    for j in range(4):
        total = jnp.where(adapter == j, every[:, 128 * j : 128 * j + 128], total)
    return total


def mate_kernel(rows, own, mate, downs, downs_core, out, core_out):
    half = KEY_WIDTH // 2
    held = rows.get()
    places = mate_places(held)
    core_out[:, :QUARTER] = held[1, :LIVE]
    core_out[:, QUARTER:] = places
    total = mm(held[0, :LIVE], own.get()[:, half:]) + mm(held[1, :LIVE], mate.get()[:, half:])
    out[:, :half] = total.astype(bf16)
    every = mm(held[0, :LIVE], down_factors(downs)) + mm(held[1, :LIVE], down_factors(downs_core))
    low = own_adapter(every, places)
    high = low.astype(bf16)
    out[:, half : half + 128] = high
    out[:, half + 128 :] = (low - high.astype(f32)).astype(bf16)


def base_own_kernel(near, own, far, mate, out):
    total = mm(near.get()[...], own.get()[...])
    out[...] = total + mm(far.get()[:, :QUARTER], mate.get()[...])


def low_own_kernel(near, far, downs, downs_core, out):
    held = far.get()
    every = mm(near.get()[...], down_factors(downs)) + mm(held[:, :QUARTER], down_factors(downs_core))
    out[...] = own_adapter(every, held[:, QUARTER:])


def identity():
    row = lax.broadcasted_iota(i32, (HEAD, HEAD), 0)
    return jnp.where(row == lax.broadcasted_iota(i32, (HEAD, HEAD), 1), 1.0, 0.0).astype(bf16)


def spread(values, places, which):
    adapter, value = places.astype(f32), values.astype(f32)
    return jnp.concatenate([jnp.where(adapter == j, value, 0.0).astype(bf16) for j in which], axis=1)


def transposed(values):
    unit = identity()
    parts = [mm_nt(unit, values[:, n : n + 128]).astype(bf16) for n in range(0, values.shape[1], 128)]
    return jnp.concatenate(parts, axis=0)


def keys_kernel(ranks, far, low, right, ups, ups_core, base, left, grads, gain, *refs):
    dlow_out, kept_out, sent_out, up, total = refs
    dp = lax.axis_index("dp")
    f = lax.axis_index("fsdp")
    c, x = f % 2, f // 2
    for j in range(4):
        for part in range(2):
            for held, side in ((ups, c), (ups_core, 1 - c)):
                target = 128 * j + 64 * (x ^ part) + 32 * side
                up[pl.ds(pl.multiple_of(target, 32), 32), :] = held.get()[dp ^ j, part]
    ids = far.get()[:, QUARTER:]
    adapter = ids.astype(f32)
    scales = [adapter_alpha_scale / jnp.full((1, HEAD), ranks[dp ^ j], i32).astype(f32) for j in range(4)]
    scale = jnp.zeros((LIVE, HEAD), f32)
    for j in range(4):
        scale = jnp.where(adapter == j, scales[j], scale)
    half = KEY_WIDTH // 2
    arrived = right.get()[:, half:].astype(f32)
    lowrank = (low.get()[...] + (arrived[:, :128] + arrived[:, 128:])).astype(bf16).astype(f32)
    wide = spread(lowrank, ids, range(4))
    added = mm(wide, up[...])
    parts = []
    for k in range(8):
        lanes = slice(128 * k, 128 * k + 128)
        source = left.get()[:, lanes] if k < 4 else right.get()[:, 128 * k - half : 128 * k - half + 128]
        arrived = source.astype(f32)
        held = (base.get()[:, lanes] + arrived).astype(bf16).astype(f32)
        head = held + scale * added[:, lanes]
        inverse = lax.rsqrt(jnp.mean(head * head, axis=-1, keepdims=True) + norm_epsilon)
        normed = head * inverse
        incoming = grads.get()[:, lanes].astype(f32) * gain.get()[...]
        mean = jnp.mean(incoming * normed, axis=-1, keepdims=True)
        parts.append((inverse * (incoming - normed * mean)).astype(bf16))
    key_grads = jnp.concatenate(parts, axis=1)
    every = mm_nt(key_grads, up[...])
    picked = jnp.zeros((LIVE, PADDED_RANK), f32)
    for j in range(4):
        picked = jnp.where(adapter == j, every[:, 128 * j : 128 * j + 128], picked)
    dlow_out[...] = (scale * picked).astype(bf16)
    total[...] = mm(transposed(wide), key_grads)
    for j in range(4):
        scale_j = scales[j][0:1, 0:1]
        for part in range(2):
            kept = pl.multiple_of(128 * j + 64 * (x ^ part) + 32 * c, 32)
            sent = pl.multiple_of(128 * j + 64 * (x ^ part) + 32 * (1 - c), 32)
            kept_out[part, j] = total[pl.ds(kept, 32), :] * scale_j
            sent_out[part, j] = total[pl.ds(sent, 32), :] * scale_j


def up_core_kernel(kept, arrived, own_out, mate_out):
    own_out[...] = kept.get()[0] + arrived.get()[0]
    mate_out[...] = (kept.get()[1] + arrived.get()[1]).astype(bf16)


def up_across_kernel(own, arrived, own_out, one_out, two_out, three_out):
    for j, out in enumerate((own_out, one_out, two_out, three_out)):
        out[...] = (own.get()[j] + arrived.get()[j].astype(f32)).astype(out.dtype)


def down_kernel(dlow, dlow_mate, dlow_core, dlow_cross, rows, near, far, far_core, cross, *refs):
    outs, (held, ids, sems) = refs[:4], refs[4:]
    copies = [pltpu.make_async_copy(far.at[:, pl.ds(QUARTER, 128)], ids.at[pl.ds(0, LIVE), :], sems.at[0])]
    copies.append(
        pltpu.make_async_copy(far_core.at[:, pl.ds(QUARTER, 128)], ids.at[pl.ds(2 * LIVE, LIVE), :], sems.at[1])
    )
    copies.append(
        pltpu.make_async_copy(cross.at[:, pl.ds(QUARTER, 128)], ids.at[pl.ds(3 * LIVE, LIVE), :], sems.at[2])
    )
    sources = [near, None, far_core.at[:, pl.ds(0, QUARTER)], cross.at[:, pl.ds(0, QUARTER)]]
    for n, source in enumerate(sources):
        if source is not None:
            copies.append(pltpu.make_async_copy(source, held.at[pl.ds(n * LIVE, LIVE), :], sems.at[3 + n]))
    for copy in copies:
        copy.start()
    held[LIVE : 2 * LIVE, :] = rows.get()[0, :LIVE]
    ids[LIVE : 2 * LIVE, :] = mate_places(rows.get())
    for copy in copies[:3]:
        copy.wait()
    lows = jnp.concatenate([d.get()[...] for d in (dlow, dlow_mate, dlow_core, dlow_cross)], axis=0)
    wide = transposed(spread(lows, ids[...], range(4)))
    for copy in copies[3:]:
        copy.wait()
    for j, out in enumerate(outs):
        out[...] = mm(wide[128 * j : 128 * j + 128], held[...]).astype(out.dtype)


def update_kernel(*refs):
    own, one, two, three, down, moment, variance = refs[:7]
    outs = refs[14:]
    for start in range(0, QUARTER, 128):
        part = slice(start, start + 128)
        total = own.get()[:, part] + one.get()[:, part].astype(f32)
        total = total + (two.get()[:, part].astype(f32) + three.get()[:, part].astype(f32))
        outs[0][part], outs[1][part], outs[2][part] = optimizer_update(
            down.get()[part], total.T, moment.get()[part], variance.get()[part]
        )
    own, one, two, three, up, moment, variance = refs[7:14]
    total = own.get()[...] + one.get()[...].astype(f32)
    total = total + (two.get()[...].astype(f32) + three.get()[...].astype(f32))
    outs[3][...], outs[4][...], outs[5][...] = optimizer_update(
        up.get()[...], total, moment.get()[...], variance.get()[...]
    )


def after(value, *others):
    return lax.optimization_barrier((value, *others))[0]


def local(
    tokens,
    cotangent,
    lengths,
    slot_adapter_index,
    adapter_rank_sizes,
    frozen,
    key_norm_weight,
    adapter_down_factor,
    adapter_up_factor,
    down_first_moment,
    up_first_moment,
    down_second_moment,
    up_second_moment,
):
    dp = lax.axis_index("dp")
    slots = lengths.shape[1]
    ranks = adapter_rank_sizes

    def core(value):
        return lax.ppermute(value, "fsdp", [(i, i ^ 1) for i in range(4)])

    def across(value):
        return lax.ppermute(value, "fsdp", [(i, i ^ 2) for i in range(4)])

    def along(value, distance):
        return lax.ppermute(value, "dp", [(i, i ^ distance) for i in range(4)])

    def exchange(value):
        return lax.all_to_all(value, "dp", split_axis=0, concat_axis=0, tiled=True)

    frozen_core = core(frozen)
    up_mate = across(adapter_up_factor[0])
    (sent,) = call(
        lambda *refs: pack_sent_kernel(slots, *refs),
        "pack_sent",
        [lengths, slot_adapter_index],
        [],
        [shape((2, LIVE + 16, QUARTER), bf16)],
        [tokens],
        scratch=[pltpu.VMEM((2, tokens.shape[0], QUARTER), bf16), pltpu.SemaphoreType.DMA((2,))],
    )
    rows = across(sent)

    (masked,) = call(
        down_mask_kernel,
        "down_mask",
        [ranks],
        [adapter_down_factor[0]],
        [shape((4, QUARTER, PADDED_RANK), bf16)],
        order=[sent],
    )
    downs = exchange(masked)
    near, far, grads = call(
        lambda *refs: pack_kept_kernel(slots, *refs),
        "pack_kept",
        [lengths, slot_adapter_index],
        [cotangent],
        [
            shape((LIVE, QUARTER), bf16),
            shape((LIVE, QUARTER + 128), bf16),
            shape((LIVE, KEY_WIDTH), bf16),
        ],
        [tokens],
        order=[masked, frozen_core],
        scratch=[pltpu.VMEM((2, tokens.shape[0], QUARTER), bf16), pltpu.SemaphoreType.DMA((2,))],
    )
    far_core = core(far)

    (base,) = call(
        base_own_kernel,
        "base_own",
        [],
        [near, frozen, far, frozen_core],
        [shape((LIVE, KEY_WIDTH), f32)],
    )
    (up_pair,) = call(
        up_mask_kernel,
        "up_mask",
        [ranks],
        [adapter_up_factor[0], up_mate],
        [shape((4, 2, 32, KEY_WIDTH), bf16)],
        order=[base, far_core],
    )
    ups = exchange(up_pair)
    downs = after(downs, base)
    downs_core = core(downs)
    (left,) = call(
        base_left_kernel,
        "base_left",
        [],
        [rows, frozen, frozen_core],
        [shape((LIVE, KEY_WIDTH // 2), bf16)],
        order=[up_pair],
    )
    right, cross = call(
        mate_kernel,
        "mate",
        [],
        [rows, frozen, frozen_core, downs, downs_core],
        [shape((LIVE, KEY_WIDTH // 2 + 256), bf16), shape((LIVE, QUARTER + 128), bf16)],
        order=[left],
    )
    left_in, right_in, cross_core = across(left), across(right), core(cross)
    (low,) = call(
        low_own_kernel,
        "low_own",
        [],
        [near, far, downs, downs_core],
        [shape((LIVE, PADDED_RANK), f32)],
        order=[right],
    )
    ups_core = core(ups)
    dlow, up_kept, up_core = call(
        keys_kernel,
        "keys",
        [ranks],
        [far, low, right_in, ups, ups_core, base, left_in, grads, key_norm_weight[None, :]],
        [
            shape((LIVE, PADDED_RANK), bf16),
            shape((2, 4, 32, KEY_WIDTH), f32),
            shape((2, 4, 32, KEY_WIDTH), f32),
        ],
        order=[cross_core],
        scratch=[pltpu.VMEM((512, KEY_WIDTH), bf16), pltpu.VMEM((512, KEY_WIDTH), f32)],
    )
    dlow_mate, dlow_core = across(dlow), core(dlow)
    dlow_cross = core(dlow_mate)
    up_core_in = core(up_core)

    up_total, up_sent = call(
        up_core_kernel,
        "up_core",
        [],
        [up_kept, up_core_in],
        [shape((4, 32, KEY_WIDTH), f32), shape((4, 32, KEY_WIDTH), bf16)],
    )
    own, one, two, three = call(
        down_kernel,
        "down",
        [],
        [dlow, dlow_mate, dlow_core, dlow_cross, rows],
        [shape((PADDED_RANK, QUARTER), t) for t in (f32, bf16, bf16, bf16)],
        [near, far, far_core, cross_core],
        order=[up_total],
        scratch=[
            pltpu.VMEM((4 * LIVE, QUARTER), bf16),
            pltpu.VMEM((4 * LIVE, HEAD), bf16),
            pltpu.SemaphoreType.DMA((7,)),
        ],
    )
    three_in, two_in, one_in = along(three, 3), along(two, 2), along(one, 1)

    up_parts = call(
        up_across_kernel,
        "up_across",
        [],
        [up_total, across(up_sent)],
        [shape((32, KEY_WIDTH), t) for t in (f32, bf16, bf16, bf16)],
        order=[one],
    )
    up_in = [up_parts[0]] + [along(up_parts[j], j) for j in (1, 2, 3)]

    new_down, down_first, down_second, new_up, up_first, up_second = call(
        update_kernel,
        "update",
        [],
        [own, one_in, two_in, three_in, adapter_down_factor[0], down_first_moment[0], down_second_moment[0]]
        + [*up_in, adapter_up_factor[0], up_first_moment[0], up_second_moment[0]],
        [shape(adapter_down_factor.shape[1:], f32)] * 3 + [shape(adapter_up_factor.shape[1:], f32)] * 3,
    )
    return tuple(o[None] for o in (new_down, new_up, down_first, up_first, down_second, up_second))


def solution(mesh):
    paired = mesh.shape["dp"] == 4 and mesh.shape["fsdp"] == 4
    return jax.shard_map(
        local if paired else local_general,
        mesh=mesh,
        in_specs=(
            P(("parts", "dp", "fsdp"), None),
            P(("parts", "dp", "fsdp"), None),
            P(("parts", "dp", "fsdp"), None),
            P(("parts", "dp", "fsdp"), None),
            P(),
            P("fsdp", None),
            P(),
            P(("parts", "dp"), "fsdp", None),
            P(("parts", "dp"), "fsdp", None),
            P(("parts", "dp"), "fsdp", None),
            P(("parts", "dp"), "fsdp", None),
            P(("parts", "dp"), "fsdp", None),
            P(("parts", "dp"), "fsdp", None),
        ),
        out_specs=(
            P(("parts", "dp"), "fsdp", None),
            P(("parts", "dp"), "fsdp", None),
            P(("parts", "dp"), "fsdp", None),
            P(("parts", "dp"), "fsdp", None),
            P(("parts", "dp"), "fsdp", None),
            P(("parts", "dp"), "fsdp", None),
        ),
        check_vma=False,
    )
```

```python
import jax
import jax.numpy as jnp
from jax import lax
from jax.experimental import pallas as pl
from jax.experimental.pallas import tpu as pltpu
from jax.sharding import PartitionSpec as P

MODEL_WIDTH = 5120
HEAD = 128
KEY_WIDTH = 1024
PADDED_RANK = 128
SEQ = 32
LIVE = 288
QUARTER = MODEL_WIDTH // 4


adapter_alpha_scale = 16.0
norm_epsilon = 1e-06
learn_rate = 0.001
weight_decay = 0.01
beta_one = 0.9
beta_two = 0.999
correct_one = 1.0 - 0.9**10
correct_two = 1.0 - 0.999**10
adam_epsilon = 1e-08

bf16 = jnp.bfloat16
f32 = jnp.float32
i32 = jnp.int32


def optimizer_update(weights, gradient, moment, variance):
    moment_new = beta_one * moment + (1.0 - beta_one) * gradient
    variance_new = beta_two * variance + (1.0 - beta_two) * gradient * gradient
    update = moment_new / correct_one / (jnp.sqrt(variance_new / correct_two) + adam_epsilon)
    return (weights - learn_rate * (update + weight_decay * weights), moment_new, variance_new)


def adapter_grads(
    row_tokens,
    row_base,
    row_grads,
    down_factor_weight,
    up_factor_weight,
    owned_adapter_rank,
    key_norm_weight,
):
    columns = jnp.arange(PADDED_RANK) < owned_adapter_rank
    masked_down = jnp.where(columns[None, :], down_factor_weight, jnp.zeros((), bf16))
    masked_up = jnp.where(columns[:, None], up_factor_weight, jnp.zeros((), bf16))
    adapter_scale_factor = adapter_alpha_scale / owned_adapter_rank.astype(f32)
    lowrank = jnp.dot(row_tokens, masked_down, preferred_element_type=f32).astype(bf16)
    key_rows = row_base.astype(f32) + adapter_scale_factor * jnp.dot(
        lowrank, masked_up, preferred_element_type=f32
    )
    per_head = key_rows.reshape(key_rows.shape[0], KEY_WIDTH // HEAD, HEAD)
    inverse = lax.rsqrt(jnp.mean(per_head * per_head, axis=-1, keepdims=True) + norm_epsilon)
    normed = per_head * inverse
    incoming = row_grads.astype(f32).reshape(per_head.shape) * key_norm_weight
    key_grads = inverse * (incoming - normed * jnp.mean(incoming * normed, axis=-1, keepdims=True))
    key_grads = key_grads.reshape(key_rows.shape).astype(bf16)
    up_factor_gradient = adapter_scale_factor * lax.dot_general(
        lowrank, key_grads, (((0,), (0,)), ((), ())), preferred_element_type=f32
    )
    up_factor_gradient = jnp.where(columns[:, None], up_factor_gradient, 0.0)
    low_grads = (
        adapter_scale_factor
        * lax.dot_general(key_grads, masked_up, (((1,), (1,)), ((), ())), preferred_element_type=f32)
    ).astype(bf16)
    down_factor_gradient = lax.dot_general(
        row_tokens, low_grads, (((0,), (0,)), ((), ())), preferred_element_type=f32
    )
    return (down_factor_gradient, up_factor_gradient)


def general_gradients(
    tokens,
    cotangent,
    lengths,
    slot_adapter_index,
    adapter_rank_sizes,
    frozen,
    key_norm_weight,
    adapter_down_factor,
    adapter_up_factor,
):
    data_ranks = lax.axis_size("dp")
    owning_replica = lax.axis_index("dp")
    seq_count = lengths.shape[1]
    per_pair = -(-seq_count // data_ranks)
    slot_total = data_ranks * per_pair
    token_seqs = tokens.reshape(seq_count, SEQ, MODEL_WIDTH)
    live_mask = jnp.arange(SEQ)[None, :] < lengths[0][:, None]
    upstream = jnp.where(
        live_mask[:, :, None],
        cotangent.reshape(seq_count, SEQ, KEY_WIDTH),
        jnp.zeros((), cotangent.dtype),
    )
    target = slot_adapter_index[0]
    seq_index = jnp.arange(seq_count)
    earlier = (target[None, :] == target[:, None]) & (seq_index[None, :] < seq_index[:, None])
    slot_order = jnp.sum(earlier.astype(i32), axis=1)
    slot_of = target * per_pair + slot_order
    matches = slot_of[None, :] == jnp.arange(slot_total)[:, None]
    source = jnp.sum(jnp.where(matches, seq_index[None, :], 0), axis=1)
    filled = jnp.any(matches, axis=1)

    def pack_slots(values):
        picked = jnp.take(values, source, axis=0)
        picked = jnp.where(filled[:, None, None], picked, jnp.zeros((), values.dtype))
        return picked.reshape(data_ranks, per_pair * SEQ, values.shape[-1])

    arrived_tokens, arrived_grads = (
        lax.all_to_all(pack_slots(token_seqs), "dp", split_axis=0, concat_axis=0, tiled=True),
        lax.all_to_all(pack_slots(upstream), "dp", split_axis=0, concat_axis=0, tiled=True),
    )
    row_tokens = arrived_tokens.reshape(-1, MODEL_WIDTH)
    row_base = jnp.dot(
        row_tokens,
        lax.all_gather(frozen, "fsdp", axis=0, tiled=True),
        preferred_element_type=f32,
    ).astype(bf16)
    row_grads = arrived_grads.reshape(-1, KEY_WIDTH)
    owned_adapter_rank = jnp.sum(
        jnp.where(jnp.arange(adapter_rank_sizes.shape[0]) == owning_replica, adapter_rank_sizes, 0)
    )
    full_down, full_up = (
        lax.all_gather(adapter_down_factor.astype(bf16), "fsdp", axis=1, tiled=True),
        lax.all_gather(adapter_up_factor.astype(bf16), "fsdp", axis=1, tiled=True),
    )
    down_factor_gradient, up_factor_gradient = adapter_grads(
        row_tokens,
        row_base,
        row_grads,
        full_down[0],
        full_up[0],
        owned_adapter_rank,
        key_norm_weight,
    )
    return (
        lax.psum_scatter(down_factor_gradient, "fsdp", scatter_dimension=0, tiled=True),
        lax.psum_scatter(up_factor_gradient, "fsdp", scatter_dimension=0, tiled=True),
    )


def local_general(
    tokens,
    cotangent,
    lengths,
    slot_adapter_index,
    adapter_rank_sizes,
    frozen,
    key_norm_weight,
    adapter_down_factor,
    adapter_up_factor,
    down_first_moment,
    up_first_moment,
    down_second_moment,
    up_second_moment,
):
    down_gradient, up_gradient = general_gradients(
        tokens,
        cotangent,
        lengths,
        slot_adapter_index,
        adapter_rank_sizes,
        frozen,
        key_norm_weight,
        adapter_down_factor,
        adapter_up_factor,
    )
    new_down, down_first, down_second = optimizer_update(
        adapter_down_factor[0], down_gradient, down_first_moment[0], down_second_moment[0]
    )
    new_up, up_first, up_second = optimizer_update(
        adapter_up_factor[0], up_gradient, up_first_moment[0], up_second_moment[0]
    )
    return (
        new_down[None],
        new_up[None],
        down_first[None],
        up_first[None],
        down_second[None],
        up_second[None],
    )


SMEM = pl.BlockSpec(memory_space=pltpu.SMEM)
VMEM = pl.BlockSpec(memory_space=pltpu.VMEM)
HBM = pl.BlockSpec(memory_space=pl.ANY)


class Late:
    def __init__(self, source, target, sem):
        self.copy, self.target, self.waited = pltpu.make_async_copy(source, target, sem), target, False
        self.copy.start()

    def get(self):
        if not self.waited:
            self.copy.wait()
            self.waited = True
        return self.target


def call(kernel, name, scalars, late, outs, plain=(), order=(), scratch=(), vmem=36, light=False):
    n, m, p, d, o = len(scalars), len(late), len(plain), len(order), len(outs)

    def body(*refs):
        ins, rest = refs[: n + m + p], refs[n + m + p + d :]
        outputs, held, sems, scratches = rest[:o], rest[o : o + m], rest[o + m], rest[o + m + 1 :]
        lates = [Late(ins[n + i], held[i], sems.at[i]) for i in range(m)]
        kernel(*ins[:n], *lates, *ins[n + m :], *outputs, *scratches)
        for one in lates:
            one.get()

    args = list(scalars) + list(late) + list(plain) + list(order)
    moved = sum(a.size * a.dtype.itemsize for a in list(scalars) + list(late) + list(plain) + list(outs))
    return pl.pallas_call(
        body,
        name=name,
        in_specs=[SMEM] * n + [HBM] * (m + p + d),
        out_specs=tuple(VMEM for _ in outs),
        out_shape=tuple(outs),
        scratch_shapes=[pltpu.VMEM(a.shape, a.dtype) for a in late]
        + [pltpu.SemaphoreType.DMA((max(m, 1),))]
        + list(scratch),
        compiler_params=pltpu.CompilerParams(vmem_limit_bytes=vmem * 2**20),
        cost_estimate=pl.CostEstimate(
            flops=1 if light else 3 * 10**10, bytes_accessed=1 if light else moved, transcendentals=0
        ),
    )(*args)


def shape(dims, dtype):
    return jax.ShapeDtypeStruct(dims, dtype)


def offsets(place, length, slots):
    found = []
    for s in range(slots):
        total = jnp.int32(0)
        for t in range(slots):
            if t != s:
                first = place[t] > place[s] if t > s else place[t] >= place[s]
                total = total + jnp.where(first, length[t], 0)
        found.append(total)
    return found


def slot_places(lengths, adapters, slots):
    dp = lax.axis_index("dp")
    place = [adapters[0, s] ^ dp for s in range(slots)]
    length = [lengths[0, s] for s in range(slots)]
    return place, length, offsets(place, length, slots)


def packing(place, length, start, slots):
    token = lax.broadcasted_iota(i32, (1, slots * SEQ), 1)
    row_of = jnp.full((1, slots * SEQ), -1, i32)
    for s in range(slots):
        position = token - s * SEQ
        inside = (position >= 0) & (position < length[s])
        row_of = jnp.where(inside, position + start[s], row_of)
    row = lax.broadcasted_iota(i32, (LIVE, slots * SEQ), 0)
    return jnp.where(row == row_of, 1.0, 0.0).astype(bf16)


def row_places(place, length, start, slots):
    row = lax.broadcasted_iota(i32, (LIVE, HEAD), 0)
    found = jnp.zeros((LIVE, HEAD), f32)
    for s in range(slots):
        inside = (row >= start[s]) & (row < start[s] + length[s])
        found = jnp.where(inside, place[s].astype(f32), found)
    return found.astype(bf16)


def mm(a, b):
    return jnp.dot(a, b, preferred_element_type=f32)


def mm_nt(a, b):
    return lax.dot_general(a, b, (((1,), (1,)), ((), ())), preferred_element_type=f32)


def quarter_copies(tokens, held, sems, others):
    f = lax.axis_index("fsdp")
    copies = []
    for n, other in enumerate(others):
        start = pl.multiple_of((f ^ other) * QUARTER, QUARTER)
        copies.append(pltpu.make_async_copy(tokens.at[:, pl.ds(start, QUARTER)], held.at[n], sems.at[n]))
        copies[-1].start()
    return copies


def pack_sent_kernel(slots, lengths, adapters, tokens, out, held, sems):
    copies = quarter_copies(tokens, held, sems, (2, 3))
    found = slot_places(lengths, adapters, slots)
    chosen = packing(*found, slots)
    ids = row_places(*found, slots)
    for q in range(2):
        for b in range(10):
            at = min(16 * (10 * q + b), LIVE - 16)
            out[q, LIVE:, 128 * b : 128 * b + 128] = ids[at : at + 16]
        copies[q].wait()
        out[q, :LIVE] = mm(chosen, held[q]).astype(bf16)


def pack_kept_kernel(slots, lengths, adapters, cotangent, tokens, near_out, far_out, grads_out, held, sems):
    copies = quarter_copies(tokens, held, sems, (0, 1))
    found = slot_places(lengths, adapters, slots)
    chosen = packing(*found, slots)
    far_out[:, QUARTER:] = row_places(*found, slots)
    copies[0].wait()
    near_out[...] = mm(chosen, held[0]).astype(bf16)
    copies[1].wait()
    far_out[:, :QUARTER] = mm(chosen, held[1]).astype(bf16)
    grads_out[...] = mm(chosen, cotangent.get()[...]).astype(bf16)


def weights_kernel(ranks, down, up_own, up_mate, out):
    rank = ranks[lax.axis_index("dp")]
    f = lax.axis_index("fsdp")
    column = lax.broadcasted_iota(i32, (QUARTER, PADDED_RANK), 1)
    out[:QUARTER] = jnp.where(column < rank, down.get()[...], 0.0).astype(bf16)
    row = lax.broadcasted_iota(i32, (32, KEY_WIDTH), 0)
    for part, held in enumerate((up_own, up_mate)):
        masked = jnp.where(row + 32 * (f ^ (2 * part)) < rank, held.get()[...], 0.0).astype(bf16)
        for k in range(8):
            at = QUARTER + 64 * k + 32 * part
            out[at : at + 32] = masked[:, 128 * k : 128 * k + 128]


def base_mate_kernel(rows, own, mate, out):
    total = mm(rows.get()[0, :LIVE], own.get()[...])
    out[...] = (total + mm(rows.get()[1, :LIVE], mate.get()[...])).astype(bf16)


def down_factors(own, others):
    parts = [own.get()[:QUARTER]] + [others.get()[j, :QUARTER] for j in range(3)]
    return jnp.concatenate(parts, axis=1)


def mate_places(rows):
    blocks = [rows[n // 10, LIVE:, 128 * (n % 10) : 128 * (n % 10) + 128] for n in range(LIVE // 16)]
    return jnp.concatenate(blocks, axis=0)


def own_adapter(every, places):
    adapter = places.astype(f32)
    total = jnp.zeros((LIVE, PADDED_RANK), f32)
    for j in range(4):
        total = jnp.where(adapter == j, every[:, 128 * j : 128 * j + 128], total)
    return total


def low_mate_kernel(rows, own, others, core_own, core_others, out, core_out):
    held = rows.get()
    places = mate_places(held)
    core_out[:, :QUARTER] = held[1, :LIVE]
    core_out[:, QUARTER:] = places
    every = mm(held[0, :LIVE], down_factors(own, others))
    every = every + mm(held[1, :LIVE], down_factors(core_own, core_others))
    out[...] = own_adapter(every, places)


def base_own_kernel(near, own, far, mate, out):
    total = mm(near.get()[...], own.get()[...])
    out[...] = total + mm(far.get()[:, :QUARTER], mate.get()[...])


def low_own_kernel(near, far, own, others, core_own, core_others, out, up):
    f = lax.axis_index("fsdp")
    c, x = f % 2, f // 2
    held = far.get()
    every = mm(near.get()[...], down_factors(own, others))
    every = every + mm(held[:, :QUARTER], down_factors(core_own, core_others))
    out[...] = own_adapter(every, held[:, QUARTER:])
    for j in range(4):
        for part in range(2):
            for first, rest, side in ((own, others, c), (core_own, core_others, 1 - c)):
                source = rest.get().at[j - 1] if j else first.get()
                target = pl.multiple_of(128 * j + 64 * (x ^ part) + 32 * side, 32)
                for k in range(8):
                    at = QUARTER + 64 * k + 32 * part
                    up[pl.ds(target, 32), 128 * k : 128 * k + 128] = source[at : at + 32, :]


def identity():
    row = lax.broadcasted_iota(i32, (HEAD, HEAD), 0)
    return jnp.where(row == lax.broadcasted_iota(i32, (HEAD, HEAD), 1), 1.0, 0.0).astype(bf16)


def spread(values, places, which):
    adapter, value = places.astype(f32), values.astype(f32)
    return jnp.concatenate([jnp.where(adapter == j, value, 0.0).astype(bf16) for j in which], axis=1)


def transposed(values):
    unit = identity()
    parts = [mm_nt(unit, values[:, n : n + 128]).astype(bf16) for n in range(0, values.shape[1], 128)]
    return jnp.concatenate(parts, axis=0)


def keys_kernel(ranks, far, low, low_mate, up_late, base, base_mate, grads, gain, *refs):
    dlow_out, kept_out, sent_out, total = refs
    up = up_late.get()
    dp = lax.axis_index("dp")
    f = lax.axis_index("fsdp")
    c, x = f % 2, f // 2
    ids = far.get()[:, QUARTER:]
    adapter = ids.astype(f32)
    scales = [adapter_alpha_scale / jnp.full((1, HEAD), ranks[dp ^ j], i32).astype(f32) for j in range(4)]
    scale = jnp.zeros((LIVE, HEAD), f32)
    for j in range(4):
        scale = jnp.where(adapter == j, scales[j], scale)
    lowrank = (low.get()[...] + low_mate.get()[...]).astype(bf16).astype(f32)
    wide = spread(lowrank, ids, range(4))
    added = mm(wide, up[...])
    parts = []
    for k in range(8):
        lanes = slice(128 * k, 128 * k + 128)
        held = (base.get()[:, lanes] + base_mate.get()[:, lanes].astype(f32)).astype(bf16).astype(f32)
        head = held + scale * added[:, lanes]
        inverse = lax.rsqrt(jnp.mean(head * head, axis=-1, keepdims=True) + norm_epsilon)
        normed = head * inverse
        incoming = grads.get()[:, lanes].astype(f32) * gain.get()[...]
        mean = jnp.mean(incoming * normed, axis=-1, keepdims=True)
        parts.append((inverse * (incoming - normed * mean)).astype(bf16))
    key_grads = jnp.concatenate(parts, axis=1)
    every = mm_nt(key_grads, up[...])
    picked = jnp.zeros((LIVE, PADDED_RANK), f32)
    for j in range(4):
        picked = jnp.where(adapter == j, every[:, 128 * j : 128 * j + 128], picked)
    dlow_out[...] = (scale * picked).astype(bf16)
    total[...] = mm(transposed(wide), key_grads)
    for j in range(4):
        scale_j = scales[j][0:1, 0:1]
        for part in range(2):
            kept = pl.multiple_of(128 * j + 64 * (x ^ part) + 32 * c, 32)
            sent = pl.multiple_of(128 * j + 64 * (x ^ part) + 32 * (1 - c), 32)
            kept_out[part, j] = total[pl.ds(kept, 32), :] * scale_j
            sent_out[part, j] = total[pl.ds(sent, 32), :] * scale_j


def up_core_kernel(kept, arrived, own_out, mate_out):
    own_out[...] = kept.get()[0] + arrived.get()[0]
    mate_out[...] = (kept.get()[1] + arrived.get()[1]).astype(bf16)


def up_across_kernel(own, arrived, own_out, one_out, two_out, three_out):
    for j, out in enumerate((own_out, one_out, two_out, three_out)):
        out[...] = (own.get()[j] + arrived.get()[j].astype(f32)).astype(out.dtype)


def down_kernel(dlow, dlow_mate, dlow_core, dlow_cross, rows, near, far, far_core, cross, *refs):
    outs, (held, ids, sems) = refs[:4], refs[4:]
    copies = [pltpu.make_async_copy(far.at[:, pl.ds(QUARTER, 128)], ids.at[pl.ds(0, LIVE), :], sems.at[0])]
    copies.append(
        pltpu.make_async_copy(far_core.at[:, pl.ds(QUARTER, 128)], ids.at[pl.ds(2 * LIVE, LIVE), :], sems.at[1])
    )
    copies.append(
        pltpu.make_async_copy(cross.at[:, pl.ds(QUARTER, 128)], ids.at[pl.ds(3 * LIVE, LIVE), :], sems.at[2])
    )
    sources = [near, None, far_core.at[:, pl.ds(0, QUARTER)], cross.at[:, pl.ds(0, QUARTER)]]
    for n, source in enumerate(sources):
        if source is not None:
            copies.append(pltpu.make_async_copy(source, held.at[pl.ds(n * LIVE, LIVE), :], sems.at[3 + n]))
    for copy in copies:
        copy.start()
    held[LIVE : 2 * LIVE, :] = rows.get()[0, :LIVE]
    ids[LIVE : 2 * LIVE, :] = mate_places(rows.get())
    for copy in copies[:3]:
        copy.wait()
    lows = jnp.concatenate([d.get()[...] for d in (dlow, dlow_mate, dlow_core, dlow_cross)], axis=0)
    wide = transposed(spread(lows, ids[...], range(4)))
    for copy in copies[3:]:
        copy.wait()
    for j, out in enumerate(outs):
        out[...] = mm(wide[128 * j : 128 * j + 128], held[...]).astype(out.dtype)


def update_kernel(*refs):
    own, one, two, three, down, moment, variance = refs[:7]
    outs = refs[14:]
    for start in range(0, QUARTER, 128):
        part = slice(start, start + 128)
        total = own.get()[:, part] + one.get()[:, part].astype(f32)
        total = total + (two.get()[:, part].astype(f32) + three.get()[:, part].astype(f32))
        outs[0][part], outs[1][part], outs[2][part] = optimizer_update(
            down.get()[part], total.T, moment.get()[part], variance.get()[part]
        )
    own, one, two, three, up, moment, variance = refs[7:14]
    total = own.get()[...] + one.get()[...].astype(f32)
    total = total + (two.get()[...].astype(f32) + three.get()[...].astype(f32))
    outs[3][...], outs[4][...], outs[5][...] = optimizer_update(
        up.get()[...], total, moment.get()[...], variance.get()[...]
    )


def after(value, *others):
    return lax.optimization_barrier((value, *others))[0]


def local(
    tokens,
    cotangent,
    lengths,
    slot_adapter_index,
    adapter_rank_sizes,
    frozen,
    key_norm_weight,
    adapter_down_factor,
    adapter_up_factor,
    down_first_moment,
    up_first_moment,
    down_second_moment,
    up_second_moment,
):
    dp = lax.axis_index("dp")
    slots = lengths.shape[1]
    ranks = adapter_rank_sizes

    def core(value):
        return lax.ppermute(value, "fsdp", [(i, i ^ 1) for i in range(4)])

    def across(value):
        return lax.ppermute(value, "fsdp", [(i, i ^ 2) for i in range(4)])

    def along(value, distance):
        return lax.ppermute(value, "dp", [(i, i ^ distance) for i in range(4)])

    frozen_core = core(frozen)
    up_mate = across(adapter_up_factor[0])
    (sent,) = call(
        lambda *refs: pack_sent_kernel(slots, *refs),
        "pack_sent",
        [lengths, slot_adapter_index],
        [],
        [shape((2, LIVE + 16, QUARTER), bf16)],
        [tokens],
        scratch=[pltpu.VMEM((2, tokens.shape[0], QUARTER), bf16), pltpu.SemaphoreType.DMA((2,))],
        vmem=60,
    )
    rows = across(sent)

    (message,) = call(
        weights_kernel,
        "weights",
        [ranks],
        [adapter_down_factor[0], adapter_up_factor[0], up_mate],
        [shape((QUARTER + 512, PADDED_RANK), bf16)],
        order=[sent],
    )
    arrived = [along(message, j) for j in (1, 2, 3)]
    message_core = core(message)

    near, far, grads = call(
        lambda *refs: pack_kept_kernel(slots, *refs),
        "pack_kept",
        [lengths, slot_adapter_index],
        [cotangent],
        [
            shape((LIVE, QUARTER), bf16),
            shape((LIVE, QUARTER + 128), bf16),
            shape((LIVE, KEY_WIDTH), bf16),
        ],
        [tokens],
        order=[message_core, frozen_core],
        scratch=[pltpu.VMEM((2, tokens.shape[0], QUARTER), bf16), pltpu.SemaphoreType.DMA((2,))],
    )
    far_core = core(far)

    (partial,) = call(
        base_mate_kernel,
        "base_mate",
        [],
        [rows, frozen, frozen_core],
        [shape((LIVE, KEY_WIDTH), bf16)],
        order=[near],
    )
    base_mate = across(partial)
    others = jnp.stack([after(w, partial) for w in arrived])
    others_core = core(others)
    (base,) = call(
        base_own_kernel,
        "base_own",
        [],
        [near, frozen, far, frozen_core],
        [shape((LIVE, KEY_WIDTH), f32)],
        order=[others],
    )
    weights = [message, others, message_core, others_core]
    low_sent, cross = call(
        low_mate_kernel,
        "low_mate",
        [],
        [rows, *weights],
        [shape((LIVE, PADDED_RANK), f32), shape((LIVE, QUARTER + 128), bf16)],
        order=[base],
        light=True,
    )
    low_mate, cross_core = across(low_sent), core(cross)
    low, up = call(
        low_own_kernel,
        "low_own",
        [],
        [near, far, *weights],
        [shape((LIVE, PADDED_RANK), f32), shape((512, KEY_WIDTH), bf16)],
        order=[low_sent],
        light=True,
    )
    dlow, up_kept, up_core = call(
        keys_kernel,
        "keys",
        [ranks],
        [far, low, low_mate, up, base, base_mate, grads, key_norm_weight[None, :]],
        [
            shape((LIVE, PADDED_RANK), bf16),
            shape((2, 4, 32, KEY_WIDTH), f32),
            shape((2, 4, 32, KEY_WIDTH), f32),
        ],
        order=[far_core],
        scratch=[pltpu.VMEM((512, KEY_WIDTH), f32)],
    )
    dlow_mate, dlow_core = across(dlow), core(dlow)
    dlow_cross = core(dlow_mate)
    up_core_in = core(up_core)

    up_total, up_sent = call(
        up_core_kernel,
        "up_core",
        [],
        [up_kept, up_core_in],
        [shape((4, 32, KEY_WIDTH), f32), shape((4, 32, KEY_WIDTH), bf16)],
    )
    own, one, two, three = call(
        down_kernel,
        "down",
        [],
        [dlow, dlow_mate, dlow_core, dlow_cross, rows],
        [shape((PADDED_RANK, QUARTER), t) for t in (f32, bf16, bf16, bf16)],
        [near, far, far_core, cross_core],
        order=[up_total],
        scratch=[
            pltpu.VMEM((4 * LIVE, QUARTER), bf16),
            pltpu.VMEM((4 * LIVE, HEAD), bf16),
            pltpu.SemaphoreType.DMA((7,)),
        ],
    )
    three_in, two_in, one_in = along(three, 3), along(two, 2), along(one, 1)

    up_parts = call(
        up_across_kernel,
        "up_across",
        [],
        [up_total, across(up_sent)],
        [shape((32, KEY_WIDTH), t) for t in (f32, bf16, bf16, bf16)],
        order=[one],
    )
    up_in = [up_parts[0]] + [along(up_parts[j], j) for j in (1, 2, 3)]

    new_down, down_first, down_second, new_up, up_first, up_second = call(
        update_kernel,
        "update",
        [],
        [own, one_in, two_in, three_in, adapter_down_factor[0], down_first_moment[0], down_second_moment[0]]
        + [*up_in, adapter_up_factor[0], up_first_moment[0], up_second_moment[0]],
        [shape(adapter_down_factor.shape[1:], f32)] * 3 + [shape(adapter_up_factor.shape[1:], f32)] * 3,
    )
    return tuple(o[None] for o in (new_down, new_up, down_first, up_first, down_second, up_second))


def solution(mesh):
    paired = mesh.shape["dp"] == 4 and mesh.shape["fsdp"] == 4
    return jax.shard_map(
        local if paired else local_general,
        mesh=mesh,
        in_specs=(
            P(("parts", "dp", "fsdp"), None),
            P(("parts", "dp", "fsdp"), None),
            P(("parts", "dp", "fsdp"), None),
            P(("parts", "dp", "fsdp"), None),
            P(),
            P("fsdp", None),
            P(),
            P(("parts", "dp"), "fsdp", None),
            P(("parts", "dp"), "fsdp", None),
            P(("parts", "dp"), "fsdp", None),
            P(("parts", "dp"), "fsdp", None),
            P(("parts", "dp"), "fsdp", None),
            P(("parts", "dp"), "fsdp", None),
        ),
        out_specs=(
            P(("parts", "dp"), "fsdp", None),
            P(("parts", "dp"), "fsdp", None),
            P(("parts", "dp"), "fsdp", None),
            P(("parts", "dp"), "fsdp", None),
            P(("parts", "dp"), "fsdp", None),
            P(("parts", "dp"), "fsdp", None),
        ),
        check_vma=False,
    )
```

```python
import jax
import jax.numpy as jnp
from jax import lax
from jax.experimental import pallas as pl
from jax.experimental.pallas import tpu as pltpu
from jax.sharding import PartitionSpec as P

MODEL_WIDTH = 5120
HEAD = 128
KEY_WIDTH = 1024
PADDED_RANK = 128
SEQ = 32
LIVE = 288
QUARTER = MODEL_WIDTH // 4


adapter_alpha_scale = 16.0
norm_epsilon = 1e-06
learn_rate = 0.001
weight_decay = 0.01
beta_one = 0.9
beta_two = 0.999
correct_one = 1.0 - 0.9**10
correct_two = 1.0 - 0.999**10
adam_epsilon = 1e-08

bf16 = jnp.bfloat16
f32 = jnp.float32
i32 = jnp.int32


def optimizer_update(weights, gradient, moment, variance):
    moment_new = beta_one * moment + (1.0 - beta_one) * gradient
    variance_new = beta_two * variance + (1.0 - beta_two) * gradient * gradient
    update = moment_new / correct_one / (jnp.sqrt(variance_new / correct_two) + adam_epsilon)
    return (weights - learn_rate * (update + weight_decay * weights), moment_new, variance_new)


def adapter_grads(
    row_tokens,
    row_base,
    row_grads,
    down_factor_weight,
    up_factor_weight,
    owned_adapter_rank,
    key_norm_weight,
):
    columns = jnp.arange(PADDED_RANK) < owned_adapter_rank
    masked_down = jnp.where(columns[None, :], down_factor_weight, jnp.zeros((), bf16))
    masked_up = jnp.where(columns[:, None], up_factor_weight, jnp.zeros((), bf16))
    adapter_scale_factor = adapter_alpha_scale / owned_adapter_rank.astype(f32)
    lowrank = jnp.dot(row_tokens, masked_down, preferred_element_type=f32).astype(bf16)
    key_rows = row_base.astype(f32) + adapter_scale_factor * jnp.dot(
        lowrank, masked_up, preferred_element_type=f32
    )
    per_head = key_rows.reshape(key_rows.shape[0], KEY_WIDTH // HEAD, HEAD)
    inverse = lax.rsqrt(jnp.mean(per_head * per_head, axis=-1, keepdims=True) + norm_epsilon)
    normed = per_head * inverse
    incoming = row_grads.astype(f32).reshape(per_head.shape) * key_norm_weight
    key_grads = inverse * (incoming - normed * jnp.mean(incoming * normed, axis=-1, keepdims=True))
    key_grads = key_grads.reshape(key_rows.shape).astype(bf16)
    up_factor_gradient = adapter_scale_factor * lax.dot_general(
        lowrank, key_grads, (((0,), (0,)), ((), ())), preferred_element_type=f32
    )
    up_factor_gradient = jnp.where(columns[:, None], up_factor_gradient, 0.0)
    low_grads = (
        adapter_scale_factor
        * lax.dot_general(key_grads, masked_up, (((1,), (1,)), ((), ())), preferred_element_type=f32)
    ).astype(bf16)
    down_factor_gradient = lax.dot_general(
        row_tokens, low_grads, (((0,), (0,)), ((), ())), preferred_element_type=f32
    )
    return (down_factor_gradient, up_factor_gradient)


def general_gradients(
    tokens,
    cotangent,
    lengths,
    slot_adapter_index,
    adapter_rank_sizes,
    frozen,
    key_norm_weight,
    adapter_down_factor,
    adapter_up_factor,
):
    data_ranks = lax.axis_size("dp")
    owning_replica = lax.axis_index("dp")
    seq_count = lengths.shape[1]
    per_pair = -(-seq_count // data_ranks)
    slot_total = data_ranks * per_pair
    token_seqs = tokens.reshape(seq_count, SEQ, MODEL_WIDTH)
    live_mask = jnp.arange(SEQ)[None, :] < lengths[0][:, None]
    upstream = jnp.where(
        live_mask[:, :, None],
        cotangent.reshape(seq_count, SEQ, KEY_WIDTH),
        jnp.zeros((), cotangent.dtype),
    )
    target = slot_adapter_index[0]
    seq_index = jnp.arange(seq_count)
    earlier = (target[None, :] == target[:, None]) & (seq_index[None, :] < seq_index[:, None])
    slot_order = jnp.sum(earlier.astype(i32), axis=1)
    slot_of = target * per_pair + slot_order
    matches = slot_of[None, :] == jnp.arange(slot_total)[:, None]
    source = jnp.sum(jnp.where(matches, seq_index[None, :], 0), axis=1)
    filled = jnp.any(matches, axis=1)

    def pack_slots(values):
        picked = jnp.take(values, source, axis=0)
        picked = jnp.where(filled[:, None, None], picked, jnp.zeros((), values.dtype))
        return picked.reshape(data_ranks, per_pair * SEQ, values.shape[-1])

    arrived_tokens, arrived_grads = (
        lax.all_to_all(pack_slots(token_seqs), "dp", split_axis=0, concat_axis=0, tiled=True),
        lax.all_to_all(pack_slots(upstream), "dp", split_axis=0, concat_axis=0, tiled=True),
    )
    row_tokens = arrived_tokens.reshape(-1, MODEL_WIDTH)
    row_base = jnp.dot(
        row_tokens,
        lax.all_gather(frozen, "fsdp", axis=0, tiled=True),
        preferred_element_type=f32,
    ).astype(bf16)
    row_grads = arrived_grads.reshape(-1, KEY_WIDTH)
    owned_adapter_rank = jnp.sum(
        jnp.where(jnp.arange(adapter_rank_sizes.shape[0]) == owning_replica, adapter_rank_sizes, 0)
    )
    full_down, full_up = (
        lax.all_gather(adapter_down_factor.astype(bf16), "fsdp", axis=1, tiled=True),
        lax.all_gather(adapter_up_factor.astype(bf16), "fsdp", axis=1, tiled=True),
    )
    down_factor_gradient, up_factor_gradient = adapter_grads(
        row_tokens,
        row_base,
        row_grads,
        full_down[0],
        full_up[0],
        owned_adapter_rank,
        key_norm_weight,
    )
    return (
        lax.psum_scatter(down_factor_gradient, "fsdp", scatter_dimension=0, tiled=True),
        lax.psum_scatter(up_factor_gradient, "fsdp", scatter_dimension=0, tiled=True),
    )


def local_general(
    tokens,
    cotangent,
    lengths,
    slot_adapter_index,
    adapter_rank_sizes,
    frozen,
    key_norm_weight,
    adapter_down_factor,
    adapter_up_factor,
    down_first_moment,
    up_first_moment,
    down_second_moment,
    up_second_moment,
):
    down_gradient, up_gradient = general_gradients(
        tokens,
        cotangent,
        lengths,
        slot_adapter_index,
        adapter_rank_sizes,
        frozen,
        key_norm_weight,
        adapter_down_factor,
        adapter_up_factor,
    )
    new_down, down_first, down_second = optimizer_update(
        adapter_down_factor[0], down_gradient, down_first_moment[0], down_second_moment[0]
    )
    new_up, up_first, up_second = optimizer_update(
        adapter_up_factor[0], up_gradient, up_first_moment[0], up_second_moment[0]
    )
    return (
        new_down[None],
        new_up[None],
        down_first[None],
        up_first[None],
        down_second[None],
        up_second[None],
    )


SMEM = pl.BlockSpec(memory_space=pltpu.SMEM)
VMEM = pl.BlockSpec(memory_space=pltpu.VMEM)
HBM = pl.BlockSpec(memory_space=pl.ANY)


class Late:
    def __init__(self, source, target, sem):
        self.copy, self.target, self.waited = pltpu.make_async_copy(source, target, sem), target, False
        self.copy.start()

    def get(self):
        if not self.waited:
            self.copy.wait()
            self.waited = True
        return self.target


def call(kernel, name, scalars, late, outs, plain=(), order=(), scratch=(), vmem=36, light=False, out_spec=VMEM):
    n, m, p, d, o = len(scalars), len(late), len(plain), len(order), len(outs)

    def body(*refs):
        ins, rest = refs[: n + m + p], refs[n + m + p + d :]
        outputs, held, sems, scratches = rest[:o], rest[o : o + m], rest[o + m], rest[o + m + 1 :]
        lates = [Late(ins[n + i], held[i], sems.at[i]) for i in range(m)]
        kernel(*ins[:n], *lates, *ins[n + m :], *outputs, *scratches)
        for one in lates:
            one.get()

    args = list(scalars) + list(late) + list(plain) + list(order)
    moved = sum(a.size * a.dtype.itemsize for a in list(scalars) + list(late) + list(plain) + list(outs))
    return pl.pallas_call(
        body,
        name=name,
        in_specs=[SMEM] * n + [HBM] * (m + p + d),
        out_specs=tuple(out_spec for _ in outs),
        out_shape=tuple(outs),
        scratch_shapes=[pltpu.VMEM(a.shape, a.dtype) for a in late]
        + [pltpu.SemaphoreType.DMA((max(m, 1),))]
        + list(scratch),
        compiler_params=pltpu.CompilerParams(vmem_limit_bytes=vmem * 2**20),
        cost_estimate=pl.CostEstimate(
            flops=1 if light else 3 * 10**10, bytes_accessed=1 if light else moved, transcendentals=0
        ),
    )(*args)


def shape(dims, dtype):
    return jax.ShapeDtypeStruct(dims, dtype)


def offsets(place, length, slots):
    found = []
    for s in range(slots):
        total = jnp.int32(0)
        for t in range(slots):
            if t != s:
                first = place[t] > place[s] if t > s else place[t] >= place[s]
                total = total + jnp.where(first, length[t], 0)
        found.append(total)
    return found


def slot_places(lengths, adapters, slots):
    dp = lax.axis_index("dp")
    place = [adapters[0, s] ^ dp for s in range(slots)]
    length = [lengths[0, s] for s in range(slots)]
    return place, length, offsets(place, length, slots)


def packing(place, length, start, slots):
    token = lax.broadcasted_iota(i32, (1, slots * SEQ), 1)
    row_of = jnp.full((1, slots * SEQ), -1, i32)
    for s in range(slots):
        position = token - s * SEQ
        inside = (position >= 0) & (position < length[s])
        row_of = jnp.where(inside, position + start[s], row_of)
    row = lax.broadcasted_iota(i32, (LIVE, slots * SEQ), 0)
    return jnp.where(row == row_of, 1.0, 0.0).astype(bf16)


def row_places(place, length, start, slots):
    row = lax.broadcasted_iota(i32, (LIVE, HEAD), 0)
    found = jnp.zeros((LIVE, HEAD), f32)
    for s in range(slots):
        inside = (row >= start[s]) & (row < start[s] + length[s])
        found = jnp.where(inside, place[s].astype(f32), found)
    return found.astype(bf16)


def mm(a, b):
    return jnp.dot(a, b, preferred_element_type=f32)


def mm_nt(a, b):
    return lax.dot_general(a, b, (((1,), (1,)), ((), ())), preferred_element_type=f32)


def quarter_copies(tokens, held, sems, others):
    f = lax.axis_index("fsdp")
    copies = []
    for n, other in enumerate(others):
        start = pl.multiple_of((f ^ other) * QUARTER, QUARTER)
        copies.append(pltpu.make_async_copy(tokens.at[:, pl.ds(start, QUARTER)], held.at[n], sems.at[n]))
        copies[-1].start()
    return copies


def pack_sent_kernel(slots, lengths, adapters, tokens, out, held, sems):
    copies = quarter_copies(tokens, held, sems, (2, 3))
    found = slot_places(lengths, adapters, slots)
    chosen = packing(*found, slots)
    ids = row_places(*found, slots)
    for q in range(2):
        for b in range(10):
            at = min(16 * (10 * q + b), LIVE - 16)
            out[q, LIVE:, 128 * b : 128 * b + 128] = ids[at : at + 16]
        copies[q].wait()
        out[q, :LIVE] = mm(chosen, held[q]).astype(bf16)


def pack_kept_kernel(slots, lengths, adapters, cotangent, tokens, near_out, far_out, grads_out, held, sems):
    copies = quarter_copies(tokens, held, sems, (0, 1))
    found = slot_places(lengths, adapters, slots)
    chosen = packing(*found, slots)
    far_out[:, QUARTER:] = row_places(*found, slots)
    copies[0].wait()
    near_out[...] = mm(chosen, held[0]).astype(bf16)
    copies[1].wait()
    far_out[:, :QUARTER] = mm(chosen, held[1]).astype(bf16)
    grads_out[...] = mm(chosen, cotangent.get()[...]).astype(bf16)


def weights_kernel(ranks, down, up_own, up_mate, out):
    rank = ranks[lax.axis_index("dp")]
    f = lax.axis_index("fsdp")
    column = lax.broadcasted_iota(i32, (QUARTER, PADDED_RANK), 1)
    out[:QUARTER] = jnp.where(column < rank, down.get()[...], 0.0).astype(bf16)
    row = lax.broadcasted_iota(i32, (32, KEY_WIDTH), 0)
    for part, held in enumerate((up_own, up_mate)):
        masked = jnp.where(row + 32 * (f ^ (2 * part)) < rank, held.get()[...], 0.0).astype(bf16)
        for k in range(8):
            at = QUARTER + 64 * k + 32 * part
            out[at : at + 32] = masked[:, 128 * k : 128 * k + 128]


def base_mate_kernel(rows, own, mate, out):
    total = mm(rows.get()[0, :LIVE], own.get()[...])
    out[...] = (total + mm(rows.get()[1, :LIVE], mate.get()[...])).astype(bf16)


def down_factors(weights):
    return jnp.concatenate([weights.get()[j, :QUARTER] for j in range(4)], axis=1)


def mate_places(rows):
    blocks = [rows[n // 10, LIVE:, 128 * (n % 10) : 128 * (n % 10) + 128] for n in range(LIVE // 16)]
    return jnp.concatenate(blocks, axis=0)


def own_adapter(every, places):
    adapter = places.astype(f32)
    total = jnp.zeros((LIVE, PADDED_RANK), f32)
    for j in range(4):
        total = jnp.where(adapter == j, every[:, 128 * j : 128 * j + 128], total)
    return total


def low_mate_kernel(rows, weights, weights_core, out, core_out):
    held = rows.get()
    places = mate_places(held)
    core_out[:, :QUARTER] = held[1, :LIVE]
    core_out[:, QUARTER:] = places
    every = mm(held[0, :LIVE], down_factors(weights))
    every = every + mm(held[1, :LIVE], down_factors(weights_core))
    out[...] = own_adapter(every, places).astype(bf16)


def base_own_kernel(near, own, far, mate, out):
    total = mm(near.get()[...], own.get()[...])
    out[...] = total + mm(far.get()[:, :QUARTER], mate.get()[...])


def low_own_kernel(near, far, weights, weights_core, out, up):
    f = lax.axis_index("fsdp")
    c, x = f % 2, f // 2
    held = far.get()
    every = mm(near.get()[...], down_factors(weights))
    every = every + mm(held[:, :QUARTER], down_factors(weights_core))
    out[...] = own_adapter(every, held[:, QUARTER:])
    for j in range(4):
        for part in range(2):
            for source, side in ((weights, c), (weights_core, 1 - c)):
                target = pl.multiple_of(128 * j + 64 * (x ^ part) + 32 * side, 32)
                for k in range(8):
                    at = QUARTER + 64 * k + 32 * part
                    up[pl.ds(target, 32), 128 * k : 128 * k + 128] = source.get()[j, at : at + 32]


def identity():
    row = lax.broadcasted_iota(i32, (HEAD, HEAD), 0)
    return jnp.where(row == lax.broadcasted_iota(i32, (HEAD, HEAD), 1), 1.0, 0.0).astype(bf16)


def spread(values, places, which):
    adapter, value = places.astype(f32), values.astype(f32)
    return jnp.concatenate([jnp.where(adapter == j, value, 0.0).astype(bf16) for j in which], axis=1)


def transposed(values):
    unit = identity()
    parts = [mm_nt(unit, values[:, n : n + 128]).astype(bf16) for n in range(0, values.shape[1], 128)]
    return jnp.concatenate(parts, axis=0)


def keys_kernel(ranks, far, low, low_mate, up_late, base, base_mate, grads, gain, *refs):
    dlow_out, kept_out, sent_out, total = refs
    up = up_late.get()
    dp = lax.axis_index("dp")
    f = lax.axis_index("fsdp")
    c, x = f % 2, f // 2
    ids = far.get()[:, QUARTER:]
    adapter = ids.astype(f32)
    scales = [adapter_alpha_scale / jnp.full((1, HEAD), ranks[dp ^ j], i32).astype(f32) for j in range(4)]
    scale = jnp.zeros((LIVE, HEAD), f32)
    for j in range(4):
        scale = jnp.where(adapter == j, scales[j], scale)
    lowrank = (low.get()[...] + low_mate.get()[...].astype(f32)).astype(bf16).astype(f32)
    wide = spread(lowrank, ids, range(4))
    added = mm(wide, up[...])
    parts = []
    for k in range(8):
        lanes = slice(128 * k, 128 * k + 128)
        held = (base.get()[:, lanes] + base_mate.get()[:, lanes].astype(f32)).astype(bf16).astype(f32)
        head = held + scale * added[:, lanes]
        inverse = lax.rsqrt(jnp.mean(head * head, axis=-1, keepdims=True) + norm_epsilon)
        normed = head * inverse
        incoming = grads.get()[:, lanes].astype(f32) * gain.get()[...]
        mean = jnp.mean(incoming * normed, axis=-1, keepdims=True)
        parts.append((inverse * (incoming - normed * mean)).astype(bf16))
    key_grads = jnp.concatenate(parts, axis=1)
    every = mm_nt(key_grads, up[...])
    picked = jnp.zeros((LIVE, PADDED_RANK), f32)
    for j in range(4):
        picked = jnp.where(adapter == j, every[:, 128 * j : 128 * j + 128], picked)
    dlow_out[...] = (scale * picked).astype(bf16)
    total[...] = mm(transposed(wide), key_grads)
    for j in range(4):
        scale_j = scales[j][0:1, 0:1]
        for part in range(2):
            kept = pl.multiple_of(128 * j + 64 * (x ^ part) + 32 * c, 32)
            sent = pl.multiple_of(128 * j + 64 * (x ^ part) + 32 * (1 - c), 32)
            kept_out[part, j] = total[pl.ds(kept, 32), :] * scale_j
            sent_out[part, j] = total[pl.ds(sent, 32), :] * scale_j


def up_core_kernel(kept, arrived, own_out, mate_out):
    own_out[...] = kept.get()[0] + arrived.get()[0]
    mate_out[...] = (kept.get()[1] + arrived.get()[1]).astype(bf16)


def up_across_kernel(own, arrived, own_out, one_out, two_out, three_out):
    for j, out in enumerate((own_out, one_out, two_out, three_out)):
        out[...] = (own.get()[j] + arrived.get()[j].astype(f32)).astype(out.dtype)


def down_kernel(dlow, dlow_mate, dlow_core, dlow_cross, rows, near, far, far_core, cross, *refs):
    outs, (held, ids, sems) = refs[:4], refs[4:]
    copies = [pltpu.make_async_copy(far.at[:, pl.ds(QUARTER, 128)], ids.at[pl.ds(0, LIVE), :], sems.at[0])]
    copies.append(
        pltpu.make_async_copy(far_core.at[:, pl.ds(QUARTER, 128)], ids.at[pl.ds(2 * LIVE, LIVE), :], sems.at[1])
    )
    copies.append(
        pltpu.make_async_copy(cross.at[:, pl.ds(QUARTER, 128)], ids.at[pl.ds(3 * LIVE, LIVE), :], sems.at[2])
    )
    sources = [near, None, far_core.at[:, pl.ds(0, QUARTER)], cross.at[:, pl.ds(0, QUARTER)]]
    for n, source in enumerate(sources):
        if source is not None:
            copies.append(pltpu.make_async_copy(source, held.at[pl.ds(n * LIVE, LIVE), :], sems.at[3 + n]))
    for copy in copies:
        copy.start()
    held[LIVE : 2 * LIVE, :] = rows.get()[0, :LIVE]
    ids[LIVE : 2 * LIVE, :] = mate_places(rows.get())
    for copy in copies[:3]:
        copy.wait()
    lows = jnp.concatenate([d.get()[...] for d in (dlow, dlow_mate, dlow_core, dlow_cross)], axis=0)
    wide = transposed(spread(lows, ids[...], range(4)))
    for copy in copies[3:]:
        copy.wait()
    for j, out in enumerate(outs):
        out[...] = mm(wide[128 * j : 128 * j + 128], held[...]).astype(out.dtype)


def update_kernel(*refs):
    own, one, two, three, down, moment, variance = refs[:7]
    outs, held, sems = refs[14:20], refs[20:26], refs[26]
    step = 256
    copies = []

    def leave(n, rows):
        copies.append(pltpu.make_async_copy(held[n].at[rows], outs[n].at[rows], sems.at[len(copies)]))
        copies[-1].start()

    for start in range(0, QUARTER, step):
        rows = pl.ds(start, step)
        part = slice(start, start + step)
        total = own.get()[:, part] + one.get()[:, part].astype(f32)
        total = total + (two.get()[:, part].astype(f32) + three.get()[:, part].astype(f32))
        held[0][part], held[1][part], held[2][part] = optimizer_update(
            down.get()[part], total.T, moment.get()[part], variance.get()[part]
        )
        for n in range(3):
            leave(n, rows)
    own, one, two, three, up, moment, variance = refs[7:14]
    total = own.get()[...] + one.get()[...].astype(f32)
    total = total + (two.get()[...].astype(f32) + three.get()[...].astype(f32))
    held[3][...], held[4][...], held[5][...] = optimizer_update(
        up.get()[...], total, moment.get()[...], variance.get()[...]
    )
    for n in range(3, 6):
        leave(n, pl.ds(0, 32))
    for copy in copies:
        copy.wait()


def after(value, *others):
    return lax.optimization_barrier((value, *others))[0]


def local(
    tokens,
    cotangent,
    lengths,
    slot_adapter_index,
    adapter_rank_sizes,
    frozen,
    key_norm_weight,
    adapter_down_factor,
    adapter_up_factor,
    down_first_moment,
    up_first_moment,
    down_second_moment,
    up_second_moment,
):
    dp = lax.axis_index("dp")
    slots = lengths.shape[1]
    ranks = adapter_rank_sizes

    def core(value):
        return lax.ppermute(value, "fsdp", [(i, i ^ 1) for i in range(4)])

    def across(value):
        return lax.ppermute(value, "fsdp", [(i, i ^ 2) for i in range(4)])

    def along(value, distance):
        return lax.ppermute(value, "dp", [(i, i ^ distance) for i in range(4)])

    frozen_core = core(frozen)
    up_mate = across(adapter_up_factor[0])
    (sent,) = call(
        lambda *refs: pack_sent_kernel(slots, *refs),
        "pack_sent",
        [lengths, slot_adapter_index],
        [],
        [shape((2, LIVE + 16, QUARTER), bf16)],
        [tokens],
        scratch=[pltpu.VMEM((2, tokens.shape[0], QUARTER), bf16), pltpu.SemaphoreType.DMA((2,))],
        vmem=60,
    )
    rows = across(sent)

    (message,) = call(
        weights_kernel,
        "weights",
        [ranks],
        [adapter_down_factor[0], adapter_up_factor[0], up_mate],
        [shape((QUARTER + 512, PADDED_RANK), bf16)],
        order=[sent, frozen_core],
    )
    arrived = [along(message, j) for j in (1, 2, 3)]

    near, far, grads = call(
        lambda *refs: pack_kept_kernel(slots, *refs),
        "pack_kept",
        [lengths, slot_adapter_index],
        [cotangent],
        [
            shape((LIVE, QUARTER), bf16),
            shape((LIVE, QUARTER + 128), bf16),
            shape((LIVE, KEY_WIDTH), bf16),
        ],
        [tokens],
        order=[message],
        scratch=[pltpu.VMEM((2, tokens.shape[0], QUARTER), bf16), pltpu.SemaphoreType.DMA((2,))],
    )
    far_core = core(far)

    (partial,) = call(
        base_mate_kernel,
        "base_mate",
        [],
        [rows, frozen, frozen_core],
        [shape((LIVE, KEY_WIDTH), bf16)],
        order=[near],
    )
    base_mate = across(partial)
    weights = jnp.stack([message] + [after(w, partial) for w in arrived])
    weights_core = core(weights)
    (base,) = call(
        base_own_kernel,
        "base_own",
        [],
        [near, frozen, far, frozen_core],
        [shape((LIVE, KEY_WIDTH), f32)],
        order=[weights],
    )
    low_sent, cross = call(
        low_mate_kernel,
        "low_mate",
        [],
        [rows, weights, weights_core],
        [shape((LIVE, PADDED_RANK), bf16), shape((LIVE, QUARTER + 128), bf16)],
        order=[base],
        light=True,
    )
    low_mate, cross_core = across(low_sent), core(cross)
    low, up = call(
        low_own_kernel,
        "low_own",
        [],
        [near, far, weights, weights_core],
        [shape((LIVE, PADDED_RANK), f32), shape((512, KEY_WIDTH), bf16)],
        order=[low_sent],
        light=True,
    )
    dlow, up_kept, up_core = call(
        keys_kernel,
        "keys",
        [ranks],
        [far, low, low_mate, up, base, base_mate, grads, key_norm_weight[None, :]],
        [
            shape((LIVE, PADDED_RANK), bf16),
            shape((2, 4, 32, KEY_WIDTH), f32),
            shape((2, 4, 32, KEY_WIDTH), f32),
        ],
        order=[far_core],
        scratch=[pltpu.VMEM((512, KEY_WIDTH), f32)],
    )
    dlow_mate, dlow_core = across(dlow), core(dlow)
    dlow_cross = core(dlow_mate)
    up_core_in = core(up_core)

    own, one, two, three = call(
        down_kernel,
        "down",
        [],
        [dlow, dlow_mate, dlow_core, dlow_cross, rows],
        [shape((PADDED_RANK, QUARTER), t) for t in (f32, bf16, bf16, bf16)],
        [near, far, far_core, cross_core],
        scratch=[
            pltpu.VMEM((4 * LIVE, QUARTER), bf16),
            pltpu.VMEM((4 * LIVE, HEAD), bf16),
            pltpu.SemaphoreType.DMA((7,)),
        ],
    )
    three_in, two_in, one_in = along(three, 3), along(two, 2), along(one, 1)

    up_total, up_sent = call(
        up_core_kernel,
        "up_core",
        [],
        [up_kept, up_core_in],
        [shape((4, 32, KEY_WIDTH), f32), shape((4, 32, KEY_WIDTH), bf16)],
        order=[three],
    )
    up_parts = call(
        up_across_kernel,
        "up_across",
        [],
        [up_total, across(up_sent)],
        [shape((32, KEY_WIDTH), t) for t in (f32, bf16, bf16, bf16)],
        order=[one],
    )
    up_in = [up_parts[0]] + [along(up_parts[j], j) for j in (3, 2, 1)]

    new_down, down_first, down_second, new_up, up_first, up_second = call(
        update_kernel,
        "update",
        [],
        [own, one_in, two_in, three_in, adapter_down_factor[0], down_first_moment[0], down_second_moment[0]]
        + [*up_in, adapter_up_factor[0], up_first_moment[0], up_second_moment[0]],
        [shape(adapter_down_factor.shape[1:], f32)] * 3 + [shape(adapter_up_factor.shape[1:], f32)] * 3,
        scratch=[pltpu.VMEM(adapter_down_factor.shape[1:], f32)] * 3
        + [pltpu.VMEM(adapter_up_factor.shape[1:], f32)] * 3
        + [pltpu.SemaphoreType.DMA((18,))],
        out_spec=HBM,
    )
    return tuple(o[None] for o in (new_down, new_up, down_first, up_first, down_second, up_second))


def solution(mesh):
    paired = mesh.shape["dp"] == 4 and mesh.shape["fsdp"] == 4
    return jax.shard_map(
        local if paired else local_general,
        mesh=mesh,
        in_specs=(
            P(("parts", "dp", "fsdp"), None),
            P(("parts", "dp", "fsdp"), None),
            P(("parts", "dp", "fsdp"), None),
            P(("parts", "dp", "fsdp"), None),
            P(),
            P("fsdp", None),
            P(),
            P(("parts", "dp"), "fsdp", None),
            P(("parts", "dp"), "fsdp", None),
            P(("parts", "dp"), "fsdp", None),
            P(("parts", "dp"), "fsdp", None),
            P(("parts", "dp"), "fsdp", None),
            P(("parts", "dp"), "fsdp", None),
        ),
        out_specs=(
            P(("parts", "dp"), "fsdp", None),
            P(("parts", "dp"), "fsdp", None),
            P(("parts", "dp"), "fsdp", None),
            P(("parts", "dp"), "fsdp", None),
            P(("parts", "dp"), "fsdp", None),
            P(("parts", "dp"), "fsdp", None),
        ),
        check_vma=False,
    )
```

```python
import jax
import jax.numpy as jnp
from jax import lax
from jax.experimental import pallas as pl
from jax.experimental.pallas import tpu as pltpu
from jax.sharding import PartitionSpec as P

MODEL_WIDTH = 5120
HEAD = 128
KEY_WIDTH = 1024
PADDED_RANK = 128
SEQ = 32
LIVE = 288
QUARTER = MODEL_WIDTH // 4


adapter_alpha_scale = 16.0
norm_epsilon = 1e-06
learn_rate = 0.001
weight_decay = 0.01
beta_one = 0.9
beta_two = 0.999
correct_one = 1.0 - 0.9**10
correct_two = 1.0 - 0.999**10
adam_epsilon = 1e-08

bf16 = jnp.bfloat16
f32 = jnp.float32
i32 = jnp.int32


def optimizer_update(weights, gradient, moment, variance):
    moment_new = beta_one * moment + (1.0 - beta_one) * gradient
    variance_new = beta_two * variance + (1.0 - beta_two) * gradient * gradient
    update = moment_new / correct_one / (jnp.sqrt(variance_new / correct_two) + adam_epsilon)
    return (weights - learn_rate * (update + weight_decay * weights), moment_new, variance_new)


def adapter_grads(
    row_tokens,
    row_base,
    row_grads,
    down_factor_weight,
    up_factor_weight,
    owned_adapter_rank,
    key_norm_weight,
):
    columns = jnp.arange(PADDED_RANK) < owned_adapter_rank
    masked_down = jnp.where(columns[None, :], down_factor_weight, jnp.zeros((), bf16))
    masked_up = jnp.where(columns[:, None], up_factor_weight, jnp.zeros((), bf16))
    adapter_scale_factor = adapter_alpha_scale / owned_adapter_rank.astype(f32)
    lowrank = jnp.dot(row_tokens, masked_down, preferred_element_type=f32).astype(bf16)
    key_rows = row_base.astype(f32) + adapter_scale_factor * jnp.dot(
        lowrank, masked_up, preferred_element_type=f32
    )
    per_head = key_rows.reshape(key_rows.shape[0], KEY_WIDTH // HEAD, HEAD)
    inverse = lax.rsqrt(jnp.mean(per_head * per_head, axis=-1, keepdims=True) + norm_epsilon)
    normed = per_head * inverse
    incoming = row_grads.astype(f32).reshape(per_head.shape) * key_norm_weight
    key_grads = inverse * (incoming - normed * jnp.mean(incoming * normed, axis=-1, keepdims=True))
    key_grads = key_grads.reshape(key_rows.shape).astype(bf16)
    up_factor_gradient = adapter_scale_factor * lax.dot_general(
        lowrank, key_grads, (((0,), (0,)), ((), ())), preferred_element_type=f32
    )
    up_factor_gradient = jnp.where(columns[:, None], up_factor_gradient, 0.0)
    low_grads = (
        adapter_scale_factor
        * lax.dot_general(key_grads, masked_up, (((1,), (1,)), ((), ())), preferred_element_type=f32)
    ).astype(bf16)
    down_factor_gradient = lax.dot_general(
        row_tokens, low_grads, (((0,), (0,)), ((), ())), preferred_element_type=f32
    )
    return (down_factor_gradient, up_factor_gradient)


def general_gradients(
    tokens,
    cotangent,
    lengths,
    slot_adapter_index,
    adapter_rank_sizes,
    frozen,
    key_norm_weight,
    adapter_down_factor,
    adapter_up_factor,
):
    data_ranks = lax.axis_size("dp")
    owning_replica = lax.axis_index("dp")
    seq_count = lengths.shape[1]
    per_pair = -(-seq_count // data_ranks)
    slot_total = data_ranks * per_pair
    token_seqs = tokens.reshape(seq_count, SEQ, MODEL_WIDTH)
    live_mask = jnp.arange(SEQ)[None, :] < lengths[0][:, None]
    upstream = jnp.where(
        live_mask[:, :, None],
        cotangent.reshape(seq_count, SEQ, KEY_WIDTH),
        jnp.zeros((), cotangent.dtype),
    )
    target = slot_adapter_index[0]
    seq_index = jnp.arange(seq_count)
    earlier = (target[None, :] == target[:, None]) & (seq_index[None, :] < seq_index[:, None])
    slot_order = jnp.sum(earlier.astype(i32), axis=1)
    slot_of = target * per_pair + slot_order
    matches = slot_of[None, :] == jnp.arange(slot_total)[:, None]
    source = jnp.sum(jnp.where(matches, seq_index[None, :], 0), axis=1)
    filled = jnp.any(matches, axis=1)

    def pack_slots(values):
        picked = jnp.take(values, source, axis=0)
        picked = jnp.where(filled[:, None, None], picked, jnp.zeros((), values.dtype))
        return picked.reshape(data_ranks, per_pair * SEQ, values.shape[-1])

    arrived_tokens, arrived_grads = (
        lax.all_to_all(pack_slots(token_seqs), "dp", split_axis=0, concat_axis=0, tiled=True),
        lax.all_to_all(pack_slots(upstream), "dp", split_axis=0, concat_axis=0, tiled=True),
    )
    row_tokens = arrived_tokens.reshape(-1, MODEL_WIDTH)
    row_base = jnp.dot(
        row_tokens,
        lax.all_gather(frozen, "fsdp", axis=0, tiled=True),
        preferred_element_type=f32,
    ).astype(bf16)
    row_grads = arrived_grads.reshape(-1, KEY_WIDTH)
    owned_adapter_rank = jnp.sum(
        jnp.where(jnp.arange(adapter_rank_sizes.shape[0]) == owning_replica, adapter_rank_sizes, 0)
    )
    full_down, full_up = (
        lax.all_gather(adapter_down_factor.astype(bf16), "fsdp", axis=1, tiled=True),
        lax.all_gather(adapter_up_factor.astype(bf16), "fsdp", axis=1, tiled=True),
    )
    down_factor_gradient, up_factor_gradient = adapter_grads(
        row_tokens,
        row_base,
        row_grads,
        full_down[0],
        full_up[0],
        owned_adapter_rank,
        key_norm_weight,
    )
    return (
        lax.psum_scatter(down_factor_gradient, "fsdp", scatter_dimension=0, tiled=True),
        lax.psum_scatter(up_factor_gradient, "fsdp", scatter_dimension=0, tiled=True),
    )


def local_general(
    tokens,
    cotangent,
    lengths,
    slot_adapter_index,
    adapter_rank_sizes,
    frozen,
    key_norm_weight,
    adapter_down_factor,
    adapter_up_factor,
    down_first_moment,
    up_first_moment,
    down_second_moment,
    up_second_moment,
):
    down_gradient, up_gradient = general_gradients(
        tokens,
        cotangent,
        lengths,
        slot_adapter_index,
        adapter_rank_sizes,
        frozen,
        key_norm_weight,
        adapter_down_factor,
        adapter_up_factor,
    )
    new_down, down_first, down_second = optimizer_update(
        adapter_down_factor[0], down_gradient, down_first_moment[0], down_second_moment[0]
    )
    new_up, up_first, up_second = optimizer_update(
        adapter_up_factor[0], up_gradient, up_first_moment[0], up_second_moment[0]
    )
    return (
        new_down[None],
        new_up[None],
        down_first[None],
        up_first[None],
        down_second[None],
        up_second[None],
    )


SMEM = pl.BlockSpec(memory_space=pltpu.SMEM)
VMEM = pl.BlockSpec(memory_space=pltpu.VMEM)
HBM = pl.BlockSpec(memory_space=pl.ANY)


class Late:
    def __init__(self, source, target, sem):
        self.copy, self.target, self.waited = pltpu.make_async_copy(source, target, sem), target, False
        self.copy.start()

    def get(self):
        if not self.waited:
            self.copy.wait()
            self.waited = True
        return self.target


def call(kernel, name, scalars, late, outs, plain=(), order=(), scratch=(), vmem=36, light=False, out_spec=VMEM):
    n, m, p, d, o = len(scalars), len(late), len(plain), len(order), len(outs)

    def body(*refs):
        ins, rest = refs[: n + m + p], refs[n + m + p + d :]
        outputs, held, sems, scratches = rest[:o], rest[o : o + m], rest[o + m], rest[o + m + 1 :]
        lates = [Late(ins[n + i], held[i], sems.at[i]) for i in range(m)]
        kernel(*ins[:n], *lates, *ins[n + m :], *outputs, *scratches)
        for one in lates:
            one.get()

    args = list(scalars) + list(late) + list(plain) + list(order)
    moved = sum(a.size * a.dtype.itemsize for a in list(scalars) + list(late) + list(plain) + list(outs))
    return pl.pallas_call(
        body,
        name=name,
        in_specs=[SMEM] * n + [HBM] * (m + p + d),
        out_specs=tuple(out_spec for _ in outs),
        out_shape=tuple(outs),
        scratch_shapes=[pltpu.VMEM(a.shape, a.dtype) for a in late]
        + [pltpu.SemaphoreType.DMA((max(m, 1),))]
        + list(scratch),
        compiler_params=pltpu.CompilerParams(vmem_limit_bytes=vmem * 2**20),
        cost_estimate=pl.CostEstimate(
            flops=1 if light else 3 * 10**10, bytes_accessed=1 if light else moved, transcendentals=0
        ),
    )(*args)


def shape(dims, dtype):
    return jax.ShapeDtypeStruct(dims, dtype)


def offsets(place, length, slots):
    found = []
    for s in range(slots):
        total = jnp.int32(0)
        for t in range(slots):
            if t != s:
                first = place[t] > place[s] if t > s else place[t] >= place[s]
                total = total + jnp.where(first, length[t], 0)
        found.append(total)
    return found


def slot_places(lengths, adapters, slots):
    dp = lax.axis_index("dp")
    place = [adapters[0, s] ^ dp for s in range(slots)]
    length = [lengths[0, s] for s in range(slots)]
    return place, length, offsets(place, length, slots)


def packing(place, length, start, slots):
    token = lax.broadcasted_iota(i32, (1, slots * SEQ), 1)
    row_of = jnp.full((1, slots * SEQ), -1, i32)
    for s in range(slots):
        position = token - s * SEQ
        inside = (position >= 0) & (position < length[s])
        row_of = jnp.where(inside, position + start[s], row_of)
    row = lax.broadcasted_iota(i32, (LIVE, slots * SEQ), 0)
    return jnp.where(row == row_of, 1.0, 0.0).astype(bf16)


def row_places(place, length, start, slots):
    row = lax.broadcasted_iota(i32, (LIVE, HEAD), 0)
    found = jnp.zeros((LIVE, HEAD), f32)
    for s in range(slots):
        inside = (row >= start[s]) & (row < start[s] + length[s])
        found = jnp.where(inside, place[s].astype(f32), found)
    return found.astype(bf16)


def mm(a, b):
    return jnp.dot(a, b, preferred_element_type=f32)


def mm_nt(a, b):
    return lax.dot_general(a, b, (((1,), (1,)), ((), ())), preferred_element_type=f32)


def quarter_copies(tokens, held, sems, others):
    f = lax.axis_index("fsdp")
    copies = []
    for n, other in enumerate(others):
        start = pl.multiple_of((f ^ other) * QUARTER, QUARTER)
        copies.append(pltpu.make_async_copy(tokens.at[:, pl.ds(start, QUARTER)], held.at[n], sems.at[n]))
        copies[-1].start()
    return copies


def pack_sent_kernel(slots, lengths, adapters, tokens, out, held, packed, sems):
    copies = quarter_copies(tokens, held, sems, (2, 3))
    found = slot_places(lengths, adapters, slots)
    chosen = packing(*found, slots)
    ids = row_places(*found, slots)
    for q in range(2):
        for b in range(10):
            at = min(16 * (10 * q + b), LIVE - 16)
            packed[q, LIVE:, 128 * b : 128 * b + 128] = ids[at : at + 16]
        copies[q].wait()
        packed[q, :LIVE] = mm(chosen, held[q]).astype(bf16)
        copies.append(pltpu.make_async_copy(packed.at[q], out.at[q], sems.at[2 + q]))
        copies[-1].start()
    for copy in copies[2:]:
        copy.wait()


def pack_kept_kernel(slots, lengths, adapters, cotangent, tokens, near_out, far_out, grads_out, held, sems):
    copies = quarter_copies(tokens, held, sems, (0, 1))
    found = slot_places(lengths, adapters, slots)
    chosen = packing(*found, slots)
    far_out[:, QUARTER:] = row_places(*found, slots)
    copies[0].wait()
    near_out[...] = mm(chosen, held[0]).astype(bf16)
    copies[1].wait()
    far_out[:, :QUARTER] = mm(chosen, held[1]).astype(bf16)
    grads_out[...] = mm(chosen, cotangent.get()[...]).astype(bf16)


def weights_kernel(ranks, down, up_own, up_mate, out):
    rank = ranks[lax.axis_index("dp")]
    f = lax.axis_index("fsdp")
    column = lax.broadcasted_iota(i32, (QUARTER, PADDED_RANK), 1)
    out[:QUARTER] = jnp.where(column < rank, down.get()[...], 0.0).astype(bf16)
    row = lax.broadcasted_iota(i32, (32, KEY_WIDTH), 0)
    for part, held in enumerate((up_own, up_mate)):
        masked = jnp.where(row + 32 * (f ^ (2 * part)) < rank, held.get()[...], 0.0).astype(bf16)
        for k in range(8):
            at = QUARTER + 64 * k + 32 * part
            out[at : at + 32] = masked[:, 128 * k : 128 * k + 128]


def base_mate_kernel(rows, own, mate, out):
    total = mm(rows.get()[0, :LIVE], own.get()[...])
    out[...] = (total + mm(rows.get()[1, :LIVE], mate.get()[...])).astype(bf16)


def down_factors(weights):
    return jnp.concatenate([weights.get()[j, :QUARTER] for j in range(4)], axis=1)


def mate_places(rows):
    blocks = [rows[n // 10, LIVE:, 128 * (n % 10) : 128 * (n % 10) + 128] for n in range(LIVE // 16)]
    return jnp.concatenate(blocks, axis=0)


def own_adapter(every, places):
    adapter = places.astype(f32)
    total = jnp.zeros((LIVE, PADDED_RANK), f32)
    for j in range(4):
        total = jnp.where(adapter == j, every[:, 128 * j : 128 * j + 128], total)
    return total


def low_mate_kernel(rows, weights, weights_core, out, core_out):
    held = rows.get()
    places = mate_places(held)
    core_out[:, :QUARTER] = held[1, :LIVE]
    core_out[:, QUARTER:] = places
    every = mm(held[0, :LIVE], down_factors(weights))
    every = every + mm(held[1, :LIVE], down_factors(weights_core))
    out[...] = own_adapter(every, places).astype(bf16)


def base_own_kernel(near, own, far, mate, out):
    total = mm(near.get()[...], own.get()[...])
    out[...] = total + mm(far.get()[:, :QUARTER], mate.get()[...])


def low_own_kernel(near, far, weights, weights_core, out, up):
    f = lax.axis_index("fsdp")
    c, x = f % 2, f // 2
    held = far.get()
    every = mm(near.get()[...], down_factors(weights))
    every = every + mm(held[:, :QUARTER], down_factors(weights_core))
    out[...] = own_adapter(every, held[:, QUARTER:])
    for j in range(4):
        for part in range(2):
            for source, side in ((weights, c), (weights_core, 1 - c)):
                target = pl.multiple_of(128 * j + 64 * (x ^ part) + 32 * side, 32)
                for k in range(8):
                    at = QUARTER + 64 * k + 32 * part
                    up[pl.ds(target, 32), 128 * k : 128 * k + 128] = source.get()[j, at : at + 32]


def identity():
    row = lax.broadcasted_iota(i32, (HEAD, HEAD), 0)
    return jnp.where(row == lax.broadcasted_iota(i32, (HEAD, HEAD), 1), 1.0, 0.0).astype(bf16)


def spread(values, places, which):
    adapter, value = places.astype(f32), values.astype(f32)
    return jnp.concatenate([jnp.where(adapter == j, value, 0.0).astype(bf16) for j in which], axis=1)


def transposed(values):
    unit = identity()
    parts = [mm_nt(unit, values[:, n : n + 128]).astype(bf16) for n in range(0, values.shape[1], 128)]
    return jnp.concatenate(parts, axis=0)


def keys_kernel(ranks, far, low, low_mate, up_late, base, base_mate, grads, gain, *refs):
    dlow_out, key_grads_out, wide_out = refs
    up = up_late.get()
    dp = lax.axis_index("dp")
    f = lax.axis_index("fsdp")
    c, x = f % 2, f // 2
    ids = far.get()[:, QUARTER:]
    adapter = ids.astype(f32)
    scales = [adapter_alpha_scale / jnp.full((1, HEAD), ranks[dp ^ j], i32).astype(f32) for j in range(4)]
    scale = jnp.zeros((LIVE, HEAD), f32)
    for j in range(4):
        scale = jnp.where(adapter == j, scales[j], scale)
    lowrank = (low.get()[...] + low_mate.get()[...].astype(f32)).astype(bf16).astype(f32)
    wide = spread(lowrank, ids, range(4))
    added = mm(wide, up[...])
    parts = []
    for k in range(8):
        lanes = slice(128 * k, 128 * k + 128)
        held = (base.get()[:, lanes] + base_mate.get()[:, lanes].astype(f32)).astype(bf16).astype(f32)
        head = held + scale * added[:, lanes]
        inverse = lax.rsqrt(jnp.mean(head * head, axis=-1, keepdims=True) + norm_epsilon)
        normed = head * inverse
        incoming = grads.get()[:, lanes].astype(f32) * gain.get()[...]
        mean = jnp.mean(incoming * normed, axis=-1, keepdims=True)
        parts.append((inverse * (incoming - normed * mean)).astype(bf16))
    key_grads = jnp.concatenate(parts, axis=1)
    every = mm_nt(key_grads, up[...])
    picked = jnp.zeros((LIVE, PADDED_RANK), f32)
    for j in range(4):
        picked = jnp.where(adapter == j, every[:, 128 * j : 128 * j + 128], picked)
    dlow_out[...] = (scale * picked).astype(bf16)
    key_grads_out[...] = key_grads
    wide_out[...] = wide


def up_sums_kernel(ranks, wide, key_grads, kept_out, sent_out, total):
    dp = lax.axis_index("dp")
    f = lax.axis_index("fsdp")
    c, x = f % 2, f // 2
    scales = [adapter_alpha_scale / jnp.full((1, HEAD), ranks[dp ^ j], i32).astype(f32) for j in range(4)]
    total[...] = mm(transposed(wide.get()[...]), key_grads.get()[...])
    for j in range(4):
        scale_j = scales[j][0:1, 0:1]
        for part in range(2):
            kept = pl.multiple_of(128 * j + 64 * (x ^ part) + 32 * c, 32)
            sent = pl.multiple_of(128 * j + 64 * (x ^ part) + 32 * (1 - c), 32)
            kept_out[part, j] = total[pl.ds(kept, 32), :] * scale_j
            sent_out[part, j] = total[pl.ds(sent, 32), :] * scale_j


def up_core_kernel(kept, arrived, own_out, mate_out):
    own_out[...] = kept.get()[0] + arrived.get()[0]
    mate_out[...] = (kept.get()[1] + arrived.get()[1]).astype(bf16)


def up_across_kernel(own, arrived, own_out, one_out, two_out, three_out):
    for j, out in enumerate((own_out, one_out, two_out, three_out)):
        out[...] = (own.get()[j] + arrived.get()[j].astype(f32)).astype(out.dtype)


def down_kernel(places, dlow, dlow_mate, dlow_core, dlow_cross, rows, near, far, far_core, cross, *refs):
    outs, (held, ids, sems) = refs[:2], refs[2:]
    copies = [pltpu.make_async_copy(far.at[:, pl.ds(QUARTER, 128)], ids.at[pl.ds(0, LIVE), :], sems.at[0])]
    copies.append(
        pltpu.make_async_copy(far_core.at[:, pl.ds(QUARTER, 128)], ids.at[pl.ds(2 * LIVE, LIVE), :], sems.at[1])
    )
    copies.append(
        pltpu.make_async_copy(cross.at[:, pl.ds(QUARTER, 128)], ids.at[pl.ds(3 * LIVE, LIVE), :], sems.at[2])
    )
    sources = [near, None, far_core.at[:, pl.ds(0, QUARTER)], cross.at[:, pl.ds(0, QUARTER)]]
    for n, source in enumerate(sources):
        if source is not None:
            copies.append(pltpu.make_async_copy(source, held.at[pl.ds(n * LIVE, LIVE), :], sems.at[3 + n]))
    for copy in copies:
        copy.start()
    held[LIVE : 2 * LIVE, :] = rows.get()[0, :LIVE]
    ids[LIVE : 2 * LIVE, :] = mate_places(rows.get())
    for copy in copies[:3]:
        copy.wait()
    lows = jnp.concatenate([d.get()[...] for d in (dlow, dlow_mate, dlow_core, dlow_cross)], axis=0)
    wide = transposed(spread(lows, ids[...], places))
    for copy in copies[3:]:
        copy.wait()
    total = mm(wide, held[...])
    for n, out in enumerate(outs):
        out[...] = total[128 * n : 128 * n + 128].astype(out.dtype)


def update_kernel(*refs):
    own, one, two, three, down, moment, variance = refs[:7]
    outs, held, sems = refs[14:20], refs[20:26], refs[26]
    step = 256
    copies = []

    def leave(n, rows):
        copies.append(pltpu.make_async_copy(held[n].at[rows], outs[n].at[rows], sems.at[len(copies)]))
        copies[-1].start()

    for start in range(0, QUARTER, step):
        rows = pl.ds(start, step)
        part = slice(start, start + step)
        total = own.get()[:, part] + one.get()[:, part].astype(f32)
        total = total + (two.get()[:, part].astype(f32) + three.get()[:, part].astype(f32))
        held[0][part], held[1][part], held[2][part] = optimizer_update(
            down.get()[part], total.T, moment.get()[part], variance.get()[part]
        )
        for n in range(3):
            leave(n, rows)
    own, one, two, three, up, moment, variance = refs[7:14]
    total = own.get()[...] + one.get()[...].astype(f32)
    total = total + (two.get()[...].astype(f32) + three.get()[...].astype(f32))
    held[3][...], held[4][...], held[5][...] = optimizer_update(
        up.get()[...], total, moment.get()[...], variance.get()[...]
    )
    for n in range(3, 6):
        leave(n, pl.ds(0, 32))
    for copy in copies:
        copy.wait()


def after(value, *others):
    return lax.optimization_barrier((value, *others))[0]


def local(
    tokens,
    cotangent,
    lengths,
    slot_adapter_index,
    adapter_rank_sizes,
    frozen,
    key_norm_weight,
    adapter_down_factor,
    adapter_up_factor,
    down_first_moment,
    up_first_moment,
    down_second_moment,
    up_second_moment,
):
    dp = lax.axis_index("dp")
    slots = lengths.shape[1]
    ranks = adapter_rank_sizes

    def core(value):
        return lax.ppermute(value, "fsdp", [(i, i ^ 1) for i in range(4)])

    def across(value):
        return lax.ppermute(value, "fsdp", [(i, i ^ 2) for i in range(4)])

    def along(value, distance):
        return lax.ppermute(value, "dp", [(i, i ^ distance) for i in range(4)])

    frozen_core = core(frozen)
    up_mate = across(adapter_up_factor[0])
    (sent,) = call(
        lambda *refs: pack_sent_kernel(slots, *refs),
        "pack_sent",
        [lengths, slot_adapter_index],
        [],
        [shape((2, LIVE + 16, QUARTER), bf16)],
        [tokens],
        scratch=[
            pltpu.VMEM((2, tokens.shape[0], QUARTER), bf16),
            pltpu.VMEM((2, LIVE + 16, QUARTER), bf16),
            pltpu.SemaphoreType.DMA((4,)),
        ],
        vmem=60,
        out_spec=HBM,
    )
    rows = across(sent)

    (message,) = call(
        weights_kernel,
        "weights",
        [ranks],
        [adapter_down_factor[0], adapter_up_factor[0], up_mate],
        [shape((QUARTER + 512, PADDED_RANK), bf16)],
        order=[sent, frozen_core],
    )
    arrived = [along(message, j) for j in (1, 2, 3)]

    near, far, grads = call(
        lambda *refs: pack_kept_kernel(slots, *refs),
        "pack_kept",
        [lengths, slot_adapter_index],
        [cotangent],
        [
            shape((LIVE, QUARTER), bf16),
            shape((LIVE, QUARTER + 128), bf16),
            shape((LIVE, KEY_WIDTH), bf16),
        ],
        [tokens],
        order=[message],
        scratch=[pltpu.VMEM((2, tokens.shape[0], QUARTER), bf16), pltpu.SemaphoreType.DMA((2,))],
    )
    far_core = core(far)

    (partial,) = call(
        base_mate_kernel,
        "base_mate",
        [],
        [rows, frozen, frozen_core],
        [shape((LIVE, KEY_WIDTH), bf16)],
        order=[near],
    )
    base_mate = across(partial)
    weights = jnp.stack([message] + [after(w, partial) for w in arrived])
    weights_core = core(weights)
    (base,) = call(
        base_own_kernel,
        "base_own",
        [],
        [near, frozen, far, frozen_core],
        [shape((LIVE, KEY_WIDTH), f32)],
        order=[weights],
    )
    low_sent, cross = call(
        low_mate_kernel,
        "low_mate",
        [],
        [rows, weights, weights_core],
        [shape((LIVE, PADDED_RANK), bf16), shape((LIVE, QUARTER + 128), bf16)],
        order=[base],
        light=True,
    )
    low_mate, cross_core = across(low_sent), core(cross)
    low, up = call(
        low_own_kernel,
        "low_own",
        [],
        [near, far, weights, weights_core],
        [shape((LIVE, PADDED_RANK), f32), shape((512, KEY_WIDTH), bf16)],
        order=[low_sent],
        light=True,
    )
    dlow, key_grads, wide = call(
        keys_kernel,
        "keys",
        [ranks],
        [far, low, low_mate, up, base, base_mate, grads, key_norm_weight[None, :]],
        [
            shape((LIVE, PADDED_RANK), bf16),
            shape((LIVE, KEY_WIDTH), bf16),
            shape((LIVE, 512), bf16),
        ],
        order=[far_core],
    )
    up_kept, up_core = call(
        up_sums_kernel,
        "up_sums",
        [ranks],
        [wide, key_grads],
        [shape((2, 4, 32, KEY_WIDTH), f32)] * 2,
        scratch=[pltpu.VMEM((512, KEY_WIDTH), f32)],
    )
    dlow_mate, dlow_core = across(dlow), core(dlow)
    dlow_mate = after(dlow_mate, up_kept)
    dlow_cross = core(dlow_mate)
    up_core_in = core(up_core)

    def down(places, types, order):
        return call(
            lambda *refs: down_kernel(places, *refs),
            "down",
            [],
            [dlow, dlow_mate, dlow_core, dlow_cross, rows],
            [shape((PADDED_RANK, QUARTER), t) for t in types],
            [near, far, far_core, cross_core],
            order=order,
            scratch=[
                pltpu.VMEM((4 * LIVE, QUARTER), bf16),
                pltpu.VMEM((4 * LIVE, HEAD), bf16),
                pltpu.SemaphoreType.DMA((7,)),
            ],
        )

    three, two = down((3, 2), (bf16, bf16), [])
    three_in, two_in = along(three, 3), along(two, 2)

    up_total, up_sent = call(
        up_core_kernel,
        "up_core",
        [],
        [up_kept, up_core_in],
        [shape((4, 32, KEY_WIDTH), f32), shape((4, 32, KEY_WIDTH), bf16)],
        order=[three],
    )
    up_arrived = across(up_sent)
    own, one = down((0, 1), (f32, bf16), [up_arrived])
    one_in = along(one, 1)
    up_parts = call(
        up_across_kernel,
        "up_across",
        [],
        [up_total, up_arrived],
        [shape((32, KEY_WIDTH), t) for t in (f32, bf16, bf16, bf16)],
        order=[one],
    )
    up_in = [up_parts[0], along(up_parts[3], 3), along(up_parts[2], 2), along(after(up_parts[1], one_in), 1)]

    new_down, down_first, down_second, new_up, up_first, up_second = call(
        update_kernel,
        "update",
        [],
        [own, one_in, two_in, three_in, adapter_down_factor[0], down_first_moment[0], down_second_moment[0]]
        + [*up_in, adapter_up_factor[0], up_first_moment[0], up_second_moment[0]],
        [shape(adapter_down_factor.shape[1:], f32)] * 3 + [shape(adapter_up_factor.shape[1:], f32)] * 3,
        scratch=[pltpu.VMEM(adapter_down_factor.shape[1:], f32)] * 3
        + [pltpu.VMEM(adapter_up_factor.shape[1:], f32)] * 3
        + [pltpu.SemaphoreType.DMA((18,))],
        out_spec=HBM,
    )
    return tuple(o[None] for o in (new_down, new_up, down_first, up_first, down_second, up_second))


def solution(mesh):
    paired = mesh.shape["dp"] == 4 and mesh.shape["fsdp"] == 4
    return jax.shard_map(
        local if paired else local_general,
        mesh=mesh,
        in_specs=(
            P(("parts", "dp", "fsdp"), None),
            P(("parts", "dp", "fsdp"), None),
            P(("parts", "dp", "fsdp"), None),
            P(("parts", "dp", "fsdp"), None),
            P(),
            P("fsdp", None),
            P(),
            P(("parts", "dp"), "fsdp", None),
            P(("parts", "dp"), "fsdp", None),
            P(("parts", "dp"), "fsdp", None),
            P(("parts", "dp"), "fsdp", None),
            P(("parts", "dp"), "fsdp", None),
            P(("parts", "dp"), "fsdp", None),
        ),
        out_specs=(
            P(("parts", "dp"), "fsdp", None),
            P(("parts", "dp"), "fsdp", None),
            P(("parts", "dp"), "fsdp", None),
            P(("parts", "dp"), "fsdp", None),
            P(("parts", "dp"), "fsdp", None),
            P(("parts", "dp"), "fsdp", None),
        ),
        check_vma=False,
    )
```

```python
import jax
import jax.numpy as jnp
from jax import lax
from jax.experimental import pallas as pl
from jax.experimental.pallas import tpu as pltpu
from jax.sharding import PartitionSpec as P

MODEL_WIDTH = 5120
HEAD = 128
KEY_WIDTH = 1024
PADDED_RANK = 128
SEQ = 32
LIVE = 288
QUARTER = MODEL_WIDTH // 4


adapter_alpha_scale = 16.0
norm_epsilon = 1e-06
learn_rate = 0.001
weight_decay = 0.01
beta_one = 0.9
beta_two = 0.999
correct_one = 1.0 - 0.9**10
correct_two = 1.0 - 0.999**10
adam_epsilon = 1e-08

bf16 = jnp.bfloat16
f32 = jnp.float32
i32 = jnp.int32


def optimizer_update(weights, gradient, moment, variance):
    moment_new = beta_one * moment + (1.0 - beta_one) * gradient
    variance_new = beta_two * variance + (1.0 - beta_two) * gradient * gradient
    update = moment_new / correct_one / (jnp.sqrt(variance_new / correct_two) + adam_epsilon)
    return (weights - learn_rate * (update + weight_decay * weights), moment_new, variance_new)


def adapter_grads(
    row_tokens,
    row_base,
    row_grads,
    down_factor_weight,
    up_factor_weight,
    owned_adapter_rank,
    key_norm_weight,
):
    columns = jnp.arange(PADDED_RANK) < owned_adapter_rank
    masked_down = jnp.where(columns[None, :], down_factor_weight, jnp.zeros((), bf16))
    masked_up = jnp.where(columns[:, None], up_factor_weight, jnp.zeros((), bf16))
    adapter_scale_factor = adapter_alpha_scale / owned_adapter_rank.astype(f32)
    lowrank = jnp.dot(row_tokens, masked_down, preferred_element_type=f32).astype(bf16)
    key_rows = row_base.astype(f32) + adapter_scale_factor * jnp.dot(
        lowrank, masked_up, preferred_element_type=f32
    )
    per_head = key_rows.reshape(key_rows.shape[0], KEY_WIDTH // HEAD, HEAD)
    inverse = lax.rsqrt(jnp.mean(per_head * per_head, axis=-1, keepdims=True) + norm_epsilon)
    normed = per_head * inverse
    incoming = row_grads.astype(f32).reshape(per_head.shape) * key_norm_weight
    key_grads = inverse * (incoming - normed * jnp.mean(incoming * normed, axis=-1, keepdims=True))
    key_grads = key_grads.reshape(key_rows.shape).astype(bf16)
    up_factor_gradient = adapter_scale_factor * lax.dot_general(
        lowrank, key_grads, (((0,), (0,)), ((), ())), preferred_element_type=f32
    )
    up_factor_gradient = jnp.where(columns[:, None], up_factor_gradient, 0.0)
    low_grads = (
        adapter_scale_factor
        * lax.dot_general(key_grads, masked_up, (((1,), (1,)), ((), ())), preferred_element_type=f32)
    ).astype(bf16)
    down_factor_gradient = lax.dot_general(
        row_tokens, low_grads, (((0,), (0,)), ((), ())), preferred_element_type=f32
    )
    return (down_factor_gradient, up_factor_gradient)


def general_gradients(
    tokens,
    cotangent,
    lengths,
    slot_adapter_index,
    adapter_rank_sizes,
    frozen,
    key_norm_weight,
    adapter_down_factor,
    adapter_up_factor,
):
    data_ranks = lax.axis_size("dp")
    owning_replica = lax.axis_index("dp")
    seq_count = lengths.shape[1]
    per_pair = -(-seq_count // data_ranks)
    slot_total = data_ranks * per_pair
    token_seqs = tokens.reshape(seq_count, SEQ, MODEL_WIDTH)
    live_mask = jnp.arange(SEQ)[None, :] < lengths[0][:, None]
    upstream = jnp.where(
        live_mask[:, :, None],
        cotangent.reshape(seq_count, SEQ, KEY_WIDTH),
        jnp.zeros((), cotangent.dtype),
    )
    target = slot_adapter_index[0]
    seq_index = jnp.arange(seq_count)
    earlier = (target[None, :] == target[:, None]) & (seq_index[None, :] < seq_index[:, None])
    slot_order = jnp.sum(earlier.astype(i32), axis=1)
    slot_of = target * per_pair + slot_order
    matches = slot_of[None, :] == jnp.arange(slot_total)[:, None]
    source = jnp.sum(jnp.where(matches, seq_index[None, :], 0), axis=1)
    filled = jnp.any(matches, axis=1)

    def pack_slots(values):
        picked = jnp.take(values, source, axis=0)
        picked = jnp.where(filled[:, None, None], picked, jnp.zeros((), values.dtype))
        return picked.reshape(data_ranks, per_pair * SEQ, values.shape[-1])

    arrived_tokens, arrived_grads = (
        lax.all_to_all(pack_slots(token_seqs), "dp", split_axis=0, concat_axis=0, tiled=True),
        lax.all_to_all(pack_slots(upstream), "dp", split_axis=0, concat_axis=0, tiled=True),
    )
    row_tokens = arrived_tokens.reshape(-1, MODEL_WIDTH)
    row_base = jnp.dot(
        row_tokens,
        lax.all_gather(frozen, "fsdp", axis=0, tiled=True),
        preferred_element_type=f32,
    ).astype(bf16)
    row_grads = arrived_grads.reshape(-1, KEY_WIDTH)
    owned_adapter_rank = jnp.sum(
        jnp.where(jnp.arange(adapter_rank_sizes.shape[0]) == owning_replica, adapter_rank_sizes, 0)
    )
    full_down, full_up = (
        lax.all_gather(adapter_down_factor.astype(bf16), "fsdp", axis=1, tiled=True),
        lax.all_gather(adapter_up_factor.astype(bf16), "fsdp", axis=1, tiled=True),
    )
    down_factor_gradient, up_factor_gradient = adapter_grads(
        row_tokens,
        row_base,
        row_grads,
        full_down[0],
        full_up[0],
        owned_adapter_rank,
        key_norm_weight,
    )
    return (
        lax.psum_scatter(down_factor_gradient, "fsdp", scatter_dimension=0, tiled=True),
        lax.psum_scatter(up_factor_gradient, "fsdp", scatter_dimension=0, tiled=True),
    )


def local_general(
    tokens,
    cotangent,
    lengths,
    slot_adapter_index,
    adapter_rank_sizes,
    frozen,
    key_norm_weight,
    adapter_down_factor,
    adapter_up_factor,
    down_first_moment,
    up_first_moment,
    down_second_moment,
    up_second_moment,
):
    down_gradient, up_gradient = general_gradients(
        tokens,
        cotangent,
        lengths,
        slot_adapter_index,
        adapter_rank_sizes,
        frozen,
        key_norm_weight,
        adapter_down_factor,
        adapter_up_factor,
    )
    new_down, down_first, down_second = optimizer_update(
        adapter_down_factor[0], down_gradient, down_first_moment[0], down_second_moment[0]
    )
    new_up, up_first, up_second = optimizer_update(
        adapter_up_factor[0], up_gradient, up_first_moment[0], up_second_moment[0]
    )
    return (
        new_down[None],
        new_up[None],
        down_first[None],
        up_first[None],
        down_second[None],
        up_second[None],
    )


SMEM = pl.BlockSpec(memory_space=pltpu.SMEM)
VMEM = pl.BlockSpec(memory_space=pltpu.VMEM)
HBM = pl.BlockSpec(memory_space=pl.ANY)


class Late:
    def __init__(self, source, target, sem):
        self.copy, self.target, self.waited = pltpu.make_async_copy(source, target, sem), target, False
        self.copy.start()

    def get(self):
        if not self.waited:
            self.copy.wait()
            self.waited = True
        return self.target


def call(kernel, name, scalars, late, outs, plain=(), order=(), scratch=(), vmem=36, light=False, out_spec=VMEM):
    n, m, p, d, o = len(scalars), len(late), len(plain), len(order), len(outs)

    def body(*refs):
        ins, rest = refs[: n + m + p], refs[n + m + p + d :]
        outputs, held, sems, scratches = rest[:o], rest[o : o + m], rest[o + m], rest[o + m + 1 :]
        lates = [Late(ins[n + i], held[i], sems.at[i]) for i in range(m)]
        kernel(*ins[:n], *lates, *ins[n + m :], *outputs, *scratches)
        for one in lates:
            one.get()

    args = list(scalars) + list(late) + list(plain) + list(order)
    moved = sum(a.size * a.dtype.itemsize for a in list(scalars) + list(late) + list(plain) + list(outs))
    return pl.pallas_call(
        body,
        name=name,
        in_specs=[SMEM] * n + [HBM] * (m + p + d),
        out_specs=tuple(out_spec for _ in outs),
        out_shape=tuple(outs),
        scratch_shapes=[pltpu.VMEM(a.shape, a.dtype) for a in late]
        + [pltpu.SemaphoreType.DMA((max(m, 1),))]
        + list(scratch),
        compiler_params=pltpu.CompilerParams(vmem_limit_bytes=vmem * 2**20),
        cost_estimate=pl.CostEstimate(
            flops=1 if light else 3 * 10**10, bytes_accessed=1 if light else moved, transcendentals=0
        ),
    )(*args)


def shape(dims, dtype):
    return jax.ShapeDtypeStruct(dims, dtype)


def offsets(place, length, slots):
    found = []
    for s in range(slots):
        total = jnp.int32(0)
        for t in range(slots):
            if t != s:
                first = place[t] > place[s] if t > s else place[t] >= place[s]
                total = total + jnp.where(first, length[t], 0)
        found.append(total)
    return found


def slot_places(lengths, adapters, slots):
    dp = lax.axis_index("dp")
    place = [adapters[0, s] ^ dp for s in range(slots)]
    length = [lengths[0, s] for s in range(slots)]
    return place, length, offsets(place, length, slots)


def packing(place, length, start, slots):
    token = lax.broadcasted_iota(i32, (1, slots * SEQ), 1)
    row_of = jnp.full((1, slots * SEQ), -1, i32)
    for s in range(slots):
        position = token - s * SEQ
        inside = (position >= 0) & (position < length[s])
        row_of = jnp.where(inside, position + start[s], row_of)
    row = lax.broadcasted_iota(i32, (LIVE, slots * SEQ), 0)
    return jnp.where(row == row_of, 1.0, 0.0).astype(bf16)


def row_places(place, length, start, slots):
    row = lax.broadcasted_iota(i32, (LIVE, HEAD), 0)
    found = jnp.zeros((LIVE, HEAD), f32)
    for s in range(slots):
        inside = (row >= start[s]) & (row < start[s] + length[s])
        found = jnp.where(inside, place[s].astype(f32), found)
    return found.astype(bf16)


def mm(a, b):
    return jnp.dot(a, b, preferred_element_type=f32)


def mm_nt(a, b):
    return lax.dot_general(a, b, (((1,), (1,)), ((), ())), preferred_element_type=f32)


def quarter_copies(tokens, held, sems, others):
    f = lax.axis_index("fsdp")
    copies = []
    for n, other in enumerate(others):
        start = pl.multiple_of((f ^ other) * QUARTER, QUARTER)
        copies.append(pltpu.make_async_copy(tokens.at[:, pl.ds(start, QUARTER)], held.at[n], sems.at[n]))
        copies[-1].start()
    return copies


def pack_sent_kernel(slots, lengths, adapters, tokens, out, held, packed, sems):
    copies = quarter_copies(tokens, held, sems, (2, 3))
    found = slot_places(lengths, adapters, slots)
    chosen = packing(*found, slots)
    ids = row_places(*found, slots)
    for q in range(2):
        for b in range(10):
            at = min(16 * (10 * q + b), LIVE - 16)
            packed[q, LIVE:, 128 * b : 128 * b + 128] = ids[at : at + 16]
        copies[q].wait()
        packed[q, :LIVE] = mm(chosen, held[q]).astype(bf16)
        copies.append(pltpu.make_async_copy(packed.at[q], out.at[q], sems.at[2 + q]))
        copies[-1].start()
    for copy in copies[2:]:
        copy.wait()


def pack_kept_kernel(slots, lengths, adapters, cotangent, tokens, near_out, far_out, grads_out, held, sems):
    copies = quarter_copies(tokens, held, sems, (0, 1))
    found = slot_places(lengths, adapters, slots)
    chosen = packing(*found, slots)
    far_out[:, QUARTER:] = row_places(*found, slots)
    copies[0].wait()
    near_out[...] = mm(chosen, held[0]).astype(bf16)
    copies[1].wait()
    far_out[:, :QUARTER] = mm(chosen, held[1]).astype(bf16)
    grads_out[...] = mm(chosen, cotangent.get()[...]).astype(bf16)


def weights_kernel(ranks, down, up_own, up_mate, out):
    rank = ranks[lax.axis_index("dp")]
    f = lax.axis_index("fsdp")
    column = lax.broadcasted_iota(i32, (QUARTER, PADDED_RANK), 1)
    out[:QUARTER] = jnp.where(column < rank, down.get()[...], 0.0).astype(bf16)
    row = lax.broadcasted_iota(i32, (32, KEY_WIDTH), 0)
    for part, held in enumerate((up_own, up_mate)):
        masked = jnp.where(row + 32 * (f ^ (2 * part)) < rank, held.get()[...], 0.0).astype(bf16)
        for k in range(8):
            at = QUARTER + 64 * k + 32 * part
            out[at : at + 32] = masked[:, 128 * k : 128 * k + 128]


def base_mate_kernel(lanes, rows, own, mate, out):
    total = mm(rows.get()[0, :LIVE], own.get()[:, lanes])
    out[...] = (total + mm(rows.get()[1, :LIVE], mate.get()[:, lanes])).astype(bf16)


def down_factors(weights):
    return jnp.concatenate([weights.get()[j, :QUARTER] for j in range(4)], axis=1)


def mate_places(rows):
    blocks = [rows[n // 10, LIVE:, 128 * (n % 10) : 128 * (n % 10) + 128] for n in range(LIVE // 16)]
    return jnp.concatenate(blocks, axis=0)


def own_adapter(every, places):
    adapter = places.astype(f32)
    total = jnp.zeros((LIVE, PADDED_RANK), f32)
    for j in range(4):
        total = jnp.where(adapter == j, every[:, 128 * j : 128 * j + 128], total)
    return total


def low_mate_kernel(rows, weights, weights_core, out, core_out):
    held = rows.get()
    places = mate_places(held)
    core_out[:, :QUARTER] = held[1, :LIVE]
    core_out[:, QUARTER:] = places
    every = mm(held[0, :LIVE], down_factors(weights))
    every = every + mm(held[1, :LIVE], down_factors(weights_core))
    out[...] = own_adapter(every, places).astype(bf16)


def base_own_kernel(near, own, far, mate, out):
    total = mm(near.get()[...], own.get()[...])
    out[...] = total + mm(far.get()[:, :QUARTER], mate.get()[...])


def low_own_kernel(near, far, weights, weights_core, out, up):
    f = lax.axis_index("fsdp")
    c, x = f % 2, f // 2
    held = far.get()
    every = mm(near.get()[...], down_factors(weights))
    every = every + mm(held[:, :QUARTER], down_factors(weights_core))
    out[...] = own_adapter(every, held[:, QUARTER:])
    for j in range(4):
        for part in range(2):
            for source, side in ((weights, c), (weights_core, 1 - c)):
                target = pl.multiple_of(128 * j + 64 * (x ^ part) + 32 * side, 32)
                for k in range(8):
                    at = QUARTER + 64 * k + 32 * part
                    up[pl.ds(target, 32), 128 * k : 128 * k + 128] = source.get()[j, at : at + 32]


def identity():
    row = lax.broadcasted_iota(i32, (HEAD, HEAD), 0)
    return jnp.where(row == lax.broadcasted_iota(i32, (HEAD, HEAD), 1), 1.0, 0.0).astype(bf16)


def spread(values, places, which):
    adapter, value = places.astype(f32), values.astype(f32)
    return jnp.concatenate([jnp.where(adapter == j, value, 0.0).astype(bf16) for j in which], axis=1)


def transposed(values):
    unit = identity()
    parts = [mm_nt(unit, values[:, n : n + 128]).astype(bf16) for n in range(0, values.shape[1], 128)]
    return jnp.concatenate(parts, axis=0)


def keys_kernel(ranks, far, low, low_mate, up_late, base, left, right, grads, gain, *refs):
    dlow_out, key_grads_out, wide_out = refs
    up = up_late.get()
    dp = lax.axis_index("dp")
    f = lax.axis_index("fsdp")
    c, x = f % 2, f // 2
    ids = far.get()[:, QUARTER:]
    adapter = ids.astype(f32)
    scales = [adapter_alpha_scale / jnp.full((1, HEAD), ranks[dp ^ j], i32).astype(f32) for j in range(4)]
    scale = jnp.zeros((LIVE, HEAD), f32)
    for j in range(4):
        scale = jnp.where(adapter == j, scales[j], scale)
    lowrank = (low.get()[...] + low_mate.get()[...].astype(f32)).astype(bf16).astype(f32)
    wide = spread(lowrank, ids, range(4))
    added = mm(wide, up[...])
    parts = []
    for k in range(8):
        lanes = slice(128 * k, 128 * k + 128)
        arrived = (left if k < 4 else right).get()[:, 128 * (k % 4) : 128 * (k % 4) + 128].astype(f32)
        held = (base.get()[:, lanes] + arrived).astype(bf16).astype(f32)
        head = held + scale * added[:, lanes]
        inverse = lax.rsqrt(jnp.mean(head * head, axis=-1, keepdims=True) + norm_epsilon)
        normed = head * inverse
        incoming = grads.get()[:, lanes].astype(f32) * gain.get()[...]
        mean = jnp.mean(incoming * normed, axis=-1, keepdims=True)
        parts.append((inverse * (incoming - normed * mean)).astype(bf16))
    key_grads = jnp.concatenate(parts, axis=1)
    every = mm_nt(key_grads, up[...])
    picked = jnp.zeros((LIVE, PADDED_RANK), f32)
    for j in range(4):
        picked = jnp.where(adapter == j, every[:, 128 * j : 128 * j + 128], picked)
    dlow_out[...] = (scale * picked).astype(bf16)
    key_grads_out[...] = key_grads
    wide_out[...] = wide


def up_sums_kernel(ranks, wide, key_grads, kept_out, sent_out, total):
    dp = lax.axis_index("dp")
    f = lax.axis_index("fsdp")
    c, x = f % 2, f // 2
    scales = [adapter_alpha_scale / jnp.full((1, HEAD), ranks[dp ^ j], i32).astype(f32) for j in range(4)]
    total[...] = mm(transposed(wide.get()[...]), key_grads.get()[...])
    for j in range(4):
        scale_j = scales[j][0:1, 0:1]
        for part in range(2):
            kept = pl.multiple_of(128 * j + 64 * (x ^ part) + 32 * c, 32)
            sent = pl.multiple_of(128 * j + 64 * (x ^ part) + 32 * (1 - c), 32)
            kept_out[part, j] = total[pl.ds(kept, 32), :] * scale_j
            sent_out[part, j] = total[pl.ds(sent, 32), :] * scale_j


def up_core_kernel(kept, arrived, own_out, mate_out):
    own_out[...] = kept.get()[0] + arrived.get()[0]
    mate_out[...] = (kept.get()[1] + arrived.get()[1]).astype(bf16)


def up_across_kernel(own, arrived, own_out, one_out, two_out, three_out):
    for j, out in enumerate((own_out, one_out, two_out, three_out)):
        out[...] = (own.get()[j] + arrived.get()[j].astype(f32)).astype(out.dtype)


def down_kernel(places, dlow, dlow_mate, dlow_core, dlow_cross, rows, near, far, far_core, cross, *refs):
    outs, (held, ids, sems) = refs[:2], refs[2:]
    copies = [pltpu.make_async_copy(far.at[:, pl.ds(QUARTER, 128)], ids.at[pl.ds(0, LIVE), :], sems.at[0])]
    copies.append(
        pltpu.make_async_copy(far_core.at[:, pl.ds(QUARTER, 128)], ids.at[pl.ds(2 * LIVE, LIVE), :], sems.at[1])
    )
    copies.append(
        pltpu.make_async_copy(cross.at[:, pl.ds(QUARTER, 128)], ids.at[pl.ds(3 * LIVE, LIVE), :], sems.at[2])
    )
    sources = [near, None, far_core.at[:, pl.ds(0, QUARTER)], cross.at[:, pl.ds(0, QUARTER)]]
    for n, source in enumerate(sources):
        if source is not None:
            copies.append(pltpu.make_async_copy(source, held.at[pl.ds(n * LIVE, LIVE), :], sems.at[3 + n]))
    for copy in copies:
        copy.start()
    held[LIVE : 2 * LIVE, :] = rows.get()[0, :LIVE]
    ids[LIVE : 2 * LIVE, :] = mate_places(rows.get())
    for copy in copies[:3]:
        copy.wait()
    lows = jnp.concatenate([d.get()[...] for d in (dlow, dlow_mate, dlow_core, dlow_cross)], axis=0)
    wide = transposed(spread(lows, ids[...], places))
    for copy in copies[3:]:
        copy.wait()
    total = mm(wide, held[...])
    for n, out in enumerate(outs):
        out[...] = total[128 * n : 128 * n + 128].astype(out.dtype)


def update_down_kernel(own, one, two, three, down, moment, variance, *refs):
    outs, held, sems = refs[:3], refs[3:6], refs[6]
    step = 256
    copies = []
    for start in range(0, QUARTER, step):
        part = slice(start, start + step)
        total = own.get()[:, part] + one.get()[:, part].astype(f32)
        total = total + (two.get()[:, part].astype(f32) + three.get()[:, part].astype(f32))
        held[0][part], held[1][part], held[2][part] = optimizer_update(
            down.get()[part], total.T, moment.get()[part], variance.get()[part]
        )
        for n in range(3):
            rows = pl.ds(start, step)
            copies.append(pltpu.make_async_copy(held[n].at[rows], outs[n].at[rows], sems.at[len(copies)]))
            copies[-1].start()
    for copy in copies:
        copy.wait()


def update_up_kernel(own, one, two, three, up, moment, variance, *outs):
    total = own.get()[...] + one.get()[...].astype(f32)
    total = total + (two.get()[...].astype(f32) + three.get()[...].astype(f32))
    outs[0][...], outs[1][...], outs[2][...] = optimizer_update(
        up.get()[...], total, moment.get()[...], variance.get()[...]
    )


def after(value, *others):
    return lax.optimization_barrier((value, *others))[0]


def local(
    tokens,
    cotangent,
    lengths,
    slot_adapter_index,
    adapter_rank_sizes,
    frozen,
    key_norm_weight,
    adapter_down_factor,
    adapter_up_factor,
    down_first_moment,
    up_first_moment,
    down_second_moment,
    up_second_moment,
):
    dp = lax.axis_index("dp")
    slots = lengths.shape[1]
    ranks = adapter_rank_sizes

    def core(value):
        return lax.ppermute(value, "fsdp", [(i, i ^ 1) for i in range(4)])

    def across(value):
        return lax.ppermute(value, "fsdp", [(i, i ^ 2) for i in range(4)])

    def along(value, distance):
        return lax.ppermute(value, "dp", [(i, i ^ distance) for i in range(4)])

    frozen_core = core(frozen)
    up_mate = across(adapter_up_factor[0])
    (sent,) = call(
        lambda *refs: pack_sent_kernel(slots, *refs),
        "pack_sent",
        [lengths, slot_adapter_index],
        [],
        [shape((2, LIVE + 16, QUARTER), bf16)],
        [tokens],
        scratch=[
            pltpu.VMEM((2, tokens.shape[0], QUARTER), bf16),
            pltpu.VMEM((2, LIVE + 16, QUARTER), bf16),
            pltpu.SemaphoreType.DMA((4,)),
        ],
        vmem=60,
        out_spec=HBM,
    )
    rows = across(sent)

    (message,) = call(
        weights_kernel,
        "weights",
        [ranks],
        [adapter_down_factor[0], adapter_up_factor[0], up_mate],
        [shape((QUARTER + 512, PADDED_RANK), bf16)],
        order=[sent, frozen_core],
    )
    arrived = [along(message, j) for j in (1, 2, 3)]

    near, far, grads = call(
        lambda *refs: pack_kept_kernel(slots, *refs),
        "pack_kept",
        [lengths, slot_adapter_index],
        [cotangent],
        [
            shape((LIVE, QUARTER), bf16),
            shape((LIVE, QUARTER + 128), bf16),
            shape((LIVE, KEY_WIDTH), bf16),
        ],
        [tokens],
        order=[message],
        scratch=[pltpu.VMEM((2, tokens.shape[0], QUARTER), bf16), pltpu.SemaphoreType.DMA((2,))],
    )
    far_core = core(far)

    half = KEY_WIDTH // 2

    def base_mate(lanes, order):
        return call(
            lambda *refs: base_mate_kernel(lanes, *refs),
            "base_mate",
            [],
            [rows, frozen, frozen_core],
            [shape((LIVE, half), bf16)],
            order=order,
        )[0]

    left = base_mate(slice(0, half), [near])
    partial = base_mate(slice(half, KEY_WIDTH), [left])
    mate_left, mate_right = across(left), across(partial)
    weights = jnp.stack([message] + [after(w, partial) for w in arrived])
    weights_core = core(weights)
    (base,) = call(
        base_own_kernel,
        "base_own",
        [],
        [near, frozen, far, frozen_core],
        [shape((LIVE, KEY_WIDTH), f32)],
        order=[weights],
    )
    low_sent, cross = call(
        low_mate_kernel,
        "low_mate",
        [],
        [rows, weights, weights_core],
        [shape((LIVE, PADDED_RANK), bf16), shape((LIVE, QUARTER + 128), bf16)],
        order=[base],
        light=True,
    )
    low_mate, cross_core = across(low_sent), core(cross)
    low, up = call(
        low_own_kernel,
        "low_own",
        [],
        [near, far, weights, weights_core],
        [shape((LIVE, PADDED_RANK), f32), shape((512, KEY_WIDTH), bf16)],
        order=[low_sent],
        light=True,
    )
    dlow, key_grads, wide = call(
        keys_kernel,
        "keys",
        [ranks],
        [far, low, low_mate, up, base, mate_left, mate_right, grads, key_norm_weight[None, :]],
        [
            shape((LIVE, PADDED_RANK), bf16),
            shape((LIVE, KEY_WIDTH), bf16),
            shape((LIVE, 512), bf16),
        ],
        order=[far_core],
    )
    up_kept, up_core = call(
        up_sums_kernel,
        "up_sums",
        [ranks],
        [wide, key_grads],
        [shape((2, 4, 32, KEY_WIDTH), f32)] * 2,
        scratch=[pltpu.VMEM((512, KEY_WIDTH), f32)],
    )
    dlow_mate, dlow_core = across(dlow), core(dlow)
    dlow_mate = after(dlow_mate, up_kept)
    dlow_cross = core(dlow_mate)
    up_core_in = core(up_core)

    def down(places, types, order):
        return call(
            lambda *refs: down_kernel(places, *refs),
            "down",
            [],
            [dlow, dlow_mate, dlow_core, dlow_cross, rows],
            [shape((PADDED_RANK, QUARTER), t) for t in types],
            [near, far, far_core, cross_core],
            order=order,
            scratch=[
                pltpu.VMEM((4 * LIVE, QUARTER), bf16),
                pltpu.VMEM((4 * LIVE, HEAD), bf16),
                pltpu.SemaphoreType.DMA((7,)),
            ],
        )

    three, two = down((3, 2), (bf16, bf16), [])
    three_in, two_in = along(three, 3), along(two, 2)

    up_total, up_sent = call(
        up_core_kernel,
        "up_core",
        [],
        [up_kept, up_core_in],
        [shape((4, 32, KEY_WIDTH), f32), shape((4, 32, KEY_WIDTH), bf16)],
        order=[three],
    )
    up_arrived = across(up_sent)
    own, one = down((0, 1), (f32, bf16), [up_arrived])
    one_in = along(one, 1)
    up_parts = call(
        up_across_kernel,
        "up_across",
        [],
        [up_total, up_arrived],
        [shape((32, KEY_WIDTH), t) for t in (f32, bf16, bf16, bf16)],
        order=[one],
    )
    up_in = [up_parts[0], along(up_parts[3], 3), along(up_parts[2], 2), along(after(up_parts[1], one_in), 1)]

    new_down, down_first, down_second = call(
        update_down_kernel,
        "update_down",
        [],
        [own, one_in, two_in, three_in, adapter_down_factor[0], down_first_moment[0], down_second_moment[0]],
        [shape(adapter_down_factor.shape[1:], f32)] * 3,
        scratch=[pltpu.VMEM(adapter_down_factor.shape[1:], f32)] * 3 + [pltpu.SemaphoreType.DMA((15,))],
        out_spec=HBM,
    )
    new_up, up_first, up_second = call(
        update_up_kernel,
        "update_up",
        [],
        [*up_in, adapter_up_factor[0], up_first_moment[0], up_second_moment[0]],
        [shape(adapter_up_factor.shape[1:], f32)] * 3,
        order=[new_down],
        vmem=60,
    )
    return tuple(o[None] for o in (new_down, new_up, down_first, up_first, down_second, up_second))


def solution(mesh):
    paired = mesh.shape["dp"] == 4 and mesh.shape["fsdp"] == 4
    return jax.shard_map(
        local if paired else local_general,
        mesh=mesh,
        in_specs=(
            P(("parts", "dp", "fsdp"), None),
            P(("parts", "dp", "fsdp"), None),
            P(("parts", "dp", "fsdp"), None),
            P(("parts", "dp", "fsdp"), None),
            P(),
            P("fsdp", None),
            P(),
            P(("parts", "dp"), "fsdp", None),
            P(("parts", "dp"), "fsdp", None),
            P(("parts", "dp"), "fsdp", None),
            P(("parts", "dp"), "fsdp", None),
            P(("parts", "dp"), "fsdp", None),
            P(("parts", "dp"), "fsdp", None),
        ),
        out_specs=(
            P(("parts", "dp"), "fsdp", None),
            P(("parts", "dp"), "fsdp", None),
            P(("parts", "dp"), "fsdp", None),
            P(("parts", "dp"), "fsdp", None),
            P(("parts", "dp"), "fsdp", None),
            P(("parts", "dp"), "fsdp", None),
        ),
        check_vma=False,
    )
```

```python
import jax
import jax.numpy as jnp
from jax import lax
from jax.experimental import pallas as pl
from jax.experimental.pallas import tpu as pltpu
from jax.sharding import PartitionSpec as P

MODEL_WIDTH = 5120
HEAD = 128
KEY_WIDTH = 1024
PADDED_RANK = 128
SEQ = 32
LIVE = 288
QUARTER = MODEL_WIDTH // 4


adapter_alpha_scale = 16.0
norm_epsilon = 1e-06
learn_rate = 0.001
weight_decay = 0.01
beta_one = 0.9
beta_two = 0.999
correct_one = 1.0 - 0.9**10
correct_two = 1.0 - 0.999**10
adam_epsilon = 1e-08

bf16 = jnp.bfloat16
f32 = jnp.float32
i32 = jnp.int32


def optimizer_update(weights, gradient, moment, variance):
    moment_new = beta_one * moment + (1.0 - beta_one) * gradient
    variance_new = beta_two * variance + (1.0 - beta_two) * gradient * gradient
    update = moment_new / correct_one / (jnp.sqrt(variance_new / correct_two) + adam_epsilon)
    return (weights - learn_rate * (update + weight_decay * weights), moment_new, variance_new)


def adapter_grads(
    row_tokens,
    row_base,
    row_grads,
    down_factor_weight,
    up_factor_weight,
    owned_adapter_rank,
    key_norm_weight,
):
    columns = jnp.arange(PADDED_RANK) < owned_adapter_rank
    masked_down = jnp.where(columns[None, :], down_factor_weight, jnp.zeros((), bf16))
    masked_up = jnp.where(columns[:, None], up_factor_weight, jnp.zeros((), bf16))
    adapter_scale_factor = adapter_alpha_scale / owned_adapter_rank.astype(f32)
    lowrank = jnp.dot(row_tokens, masked_down, preferred_element_type=f32).astype(bf16)
    key_rows = row_base.astype(f32) + adapter_scale_factor * jnp.dot(
        lowrank, masked_up, preferred_element_type=f32
    )
    per_head = key_rows.reshape(key_rows.shape[0], KEY_WIDTH // HEAD, HEAD)
    inverse = lax.rsqrt(jnp.mean(per_head * per_head, axis=-1, keepdims=True) + norm_epsilon)
    normed = per_head * inverse
    incoming = row_grads.astype(f32).reshape(per_head.shape) * key_norm_weight
    key_grads = inverse * (incoming - normed * jnp.mean(incoming * normed, axis=-1, keepdims=True))
    key_grads = key_grads.reshape(key_rows.shape).astype(bf16)
    up_factor_gradient = adapter_scale_factor * lax.dot_general(
        lowrank, key_grads, (((0,), (0,)), ((), ())), preferred_element_type=f32
    )
    up_factor_gradient = jnp.where(columns[:, None], up_factor_gradient, 0.0)
    low_grads = (
        adapter_scale_factor
        * lax.dot_general(key_grads, masked_up, (((1,), (1,)), ((), ())), preferred_element_type=f32)
    ).astype(bf16)
    down_factor_gradient = lax.dot_general(
        row_tokens, low_grads, (((0,), (0,)), ((), ())), preferred_element_type=f32
    )
    return (down_factor_gradient, up_factor_gradient)


def general_gradients(
    tokens,
    cotangent,
    lengths,
    slot_adapter_index,
    adapter_rank_sizes,
    frozen,
    key_norm_weight,
    adapter_down_factor,
    adapter_up_factor,
):
    data_ranks = lax.axis_size("dp")
    owning_replica = lax.axis_index("dp")
    seq_count = lengths.shape[1]
    per_pair = -(-seq_count // data_ranks)
    slot_total = data_ranks * per_pair
    token_seqs = tokens.reshape(seq_count, SEQ, MODEL_WIDTH)
    live_mask = jnp.arange(SEQ)[None, :] < lengths[0][:, None]
    upstream = jnp.where(
        live_mask[:, :, None],
        cotangent.reshape(seq_count, SEQ, KEY_WIDTH),
        jnp.zeros((), cotangent.dtype),
    )
    target = slot_adapter_index[0]
    seq_index = jnp.arange(seq_count)
    earlier = (target[None, :] == target[:, None]) & (seq_index[None, :] < seq_index[:, None])
    slot_order = jnp.sum(earlier.astype(i32), axis=1)
    slot_of = target * per_pair + slot_order
    matches = slot_of[None, :] == jnp.arange(slot_total)[:, None]
    source = jnp.sum(jnp.where(matches, seq_index[None, :], 0), axis=1)
    filled = jnp.any(matches, axis=1)

    def pack_slots(values):
        picked = jnp.take(values, source, axis=0)
        picked = jnp.where(filled[:, None, None], picked, jnp.zeros((), values.dtype))
        return picked.reshape(data_ranks, per_pair * SEQ, values.shape[-1])

    arrived_tokens, arrived_grads = (
        lax.all_to_all(pack_slots(token_seqs), "dp", split_axis=0, concat_axis=0, tiled=True),
        lax.all_to_all(pack_slots(upstream), "dp", split_axis=0, concat_axis=0, tiled=True),
    )
    row_tokens = arrived_tokens.reshape(-1, MODEL_WIDTH)
    row_base = jnp.dot(
        row_tokens,
        lax.all_gather(frozen, "fsdp", axis=0, tiled=True),
        preferred_element_type=f32,
    ).astype(bf16)
    row_grads = arrived_grads.reshape(-1, KEY_WIDTH)
    owned_adapter_rank = jnp.sum(
        jnp.where(jnp.arange(adapter_rank_sizes.shape[0]) == owning_replica, adapter_rank_sizes, 0)
    )
    full_down, full_up = (
        lax.all_gather(adapter_down_factor.astype(bf16), "fsdp", axis=1, tiled=True),
        lax.all_gather(adapter_up_factor.astype(bf16), "fsdp", axis=1, tiled=True),
    )
    down_factor_gradient, up_factor_gradient = adapter_grads(
        row_tokens,
        row_base,
        row_grads,
        full_down[0],
        full_up[0],
        owned_adapter_rank,
        key_norm_weight,
    )
    return (
        lax.psum_scatter(down_factor_gradient, "fsdp", scatter_dimension=0, tiled=True),
        lax.psum_scatter(up_factor_gradient, "fsdp", scatter_dimension=0, tiled=True),
    )


def local_general(
    tokens,
    cotangent,
    lengths,
    slot_adapter_index,
    adapter_rank_sizes,
    frozen,
    key_norm_weight,
    adapter_down_factor,
    adapter_up_factor,
    down_first_moment,
    up_first_moment,
    down_second_moment,
    up_second_moment,
):
    down_gradient, up_gradient = general_gradients(
        tokens,
        cotangent,
        lengths,
        slot_adapter_index,
        adapter_rank_sizes,
        frozen,
        key_norm_weight,
        adapter_down_factor,
        adapter_up_factor,
    )
    new_down, down_first, down_second = optimizer_update(
        adapter_down_factor[0], down_gradient, down_first_moment[0], down_second_moment[0]
    )
    new_up, up_first, up_second = optimizer_update(
        adapter_up_factor[0], up_gradient, up_first_moment[0], up_second_moment[0]
    )
    return (
        new_down[None],
        new_up[None],
        down_first[None],
        up_first[None],
        down_second[None],
        up_second[None],
    )


SMEM = pl.BlockSpec(memory_space=pltpu.SMEM)
VMEM = pl.BlockSpec(memory_space=pltpu.VMEM)
HBM = pl.BlockSpec(memory_space=pl.ANY)


class Late:
    def __init__(self, source, target, sem):
        self.copy, self.target, self.waited = pltpu.make_async_copy(source, target, sem), target, False
        self.copy.start()

    def get(self):
        if not self.waited:
            self.copy.wait()
            self.waited = True
        return self.target


def call(kernel, name, scalars, late, outs, plain=(), order=(), scratch=(), vmem=36, light=False, out_spec=VMEM):
    n, m, p, d, o = len(scalars), len(late), len(plain), len(order), len(outs)

    def body(*refs):
        ins, rest = refs[: n + m + p], refs[n + m + p + d :]
        outputs, held, sems, scratches = rest[:o], rest[o : o + m], rest[o + m], rest[o + m + 1 :]
        lates = [Late(ins[n + i], held[i], sems.at[i]) for i in range(m)]
        kernel(*ins[:n], *lates, *ins[n + m :], *outputs, *scratches)
        for one in lates:
            one.get()

    args = list(scalars) + list(late) + list(plain) + list(order)
    moved = sum(a.size * a.dtype.itemsize for a in list(scalars) + list(late) + list(plain) + list(outs))
    return pl.pallas_call(
        body,
        name=name,
        in_specs=[SMEM] * n + [HBM] * (m + p + d),
        out_specs=tuple(out_spec for _ in outs),
        out_shape=tuple(outs),
        scratch_shapes=[pltpu.VMEM(a.shape, a.dtype) for a in late]
        + [pltpu.SemaphoreType.DMA((max(m, 1),))]
        + list(scratch),
        compiler_params=pltpu.CompilerParams(vmem_limit_bytes=vmem * 2**20),
        cost_estimate=pl.CostEstimate(
            flops=1 if light else 3 * 10**10, bytes_accessed=1 if light else moved, transcendentals=0
        ),
    )(*args)


def shape(dims, dtype):
    return jax.ShapeDtypeStruct(dims, dtype)


def offsets(place, length, slots):
    found = []
    for s in range(slots):
        total = jnp.int32(0)
        for t in range(slots):
            if t != s:
                first = place[t] > place[s] if t > s else place[t] >= place[s]
                total = total + jnp.where(first, length[t], 0)
        found.append(total)
    return found


def slot_places(lengths, adapters, slots):
    dp = lax.axis_index("dp")
    place = [adapters[0, s] ^ dp for s in range(slots)]
    length = [lengths[0, s] for s in range(slots)]
    return place, length, offsets(place, length, slots)


def packing(place, length, start, slots):
    token = lax.broadcasted_iota(i32, (1, slots * SEQ), 1)
    row_of = jnp.full((1, slots * SEQ), -1, i32)
    for s in range(slots):
        position = token - s * SEQ
        inside = (position >= 0) & (position < length[s])
        row_of = jnp.where(inside, position + start[s], row_of)
    row = lax.broadcasted_iota(i32, (LIVE, slots * SEQ), 0)
    return jnp.where(row == row_of, 1.0, 0.0).astype(bf16)


def row_places(place, length, start, slots):
    row = lax.broadcasted_iota(i32, (LIVE, HEAD), 0)
    found = jnp.zeros((LIVE, HEAD), f32)
    for s in range(slots):
        inside = (row >= start[s]) & (row < start[s] + length[s])
        found = jnp.where(inside, place[s].astype(f32), found)
    return found.astype(bf16)


def mm(a, b):
    return jnp.dot(a, b, preferred_element_type=f32)


def mm_nt(a, b):
    return lax.dot_general(a, b, (((1,), (1,)), ((), ())), preferred_element_type=f32)


def quarter_copies(tokens, held, sems, others):
    f = lax.axis_index("fsdp")
    copies = []
    for n, other in enumerate(others):
        start = pl.multiple_of((f ^ other) * QUARTER, QUARTER)
        copies.append(pltpu.make_async_copy(tokens.at[:, pl.ds(start, QUARTER)], held.at[n], sems.at[n]))
        copies[-1].start()
    return copies


def pack_sent_kernel(slots, lengths, adapters, tokens, out, held, packed, sems):
    copies = quarter_copies(tokens, held, sems, (2, 3))
    found = slot_places(lengths, adapters, slots)
    chosen = packing(*found, slots)
    ids = row_places(*found, slots)
    for q in range(2):
        for b in range(10):
            at = min(16 * (10 * q + b), LIVE - 16)
            packed[q, LIVE:, 128 * b : 128 * b + 128] = ids[at : at + 16]
        copies[q].wait()
        packed[q, :LIVE] = mm(chosen, held[q]).astype(bf16)
        copies.append(pltpu.make_async_copy(packed.at[q], out.at[q], sems.at[2 + q]))
        copies[-1].start()
    for copy in copies[2:]:
        copy.wait()


def pack_kept_kernel(slots, lengths, adapters, cotangent, tokens, near_out, far_out, grads_out, held, sems):
    copies = quarter_copies(tokens, held, sems, (0, 1))
    found = slot_places(lengths, adapters, slots)
    chosen = packing(*found, slots)
    far_out[:, QUARTER:] = row_places(*found, slots)
    copies[0].wait()
    near_out[...] = mm(chosen, held[0]).astype(bf16)
    copies[1].wait()
    far_out[:, :QUARTER] = mm(chosen, held[1]).astype(bf16)
    grads_out[...] = mm(chosen, cotangent.get()[...]).astype(bf16)


def weights_kernel(ranks, down, up_own, up_mate, out):
    rank = ranks[lax.axis_index("dp")]
    f = lax.axis_index("fsdp")
    column = lax.broadcasted_iota(i32, (QUARTER, PADDED_RANK), 1)
    out[:QUARTER] = jnp.where(column < rank, down.get()[...], 0.0).astype(bf16)
    row = lax.broadcasted_iota(i32, (32, KEY_WIDTH), 0)
    for part, held in enumerate((up_own, up_mate)):
        masked = jnp.where(row + 32 * (f ^ (2 * part)) < rank, held.get()[...], 0.0).astype(bf16)
        for k in range(8):
            at = QUARTER + 64 * k + 32 * part
            out[at : at + 32] = masked[:, 128 * k : 128 * k + 128]


def base_mate_kernel(lanes, rows, own, mate, out):
    total = mm(rows.get()[0, :LIVE], own.get()[:, lanes])
    out[...] = (total + mm(rows.get()[1, :LIVE], mate.get()[:, lanes])).astype(bf16)


def down_factors(weights):
    return jnp.concatenate([weights.get()[j, :QUARTER] for j in range(4)], axis=1)


def mate_places(rows):
    blocks = [rows[n // 10, LIVE:, 128 * (n % 10) : 128 * (n % 10) + 128] for n in range(LIVE // 16)]
    return jnp.concatenate(blocks, axis=0)


def own_adapter(every, places):
    adapter = places.astype(f32)
    total = jnp.zeros((LIVE, PADDED_RANK), f32)
    for j in range(4):
        total = jnp.where(adapter == j, every[:, 128 * j : 128 * j + 128], total)
    return total


def low_mate_kernel(rows, weights, weights_core, out, core_out):
    held = rows.get()
    places = mate_places(held)
    core_out[:, :QUARTER] = held[1, :LIVE]
    core_out[:, QUARTER:] = places
    every = mm(held[0, :LIVE], down_factors(weights))
    every = every + mm(held[1, :LIVE], down_factors(weights_core))
    out[...] = own_adapter(every, places).astype(bf16)


def base_own_kernel(near, own, far, mate, out):
    total = mm(near.get()[...], own.get()[...])
    out[...] = total + mm(far.get()[:, :QUARTER], mate.get()[...])


def low_own_kernel(near, far, weights, weights_core, out, up):
    f = lax.axis_index("fsdp")
    c, x = f % 2, f // 2
    held = far.get()
    every = mm(near.get()[...], down_factors(weights))
    every = every + mm(held[:, :QUARTER], down_factors(weights_core))
    out[...] = own_adapter(every, held[:, QUARTER:])
    for j in range(4):
        for part in range(2):
            for source, side in ((weights, c), (weights_core, 1 - c)):
                target = pl.multiple_of(128 * j + 64 * (x ^ part) + 32 * side, 32)
                for k in range(8):
                    at = QUARTER + 64 * k + 32 * part
                    up[pl.ds(target, 32), 128 * k : 128 * k + 128] = source.get()[j, at : at + 32]


def identity():
    row = lax.broadcasted_iota(i32, (HEAD, HEAD), 0)
    return jnp.where(row == lax.broadcasted_iota(i32, (HEAD, HEAD), 1), 1.0, 0.0).astype(bf16)


def spread(values, places, which):
    adapter, value = places.astype(f32), values.astype(f32)
    return jnp.concatenate([jnp.where(adapter == j, value, 0.0).astype(bf16) for j in which], axis=1)


def transposed(values):
    unit = identity()
    parts = [mm_nt(unit, values[:, n : n + 128]).astype(bf16) for n in range(0, values.shape[1], 128)]
    return jnp.concatenate(parts, axis=0)


def keys_kernel(ranks, far, low, low_mate, up_late, base, left, right, grads, gain, *refs):
    dlow_out, key_grads_out, wide_out = refs
    up = up_late.get()
    dp = lax.axis_index("dp")
    f = lax.axis_index("fsdp")
    c, x = f % 2, f // 2
    ids = far.get()[:, QUARTER:]
    adapter = ids.astype(f32)
    scales = [adapter_alpha_scale / jnp.full((1, HEAD), ranks[dp ^ j], i32).astype(f32) for j in range(4)]
    scale = jnp.zeros((LIVE, HEAD), f32)
    for j in range(4):
        scale = jnp.where(adapter == j, scales[j], scale)
    lowrank = (low.get()[...] + low_mate.get()[...].astype(f32)).astype(bf16).astype(f32)
    wide = spread(lowrank, ids, range(4))
    added = mm(wide, up[...])
    parts = []
    for k in range(8):
        lanes = slice(128 * k, 128 * k + 128)
        arrived = (left if k < 4 else right).get()[:, 128 * (k % 4) : 128 * (k % 4) + 128].astype(f32)
        held = (base.get()[:, lanes] + arrived).astype(bf16).astype(f32)
        head = held + scale * added[:, lanes]
        inverse = lax.rsqrt(jnp.mean(head * head, axis=-1, keepdims=True) + norm_epsilon)
        normed = head * inverse
        incoming = grads.get()[:, lanes].astype(f32) * gain.get()[...]
        mean = jnp.mean(incoming * normed, axis=-1, keepdims=True)
        parts.append((inverse * (incoming - normed * mean)).astype(bf16))
    key_grads = jnp.concatenate(parts, axis=1)
    every = mm_nt(key_grads, up[...])
    picked = jnp.zeros((LIVE, PADDED_RANK), f32)
    for j in range(4):
        picked = jnp.where(adapter == j, every[:, 128 * j : 128 * j + 128], picked)
    dlow_out[...] = (scale * picked).astype(bf16)
    key_grads_out[...] = key_grads
    wide_out[...] = wide


def up_sums_kernel(ranks, wide, key_grads, kept_out, sent_out, total):
    dp = lax.axis_index("dp")
    f = lax.axis_index("fsdp")
    c, x = f % 2, f // 2
    scales = [adapter_alpha_scale / jnp.full((1, HEAD), ranks[dp ^ j], i32).astype(f32) for j in range(4)]
    total[...] = mm(transposed(wide.get()[...]), key_grads.get()[...])
    for j in range(4):
        scale_j = scales[j][0:1, 0:1]
        for part in range(2):
            kept = pl.multiple_of(128 * j + 64 * (x ^ part) + 32 * c, 32)
            sent = pl.multiple_of(128 * j + 64 * (x ^ part) + 32 * (1 - c), 32)
            kept_out[part, j] = total[pl.ds(kept, 32), :] * scale_j
            sent_out[part, j] = total[pl.ds(sent, 32), :] * scale_j


def up_core_kernel(kept, arrived, own_out, mate_out):
    own_out[...] = kept.get()[0] + arrived.get()[0]
    mate_out[...] = (kept.get()[1] + arrived.get()[1]).astype(bf16)


def up_across_kernel(own, arrived, own_out, one_out, two_out, three_out):
    for j, out in enumerate((own_out, one_out, two_out, three_out)):
        out[...] = (own.get()[j] + arrived.get()[j].astype(f32)).astype(out.dtype)


def down_kernel(places, dlow, dlow_mate, dlow_core, dlow_cross, rows, near, far, far_core, cross, *refs):
    outs, (held, ids, sems) = refs[:2], refs[2:]
    copies = [pltpu.make_async_copy(far.at[:, pl.ds(QUARTER, 128)], ids.at[pl.ds(0, LIVE), :], sems.at[0])]
    copies.append(
        pltpu.make_async_copy(far_core.at[:, pl.ds(QUARTER, 128)], ids.at[pl.ds(2 * LIVE, LIVE), :], sems.at[1])
    )
    copies.append(
        pltpu.make_async_copy(cross.at[:, pl.ds(QUARTER, 128)], ids.at[pl.ds(3 * LIVE, LIVE), :], sems.at[2])
    )
    sources = [near, None, far_core.at[:, pl.ds(0, QUARTER)], cross.at[:, pl.ds(0, QUARTER)]]
    for n, source in enumerate(sources):
        if source is not None:
            copies.append(pltpu.make_async_copy(source, held.at[pl.ds(n * LIVE, LIVE), :], sems.at[3 + n]))
    for copy in copies:
        copy.start()
    held[LIVE : 2 * LIVE, :] = rows.get()[0, :LIVE]
    ids[LIVE : 2 * LIVE, :] = mate_places(rows.get())
    for copy in copies[:3]:
        copy.wait()
    lows = jnp.concatenate([d.get()[...] for d in (dlow, dlow_mate, dlow_core, dlow_cross)], axis=0)
    wide = transposed(spread(lows, ids[...], places))
    for copy in copies[3:]:
        copy.wait()
    total = mm(wide, held[...])
    for n, out in enumerate(outs):
        out[...] = total[128 * n : 128 * n + 128].astype(out.dtype)


def update_down_kernel(own, one, two, three, down, moment, variance, *refs):
    outs, held, sems = refs[:3], refs[3:6], refs[6]
    step = 256
    copies = []
    for start in range(0, QUARTER, step):
        part = slice(start, start + step)
        total = own.get()[:, part] + one.get()[:, part].astype(f32)
        total = total + (two.get()[:, part].astype(f32) + three.get()[:, part].astype(f32))
        held[0][part], held[1][part], held[2][part] = optimizer_update(
            down.get()[part], total.T, moment.get()[part], variance.get()[part]
        )
        for n in range(3):
            rows = pl.ds(start, step)
            copies.append(pltpu.make_async_copy(held[n].at[rows], outs[n].at[rows], sems.at[len(copies)]))
            copies[-1].start()
    for copy in copies:
        copy.wait()


def update_up_kernel(own, one, two, three, up, moment, variance, *outs):
    total = own.get()[...] + one.get()[...].astype(f32)
    total = total + (two.get()[...].astype(f32) + three.get()[...].astype(f32))
    outs[0][...], outs[1][...], outs[2][...] = optimizer_update(
        up.get()[...], total, moment.get()[...], variance.get()[...]
    )


def after(value, *others):
    return lax.optimization_barrier((value, *others))[0]


def local(
    tokens,
    cotangent,
    lengths,
    slot_adapter_index,
    adapter_rank_sizes,
    frozen,
    key_norm_weight,
    adapter_down_factor,
    adapter_up_factor,
    down_first_moment,
    up_first_moment,
    down_second_moment,
    up_second_moment,
):
    dp = lax.axis_index("dp")
    slots = lengths.shape[1]
    ranks = adapter_rank_sizes

    def core(value):
        return lax.ppermute(value, "fsdp", [(i, i ^ 1) for i in range(4)])

    def across(value):
        return lax.ppermute(value, "fsdp", [(i, i ^ 2) for i in range(4)])

    def along(value, distance):
        return lax.ppermute(value, "dp", [(i, i ^ distance) for i in range(4)])

    up_mate = across(adapter_up_factor[0])
    (sent,) = call(
        lambda *refs: pack_sent_kernel(slots, *refs),
        "pack_sent",
        [lengths, slot_adapter_index],
        [],
        [shape((2, LIVE + 16, QUARTER), bf16)],
        [tokens],
        scratch=[
            pltpu.VMEM((2, tokens.shape[0], QUARTER), bf16),
            pltpu.VMEM((2, LIVE + 16, QUARTER), bf16),
            pltpu.SemaphoreType.DMA((4,)),
        ],
        vmem=60,
        out_spec=HBM,
    )
    rows = across(sent)
    frozen_core = core(after(frozen, sent))

    (message,) = call(
        weights_kernel,
        "weights",
        [ranks],
        [adapter_down_factor[0], adapter_up_factor[0], up_mate],
        [shape((QUARTER + 512, PADDED_RANK), bf16)],
        order=[sent],
    )
    arrived = [along(message, j) for j in (1, 2, 3)]

    near, far, grads = call(
        lambda *refs: pack_kept_kernel(slots, *refs),
        "pack_kept",
        [lengths, slot_adapter_index],
        [cotangent],
        [
            shape((LIVE, QUARTER), bf16),
            shape((LIVE, QUARTER + 128), bf16),
            shape((LIVE, KEY_WIDTH), bf16),
        ],
        [tokens],
        order=[message, frozen_core],
        scratch=[pltpu.VMEM((2, tokens.shape[0], QUARTER), bf16), pltpu.SemaphoreType.DMA((2,))],
    )
    far_core = core(far)

    half = KEY_WIDTH // 2

    def base_mate(lanes, order):
        return call(
            lambda *refs: base_mate_kernel(lanes, *refs),
            "base_mate",
            [],
            [rows, frozen, frozen_core],
            [shape((LIVE, half), bf16)],
            order=order,
        )[0]

    left = base_mate(slice(0, half), [near])
    partial = base_mate(slice(half, KEY_WIDTH), [left])
    mate_left, mate_right = across(left), across(partial)
    weights = jnp.stack([message] + [after(w, partial) for w in arrived])
    weights_core = core(weights)
    (base,) = call(
        base_own_kernel,
        "base_own",
        [],
        [near, frozen, far, frozen_core],
        [shape((LIVE, KEY_WIDTH), f32)],
        order=[weights],
    )
    low_sent, cross = call(
        low_mate_kernel,
        "low_mate",
        [],
        [rows, weights, weights_core],
        [shape((LIVE, PADDED_RANK), bf16), shape((LIVE, QUARTER + 128), bf16)],
        order=[base],
        light=True,
    )
    low_mate, cross_core = across(low_sent), core(cross)
    low, up = call(
        low_own_kernel,
        "low_own",
        [],
        [near, far, weights, weights_core],
        [shape((LIVE, PADDED_RANK), f32), shape((512, KEY_WIDTH), bf16)],
        order=[low_sent],
        light=True,
    )
    dlow, key_grads, wide = call(
        keys_kernel,
        "keys",
        [ranks],
        [far, low, low_mate, up, base, mate_left, mate_right, grads, key_norm_weight[None, :]],
        [
            shape((LIVE, PADDED_RANK), bf16),
            shape((LIVE, KEY_WIDTH), bf16),
            shape((LIVE, 512), bf16),
        ],
        order=[far_core],
    )
    up_kept, up_core = call(
        up_sums_kernel,
        "up_sums",
        [ranks],
        [wide, key_grads],
        [shape((2, 4, 32, KEY_WIDTH), f32)] * 2,
        scratch=[pltpu.VMEM((512, KEY_WIDTH), f32)],
    )
    dlow_mate, dlow_core = across(dlow), core(dlow)
    dlow_mate = after(dlow_mate, up_kept)
    dlow_cross = core(dlow_mate)
    up_core_in = core(up_core)

    def down(places, types, order):
        return call(
            lambda *refs: down_kernel(places, *refs),
            "down",
            [],
            [dlow, dlow_mate, dlow_core, dlow_cross, rows],
            [shape((PADDED_RANK, QUARTER), t) for t in types],
            [near, far, far_core, cross_core],
            order=order,
            scratch=[
                pltpu.VMEM((4 * LIVE, QUARTER), bf16),
                pltpu.VMEM((4 * LIVE, HEAD), bf16),
                pltpu.SemaphoreType.DMA((7,)),
            ],
        )

    three, two = down((3, 2), (bf16, bf16), [])
    three_in, two_in = along(three, 3), along(two, 2)

    up_total, up_sent = call(
        up_core_kernel,
        "up_core",
        [],
        [up_kept, up_core_in],
        [shape((4, 32, KEY_WIDTH), f32), shape((4, 32, KEY_WIDTH), bf16)],
        order=[three],
    )
    up_arrived = across(up_sent)
    own, one = down((0, 1), (f32, bf16), [up_arrived])
    one_in = along(one, 1)
    up_parts = call(
        up_across_kernel,
        "up_across",
        [],
        [up_total, up_arrived],
        [shape((32, KEY_WIDTH), t) for t in (f32, bf16, bf16, bf16)],
        order=[one],
    )
    up_in = [up_parts[0], along(up_parts[3], 3), along(up_parts[2], 2), along(after(up_parts[1], one_in), 1)]

    new_down, down_first, down_second = call(
        update_down_kernel,
        "update_down",
        [],
        [own, one_in, two_in, three_in, adapter_down_factor[0], down_first_moment[0], down_second_moment[0]],
        [shape(adapter_down_factor.shape[1:], f32)] * 3,
        scratch=[pltpu.VMEM(adapter_down_factor.shape[1:], f32)] * 3 + [pltpu.SemaphoreType.DMA((15,))],
        out_spec=HBM,
    )
    new_up, up_first, up_second = call(
        update_up_kernel,
        "update_up",
        [],
        [*up_in, adapter_up_factor[0], up_first_moment[0], up_second_moment[0]],
        [shape(adapter_up_factor.shape[1:], f32)] * 3,
        order=[new_down],
        vmem=60,
    )
    return tuple(o[None] for o in (new_down, new_up, down_first, up_first, down_second, up_second))


def solution(mesh):
    paired = mesh.shape["dp"] == 4 and mesh.shape["fsdp"] == 4
    return jax.shard_map(
        local if paired else local_general,
        mesh=mesh,
        in_specs=(
            P(("parts", "dp", "fsdp"), None),
            P(("parts", "dp", "fsdp"), None),
            P(("parts", "dp", "fsdp"), None),
            P(("parts", "dp", "fsdp"), None),
            P(),
            P("fsdp", None),
            P(),
            P(("parts", "dp"), "fsdp", None),
            P(("parts", "dp"), "fsdp", None),
            P(("parts", "dp"), "fsdp", None),
            P(("parts", "dp"), "fsdp", None),
            P(("parts", "dp"), "fsdp", None),
            P(("parts", "dp"), "fsdp", None),
        ),
        out_specs=(
            P(("parts", "dp"), "fsdp", None),
            P(("parts", "dp"), "fsdp", None),
            P(("parts", "dp"), "fsdp", None),
            P(("parts", "dp"), "fsdp", None),
            P(("parts", "dp"), "fsdp", None),
            P(("parts", "dp"), "fsdp", None),
        ),
        check_vma=False,
    )
```

```python
import jax
import jax.numpy as jnp
from jax import lax
from jax.experimental import pallas as pl
from jax.experimental.pallas import tpu as pltpu
from jax.sharding import PartitionSpec as P

MODEL_WIDTH = 5120
HEAD = 128
KEY_WIDTH = 1024
PADDED_RANK = 128
SEQ = 32
LIVE = 288
QUARTER = MODEL_WIDTH // 4


adapter_alpha_scale = 16.0
norm_epsilon = 1e-06
learn_rate = 0.001
weight_decay = 0.01
beta_one = 0.9
beta_two = 0.999
correct_one = 1.0 - 0.9**10
correct_two = 1.0 - 0.999**10
adam_epsilon = 1e-08

bf16 = jnp.bfloat16
f32 = jnp.float32
i32 = jnp.int32


def optimizer_update(weights, gradient, moment, variance):
    moment_new = beta_one * moment + (1.0 - beta_one) * gradient
    variance_new = beta_two * variance + (1.0 - beta_two) * gradient * gradient
    update = moment_new / correct_one / (jnp.sqrt(variance_new / correct_two) + adam_epsilon)
    return (weights - learn_rate * (update + weight_decay * weights), moment_new, variance_new)


def adapter_grads(
    row_tokens,
    row_base,
    row_grads,
    down_factor_weight,
    up_factor_weight,
    owned_adapter_rank,
    key_norm_weight,
):
    columns = jnp.arange(PADDED_RANK) < owned_adapter_rank
    masked_down = jnp.where(columns[None, :], down_factor_weight, jnp.zeros((), bf16))
    masked_up = jnp.where(columns[:, None], up_factor_weight, jnp.zeros((), bf16))
    adapter_scale_factor = adapter_alpha_scale / owned_adapter_rank.astype(f32)
    lowrank = jnp.dot(row_tokens, masked_down, preferred_element_type=f32).astype(bf16)
    key_rows = row_base.astype(f32) + adapter_scale_factor * jnp.dot(
        lowrank, masked_up, preferred_element_type=f32
    )
    per_head = key_rows.reshape(key_rows.shape[0], KEY_WIDTH // HEAD, HEAD)
    inverse = lax.rsqrt(jnp.mean(per_head * per_head, axis=-1, keepdims=True) + norm_epsilon)
    normed = per_head * inverse
    incoming = row_grads.astype(f32).reshape(per_head.shape) * key_norm_weight
    key_grads = inverse * (incoming - normed * jnp.mean(incoming * normed, axis=-1, keepdims=True))
    key_grads = key_grads.reshape(key_rows.shape).astype(bf16)
    up_factor_gradient = adapter_scale_factor * lax.dot_general(
        lowrank, key_grads, (((0,), (0,)), ((), ())), preferred_element_type=f32
    )
    up_factor_gradient = jnp.where(columns[:, None], up_factor_gradient, 0.0)
    low_grads = (
        adapter_scale_factor
        * lax.dot_general(key_grads, masked_up, (((1,), (1,)), ((), ())), preferred_element_type=f32)
    ).astype(bf16)
    down_factor_gradient = lax.dot_general(
        row_tokens, low_grads, (((0,), (0,)), ((), ())), preferred_element_type=f32
    )
    return (down_factor_gradient, up_factor_gradient)


def general_gradients(
    tokens,
    cotangent,
    lengths,
    slot_adapter_index,
    adapter_rank_sizes,
    frozen,
    key_norm_weight,
    adapter_down_factor,
    adapter_up_factor,
):
    data_ranks = lax.axis_size("dp")
    owning_replica = lax.axis_index("dp")
    seq_count = lengths.shape[1]
    per_pair = -(-seq_count // data_ranks)
    slot_total = data_ranks * per_pair
    token_seqs = tokens.reshape(seq_count, SEQ, MODEL_WIDTH)
    live_mask = jnp.arange(SEQ)[None, :] < lengths[0][:, None]
    upstream = jnp.where(
        live_mask[:, :, None],
        cotangent.reshape(seq_count, SEQ, KEY_WIDTH),
        jnp.zeros((), cotangent.dtype),
    )
    target = slot_adapter_index[0]
    seq_index = jnp.arange(seq_count)
    earlier = (target[None, :] == target[:, None]) & (seq_index[None, :] < seq_index[:, None])
    slot_order = jnp.sum(earlier.astype(i32), axis=1)
    slot_of = target * per_pair + slot_order
    matches = slot_of[None, :] == jnp.arange(slot_total)[:, None]
    source = jnp.sum(jnp.where(matches, seq_index[None, :], 0), axis=1)
    filled = jnp.any(matches, axis=1)

    def pack_slots(values):
        picked = jnp.take(values, source, axis=0)
        picked = jnp.where(filled[:, None, None], picked, jnp.zeros((), values.dtype))
        return picked.reshape(data_ranks, per_pair * SEQ, values.shape[-1])

    arrived_tokens, arrived_grads = (
        lax.all_to_all(pack_slots(token_seqs), "dp", split_axis=0, concat_axis=0, tiled=True),
        lax.all_to_all(pack_slots(upstream), "dp", split_axis=0, concat_axis=0, tiled=True),
    )
    row_tokens = arrived_tokens.reshape(-1, MODEL_WIDTH)
    row_base = jnp.dot(
        row_tokens,
        lax.all_gather(frozen, "fsdp", axis=0, tiled=True),
        preferred_element_type=f32,
    ).astype(bf16)
    row_grads = arrived_grads.reshape(-1, KEY_WIDTH)
    owned_adapter_rank = jnp.sum(
        jnp.where(jnp.arange(adapter_rank_sizes.shape[0]) == owning_replica, adapter_rank_sizes, 0)
    )
    full_down, full_up = (
        lax.all_gather(adapter_down_factor.astype(bf16), "fsdp", axis=1, tiled=True),
        lax.all_gather(adapter_up_factor.astype(bf16), "fsdp", axis=1, tiled=True),
    )
    down_factor_gradient, up_factor_gradient = adapter_grads(
        row_tokens,
        row_base,
        row_grads,
        full_down[0],
        full_up[0],
        owned_adapter_rank,
        key_norm_weight,
    )
    return (
        lax.psum_scatter(down_factor_gradient, "fsdp", scatter_dimension=0, tiled=True),
        lax.psum_scatter(up_factor_gradient, "fsdp", scatter_dimension=0, tiled=True),
    )


def local_general(
    tokens,
    cotangent,
    lengths,
    slot_adapter_index,
    adapter_rank_sizes,
    frozen,
    key_norm_weight,
    adapter_down_factor,
    adapter_up_factor,
    down_first_moment,
    up_first_moment,
    down_second_moment,
    up_second_moment,
):
    down_gradient, up_gradient = general_gradients(
        tokens,
        cotangent,
        lengths,
        slot_adapter_index,
        adapter_rank_sizes,
        frozen,
        key_norm_weight,
        adapter_down_factor,
        adapter_up_factor,
    )
    new_down, down_first, down_second = optimizer_update(
        adapter_down_factor[0], down_gradient, down_first_moment[0], down_second_moment[0]
    )
    new_up, up_first, up_second = optimizer_update(
        adapter_up_factor[0], up_gradient, up_first_moment[0], up_second_moment[0]
    )
    return (
        new_down[None],
        new_up[None],
        down_first[None],
        up_first[None],
        down_second[None],
        up_second[None],
    )


SMEM = pl.BlockSpec(memory_space=pltpu.SMEM)
VMEM = pl.BlockSpec(memory_space=pltpu.VMEM)
HBM = pl.BlockSpec(memory_space=pl.ANY)


class Late:
    def __init__(self, source, target, sem):
        self.copy, self.target, self.waited = pltpu.make_async_copy(source, target, sem), target, False
        self.copy.start()

    def get(self):
        if not self.waited:
            self.copy.wait()
            self.waited = True
        return self.target


def call(kernel, name, scalars, late, outs, plain=(), order=(), scratch=(), vmem=36, light=False, out_spec=VMEM):
    n, m, p, d, o = len(scalars), len(late), len(plain), len(order), len(outs)

    def body(*refs):
        ins, rest = refs[: n + m + p], refs[n + m + p + d :]
        outputs, held, sems, scratches = rest[:o], rest[o : o + m], rest[o + m], rest[o + m + 1 :]
        lates = [Late(ins[n + i], held[i], sems.at[i]) for i in range(m)]
        kernel(*ins[:n], *lates, *ins[n + m :], *outputs, *scratches)
        for one in lates:
            one.get()

    args = list(scalars) + list(late) + list(plain) + list(order)
    moved = sum(a.size * a.dtype.itemsize for a in list(scalars) + list(late) + list(plain) + list(outs))
    return pl.pallas_call(
        body,
        name=name,
        in_specs=[SMEM] * n + [HBM] * (m + p + d),
        out_specs=tuple(out_spec for _ in outs),
        out_shape=tuple(outs),
        scratch_shapes=[pltpu.VMEM(a.shape, a.dtype) for a in late]
        + [pltpu.SemaphoreType.DMA((max(m, 1),))]
        + list(scratch),
        compiler_params=pltpu.CompilerParams(vmem_limit_bytes=vmem * 2**20),
        cost_estimate=pl.CostEstimate(
            flops=1 if light else 3 * 10**10, bytes_accessed=1 if light else moved, transcendentals=0
        ),
    )(*args)


def shape(dims, dtype):
    return jax.ShapeDtypeStruct(dims, dtype)


def offsets(place, length, slots):
    found = []
    for s in range(slots):
        total = jnp.int32(0)
        for t in range(slots):
            if t != s:
                first = place[t] > place[s] if t > s else place[t] >= place[s]
                total = total + jnp.where(first, length[t], 0)
        found.append(total)
    return found


def slot_places(lengths, adapters, slots):
    dp = lax.axis_index("dp")
    place = [adapters[0, s] ^ dp for s in range(slots)]
    length = [lengths[0, s] for s in range(slots)]
    return place, length, offsets(place, length, slots)


def packing(place, length, start, slots):
    token = lax.broadcasted_iota(i32, (1, slots * SEQ), 1)
    row_of = jnp.full((1, slots * SEQ), -1, i32)
    for s in range(slots):
        position = token - s * SEQ
        inside = (position >= 0) & (position < length[s])
        row_of = jnp.where(inside, position + start[s], row_of)
    row = lax.broadcasted_iota(i32, (LIVE, slots * SEQ), 0)
    return jnp.where(row == row_of, 1.0, 0.0).astype(bf16)


def row_places(place, length, start, slots):
    row = lax.broadcasted_iota(i32, (LIVE, HEAD), 0)
    found = jnp.zeros((LIVE, HEAD), f32)
    for s in range(slots):
        inside = (row >= start[s]) & (row < start[s] + length[s])
        found = jnp.where(inside, place[s].astype(f32), found)
    return found.astype(bf16)


def mm(a, b):
    return jnp.dot(a, b, preferred_element_type=f32)


def mm_nt(a, b):
    return lax.dot_general(a, b, (((1,), (1,)), ((), ())), preferred_element_type=f32)


def quarter_copies(tokens, held, sems, others):
    f = lax.axis_index("fsdp")
    copies = []
    for n, other in enumerate(others):
        start = pl.multiple_of((f ^ other) * QUARTER, QUARTER)
        copies.append(pltpu.make_async_copy(tokens.at[:, pl.ds(start, QUARTER)], held.at[n], sems.at[n]))
        copies[-1].start()
    return copies


def pack_sent_kernel(slots, lengths, adapters, tokens, out, held, packed, sems):
    copies = quarter_copies(tokens, held, sems, (2, 3))
    found = slot_places(lengths, adapters, slots)
    chosen = packing(*found, slots)
    ids = row_places(*found, slots)
    for q in range(2):
        for b in range(10):
            at = min(16 * (10 * q + b), LIVE - 16)
            packed[q, LIVE:, 128 * b : 128 * b + 128] = ids[at : at + 16]
        copies[q].wait()
        packed[q, :LIVE] = mm(chosen, held[q]).astype(bf16)
        copies.append(pltpu.make_async_copy(packed.at[q], out.at[q], sems.at[2 + q]))
        copies[-1].start()
    for copy in copies[2:]:
        copy.wait()


def pack_kept_kernel(slots, lengths, adapters, cotangent, tokens, near_out, far_out, grads_out, held, sems):
    copies = quarter_copies(tokens, held, sems, (0, 1))
    found = slot_places(lengths, adapters, slots)
    chosen = packing(*found, slots)
    far_out[:, QUARTER:] = row_places(*found, slots)
    copies[0].wait()
    near_out[...] = mm(chosen, held[0]).astype(bf16)
    copies[1].wait()
    far_out[:, :QUARTER] = mm(chosen, held[1]).astype(bf16)
    grads_out[...] = mm(chosen, cotangent.get()[...]).astype(bf16)


def weights_kernel(ranks, down, up_own, up_mate, out):
    rank = ranks[lax.axis_index("dp")]
    f = lax.axis_index("fsdp")
    column = lax.broadcasted_iota(i32, (QUARTER, PADDED_RANK), 1)
    out[:QUARTER] = jnp.where(column < rank, down.get()[...], 0.0).astype(bf16)
    row = lax.broadcasted_iota(i32, (32, KEY_WIDTH), 0)
    for part, held in enumerate((up_own, up_mate)):
        masked = jnp.where(row + 32 * (f ^ (2 * part)) < rank, held.get()[...], 0.0).astype(bf16)
        for k in range(8):
            at = QUARTER + 64 * k + 32 * part
            out[at : at + 32] = masked[:, 128 * k : 128 * k + 128]


def base_mate_kernel(lanes, rows, own, mate, out):
    total = mm(rows.get()[0, :LIVE], own.get()[:, lanes])
    out[...] = (total + mm(rows.get()[1, :LIVE], mate.get()[:, lanes])).astype(bf16)


def down_factors(weights):
    return jnp.concatenate([weights.get()[j, :QUARTER] for j in range(4)], axis=1)


def mate_places(rows):
    blocks = [rows[n // 10, LIVE:, 128 * (n % 10) : 128 * (n % 10) + 128] for n in range(LIVE // 16)]
    return jnp.concatenate(blocks, axis=0)


def own_adapter(every, places):
    adapter = places.astype(f32)
    total = jnp.zeros((LIVE, PADDED_RANK), f32)
    for j in range(4):
        total = jnp.where(adapter == j, every[:, 128 * j : 128 * j + 128], total)
    return total


def low_mate_kernel(rows, weights, weights_core, out, core_out):
    held = rows.get()
    places = mate_places(held)
    core_out[:, :QUARTER] = held[1, :LIVE]
    core_out[:, QUARTER:] = places
    every = mm(held[0, :LIVE], down_factors(weights))
    every = every + mm(held[1, :LIVE], down_factors(weights_core))
    out[...] = own_adapter(every, places).astype(bf16)


def base_own_kernel(near, own, far, mate, out):
    total = mm(near.get()[...], own.get()[...])
    out[...] = total + mm(far.get()[:, :QUARTER], mate.get()[...])


def low_own_kernel(near, far, weights, weights_core, out, up, places_out):
    f = lax.axis_index("fsdp")
    c, x = f % 2, f // 2
    held = far.get()
    every = mm(near.get()[...], down_factors(weights))
    every = every + mm(held[:, :QUARTER], down_factors(weights_core))
    out[...] = own_adapter(every, held[:, QUARTER:])
    places_out[...] = held[:, QUARTER:]
    for j in range(4):
        for part in range(2):
            for source, side in ((weights, c), (weights_core, 1 - c)):
                target = pl.multiple_of(128 * j + 64 * (x ^ part) + 32 * side, 32)
                for k in range(8):
                    at = QUARTER + 64 * k + 32 * part
                    up[pl.ds(target, 32), 128 * k : 128 * k + 128] = source.get()[j, at : at + 32]


def identity():
    row = lax.broadcasted_iota(i32, (HEAD, HEAD), 0)
    return jnp.where(row == lax.broadcasted_iota(i32, (HEAD, HEAD), 1), 1.0, 0.0).astype(bf16)


def spread(values, places, which):
    adapter, value = places.astype(f32), values.astype(f32)
    return jnp.concatenate([jnp.where(adapter == j, value, 0.0).astype(bf16) for j in which], axis=1)


def transposed(values):
    unit = identity()
    parts = [mm_nt(unit, values[:, n : n + 128]).astype(bf16) for n in range(0, values.shape[1], 128)]
    return jnp.concatenate(parts, axis=0)


def keys_kernel(ranks, places, low, low_mate, up_late, base, left, right, grads, gain, *refs):
    dlow_out, key_grads_out, wide_out = refs
    up = up_late.get()
    dp = lax.axis_index("dp")
    f = lax.axis_index("fsdp")
    c, x = f % 2, f // 2
    ids = places.get()[...]
    adapter = ids.astype(f32)
    scales = [adapter_alpha_scale / jnp.full((1, HEAD), ranks[dp ^ j], i32).astype(f32) for j in range(4)]
    scale = jnp.zeros((LIVE, HEAD), f32)
    for j in range(4):
        scale = jnp.where(adapter == j, scales[j], scale)
    lowrank = (low.get()[...] + low_mate.get()[...].astype(f32)).astype(bf16).astype(f32)
    wide = spread(lowrank, ids, range(4))
    added = mm(wide, up[...])
    parts = []
    for k in range(8):
        lanes = slice(128 * k, 128 * k + 128)
        arrived = (left if k < 4 else right).get()[:, 128 * (k % 4) : 128 * (k % 4) + 128].astype(f32)
        held = (base.get()[:, lanes] + arrived).astype(bf16).astype(f32)
        head = held + scale * added[:, lanes]
        inverse = lax.rsqrt(jnp.mean(head * head, axis=-1, keepdims=True) + norm_epsilon)
        normed = head * inverse
        incoming = grads.get()[:, lanes].astype(f32) * gain.get()[...]
        mean = jnp.mean(incoming * normed, axis=-1, keepdims=True)
        parts.append((inverse * (incoming - normed * mean)).astype(bf16))
    key_grads = jnp.concatenate(parts, axis=1)
    every = mm_nt(key_grads, up[...])
    picked = jnp.zeros((LIVE, PADDED_RANK), f32)
    for j in range(4):
        picked = jnp.where(adapter == j, every[:, 128 * j : 128 * j + 128], picked)
    dlow_out[...] = (scale * picked).astype(bf16)
    key_grads_out[...] = key_grads
    wide_out[...] = wide


def up_sums_kernel(ranks, wide, key_grads, kept_out, sent_out, total):
    dp = lax.axis_index("dp")
    f = lax.axis_index("fsdp")
    c, x = f % 2, f // 2
    scales = [adapter_alpha_scale / jnp.full((1, HEAD), ranks[dp ^ j], i32).astype(f32) for j in range(4)]
    total[...] = mm(transposed(wide.get()[...]), key_grads.get()[...])
    for j in range(4):
        scale_j = scales[j][0:1, 0:1]
        for part in range(2):
            kept = pl.multiple_of(128 * j + 64 * (x ^ part) + 32 * c, 32)
            sent = pl.multiple_of(128 * j + 64 * (x ^ part) + 32 * (1 - c), 32)
            kept_out[part, j] = total[pl.ds(kept, 32), :] * scale_j
            sent_out[part, j] = total[pl.ds(sent, 32), :] * scale_j


def up_core_kernel(kept, arrived, own_out, mate_out):
    own_out[...] = kept.get()[0] + arrived.get()[0]
    mate_out[...] = (kept.get()[1] + arrived.get()[1]).astype(bf16)


def up_across_kernel(own, arrived, own_out, one_out, two_out, three_out):
    for j, out in enumerate((own_out, one_out, two_out, three_out)):
        out[...] = (own.get()[j] + arrived.get()[j].astype(f32)).astype(out.dtype)


def down_kernel(places, dlow, dlow_mate, dlow_core, dlow_cross, rows, near, far, far_core, cross, *refs):
    outs, (held, ids, sems) = refs[:2], refs[2:]
    copies = [pltpu.make_async_copy(far.at[:, pl.ds(QUARTER, 128)], ids.at[pl.ds(0, LIVE), :], sems.at[0])]
    copies.append(
        pltpu.make_async_copy(far_core.at[:, pl.ds(QUARTER, 128)], ids.at[pl.ds(2 * LIVE, LIVE), :], sems.at[1])
    )
    copies.append(
        pltpu.make_async_copy(cross.at[:, pl.ds(QUARTER, 128)], ids.at[pl.ds(3 * LIVE, LIVE), :], sems.at[2])
    )
    sources = [near, None, far_core.at[:, pl.ds(0, QUARTER)], cross.at[:, pl.ds(0, QUARTER)]]
    for n, source in enumerate(sources):
        if source is not None:
            copies.append(pltpu.make_async_copy(source, held.at[pl.ds(n * LIVE, LIVE), :], sems.at[3 + n]))
    for copy in copies:
        copy.start()
    held[LIVE : 2 * LIVE, :] = rows.get()[0, :LIVE]
    ids[LIVE : 2 * LIVE, :] = mate_places(rows.get())
    for copy in copies[:3]:
        copy.wait()
    lows = jnp.concatenate([d.get()[...] for d in (dlow, dlow_mate, dlow_core, dlow_cross)], axis=0)
    wide = transposed(spread(lows, ids[...], places))
    for copy in copies[3:]:
        copy.wait()
    total = mm(wide, held[...])
    for n, out in enumerate(outs):
        out[...] = total[128 * n : 128 * n + 128].astype(out.dtype)


def update_down_kernel(own, one, two, three, down, moment, variance, *refs):
    outs, held, sems = refs[:3], refs[3:6], refs[6]
    step = 256
    copies = []
    for start in range(0, QUARTER, step):
        part = slice(start, start + step)
        total = own.get()[:, part] + one.get()[:, part].astype(f32)
        total = total + (two.get()[:, part].astype(f32) + three.get()[:, part].astype(f32))
        held[0][part], held[1][part], held[2][part] = optimizer_update(
            down.get()[part], total.T, moment.get()[part], variance.get()[part]
        )
        for n in range(3):
            rows = pl.ds(start, step)
            copies.append(pltpu.make_async_copy(held[n].at[rows], outs[n].at[rows], sems.at[len(copies)]))
            copies[-1].start()
    for copy in copies:
        copy.wait()


def update_up_kernel(own, one, two, three, up, moment, variance, *outs):
    total = own.get()[...] + one.get()[...].astype(f32)
    total = total + (two.get()[...].astype(f32) + three.get()[...].astype(f32))
    outs[0][...], outs[1][...], outs[2][...] = optimizer_update(
        up.get()[...], total, moment.get()[...], variance.get()[...]
    )


def after(value, *others):
    return lax.optimization_barrier((value, *others))[0]


def local(
    tokens,
    cotangent,
    lengths,
    slot_adapter_index,
    adapter_rank_sizes,
    frozen,
    key_norm_weight,
    adapter_down_factor,
    adapter_up_factor,
    down_first_moment,
    up_first_moment,
    down_second_moment,
    up_second_moment,
):
    dp = lax.axis_index("dp")
    slots = lengths.shape[1]
    ranks = adapter_rank_sizes

    def core(value):
        return lax.ppermute(value, "fsdp", [(i, i ^ 1) for i in range(4)])

    def across(value):
        return lax.ppermute(value, "fsdp", [(i, i ^ 2) for i in range(4)])

    def along(value, distance):
        return lax.ppermute(value, "dp", [(i, i ^ distance) for i in range(4)])

    up_mate = across(adapter_up_factor[0])
    (sent,) = call(
        lambda *refs: pack_sent_kernel(slots, *refs),
        "pack_sent",
        [lengths, slot_adapter_index],
        [],
        [shape((2, LIVE + 16, QUARTER), bf16)],
        [tokens],
        scratch=[
            pltpu.VMEM((2, tokens.shape[0], QUARTER), bf16),
            pltpu.VMEM((2, LIVE + 16, QUARTER), bf16),
            pltpu.SemaphoreType.DMA((4,)),
        ],
        vmem=60,
        out_spec=HBM,
    )
    rows = across(sent)
    frozen_core = core(after(frozen, sent))

    (message,) = call(
        weights_kernel,
        "weights",
        [ranks],
        [adapter_down_factor[0], adapter_up_factor[0], up_mate],
        [shape((QUARTER + 512, PADDED_RANK), bf16)],
        order=[sent],
    )
    arrived = [along(message, j) for j in (1, 2, 3)]

    near, far, grads = call(
        lambda *refs: pack_kept_kernel(slots, *refs),
        "pack_kept",
        [lengths, slot_adapter_index],
        [cotangent],
        [
            shape((LIVE, QUARTER), bf16),
            shape((LIVE, QUARTER + 128), bf16),
            shape((LIVE, KEY_WIDTH), bf16),
        ],
        [tokens],
        order=[message, frozen_core],
        scratch=[pltpu.VMEM((2, tokens.shape[0], QUARTER), bf16), pltpu.SemaphoreType.DMA((2,))],
    )
    far_core = core(far)

    half = KEY_WIDTH // 2

    def base_mate(lanes, order):
        return call(
            lambda *refs: base_mate_kernel(lanes, *refs),
            "base_mate",
            [],
            [rows, frozen, frozen_core],
            [shape((LIVE, half), bf16)],
            order=order,
        )[0]

    left = base_mate(slice(0, half), [near])
    partial = base_mate(slice(half, KEY_WIDTH), [left])
    mate_left, mate_right = across(left), across(partial)
    weights = jnp.stack([message] + [after(w, partial) for w in arrived])
    weights_core = core(weights)
    (base,) = call(
        base_own_kernel,
        "base_own",
        [],
        [near, frozen, far, frozen_core],
        [shape((LIVE, KEY_WIDTH), f32)],
        order=[weights],
    )
    low_sent, cross = call(
        low_mate_kernel,
        "low_mate",
        [],
        [rows, weights, weights_core],
        [shape((LIVE, PADDED_RANK), bf16), shape((LIVE, QUARTER + 128), bf16)],
        order=[base],
        light=True,
    )
    low_mate, cross_core = across(low_sent), core(cross)
    low, up, places = call(
        low_own_kernel,
        "low_own",
        [],
        [near, far, weights, weights_core],
        [shape((LIVE, PADDED_RANK), f32), shape((512, KEY_WIDTH), bf16), shape((LIVE, HEAD), bf16)],
        order=[low_sent],
        light=True,
    )
    dlow, key_grads, wide = call(
        keys_kernel,
        "keys",
        [ranks],
        [places, low, low_mate, up, base, mate_left, mate_right, grads, key_norm_weight[None, :]],
        [
            shape((LIVE, PADDED_RANK), bf16),
            shape((LIVE, KEY_WIDTH), bf16),
            shape((LIVE, 512), bf16),
        ],
        order=[far_core],
    )
    up_kept, up_core = call(
        up_sums_kernel,
        "up_sums",
        [ranks],
        [wide, key_grads],
        [shape((2, 4, 32, KEY_WIDTH), f32)] * 2,
        scratch=[pltpu.VMEM((512, KEY_WIDTH), f32)],
    )
    dlow_mate, dlow_core = across(dlow), core(dlow)
    dlow_mate = after(dlow_mate, up_kept)
    dlow_cross = core(dlow_mate)
    up_core_in = core(up_core)

    def down(places, types, order):
        return call(
            lambda *refs: down_kernel(places, *refs),
            "down",
            [],
            [dlow, dlow_mate, dlow_core, dlow_cross, rows],
            [shape((PADDED_RANK, QUARTER), t) for t in types],
            [near, far, far_core, cross_core],
            order=order,
            scratch=[
                pltpu.VMEM((4 * LIVE, QUARTER), bf16),
                pltpu.VMEM((4 * LIVE, HEAD), bf16),
                pltpu.SemaphoreType.DMA((7,)),
            ],
        )

    three, two = down((3, 2), (bf16, bf16), [])
    three_in, two_in = along(three, 3), along(two, 2)

    up_total, up_sent = call(
        up_core_kernel,
        "up_core",
        [],
        [up_kept, up_core_in],
        [shape((4, 32, KEY_WIDTH), f32), shape((4, 32, KEY_WIDTH), bf16)],
        order=[three],
    )
    up_arrived = across(up_sent)
    own, one = down((0, 1), (f32, bf16), [up_arrived])
    one_in = along(one, 1)
    up_parts = call(
        up_across_kernel,
        "up_across",
        [],
        [up_total, up_arrived],
        [shape((32, KEY_WIDTH), t) for t in (f32, bf16, bf16, bf16)],
        order=[one],
    )
    up_in = [up_parts[0], along(up_parts[3], 3), along(up_parts[2], 2), along(after(up_parts[1], one_in), 1)]

    new_down, down_first, down_second = call(
        update_down_kernel,
        "update_down",
        [],
        [own, one_in, two_in, three_in, adapter_down_factor[0], down_first_moment[0], down_second_moment[0]],
        [shape(adapter_down_factor.shape[1:], f32)] * 3,
        scratch=[pltpu.VMEM(adapter_down_factor.shape[1:], f32)] * 3 + [pltpu.SemaphoreType.DMA((15,))],
        out_spec=HBM,
    )
    new_up, up_first, up_second = call(
        update_up_kernel,
        "update_up",
        [],
        [*up_in, adapter_up_factor[0], up_first_moment[0], up_second_moment[0]],
        [shape(adapter_up_factor.shape[1:], f32)] * 3,
        order=[new_down],
        vmem=60,
    )
    return tuple(o[None] for o in (new_down, new_up, down_first, up_first, down_second, up_second))


def solution(mesh):
    paired = mesh.shape["dp"] == 4 and mesh.shape["fsdp"] == 4
    return jax.shard_map(
        local if paired else local_general,
        mesh=mesh,
        in_specs=(
            P(("parts", "dp", "fsdp"), None),
            P(("parts", "dp", "fsdp"), None),
            P(("parts", "dp", "fsdp"), None),
            P(("parts", "dp", "fsdp"), None),
            P(),
            P("fsdp", None),
            P(),
            P(("parts", "dp"), "fsdp", None),
            P(("parts", "dp"), "fsdp", None),
            P(("parts", "dp"), "fsdp", None),
            P(("parts", "dp"), "fsdp", None),
            P(("parts", "dp"), "fsdp", None),
            P(("parts", "dp"), "fsdp", None),
        ),
        out_specs=(
            P(("parts", "dp"), "fsdp", None),
            P(("parts", "dp"), "fsdp", None),
            P(("parts", "dp"), "fsdp", None),
            P(("parts", "dp"), "fsdp", None),
            P(("parts", "dp"), "fsdp", None),
            P(("parts", "dp"), "fsdp", None),
        ),
        check_vma=False,
    )
```
